32 devices in a mesh: along: 4 (over z), cross: 2 (over core), batch: 4 (over y, x).
Axes of the slice: x: 2, y: 2, z: 4, core: 2. Of those that a mesh axis runs over, the one named last changes fastest.
Arguments:
- pressure_start: float32 [4, 16, 256, 256], P('batch', None, 'along', 'cross'), may hold values from -6 to 6
- along_start: float32 [4, 16, 256, 256], P('batch', None, 'along', 'cross'), may hold values from -6 to 6
- cross_start: float32 [4, 16, 256, 256], P('batch', None, 'along', 'cross'), may hold values from -6 to 6
- depth_layers: int32 [256, 256], P('along', 'cross'), may hold values from 1 to 16
- stiffness: float32 [256, 256], P('along', 'cross'), may hold values from 0.1 to 0.45
- patch_lists: int32 [4, 512], P('batch'), may hold values from 0 to 1023, all different within a row
- owner_map: int32 [8, 128], P(('along', 'cross')), may hold values from 0 to 7, as said below
Outputs:
- adjoint_pressure: float32 [4, 16, 256, 256], P('batch', None, 'along', 'cross')
- panel_store: float32 [8, 136, 4, 512], P(('along', 'cross'), None, 'batch')
The draws below stay inside these ranges and needn't reach their ends.
Inputs may be any that keep to these rules, and one draw needn't show every extreme that they name: `owner_map`: each entry is an owner, numbered as the grid blocks. Of the 128 patches of one block at most 17 have one owner, and in every draw some owner holds exactly 17 patches of every block. `patch_lists`: each row names 512 different patch ids; every patch is named by some row.
All inputs are finite; a program needn't handle non-finite values.
Results may differ from the reference program's by a relative error of at most 0.0003.
Values sent between devices are 32-bit elements; how exact they have to be, the bound alone decides.
No kernel may reach another device: no remote copies, remote signals or barrier semaphores. Data moves between devices by JAX's collectives and lax.ppermute only.
A program may use at most 64 MiB of HBM per device.

```python
import math
import jax
import jax.numpy as jnp
from jax import lax

A_DEV = 64
C_DEV = 128
NZ = 16
STEPS = 8
S = 4
NA = 256
NC = 256
PC = 64
NP_DEV = 128
OWNERS = 8
NPATCH = 1024
K = 512
ROUNDS = 16
CAP = 17
SLOTS = 136
TP = 512
N_CROSS = 2


def draw_owner_map(key, part):
    global_key, rows_key = jax.random.split(jax.random.fold_in(key, 11))
    order = jax.random.permutation(global_key, OWNERS)
    hot_owners = order[:4]
    cold_owners = order[4:]

    def one_block(block_key):
        keys = jax.random.split(block_key, ROUNDS + 3)
        rounds = [jax.random.permutation(keys[r], OWNERS) for r in range(ROUNDS - 1)]
        mixed = jax.random.permutation(keys[ROUNDS - 1], cold_owners)
        flips = jax.random.randint(keys[ROUNDS], (3,), 0, 2)
        picks = jnp.where(flips == 1, hot_owners[1:], mixed[OWNERS - 8:OWNERS - 5])
        final_round = jnp.concatenate([hot_owners[0:1], hot_owners[0:1], hot_owners[1:2], picks[0:1], hot_owners[2:3], picks[1:2], hot_owners[3:4], picks[2:3], mixed[:OWNERS - 8]])
        every = jnp.concatenate(rounds + [final_round])
        shuffle = jax.random.permutation(keys[ROUNDS + 1], NP_DEV)
        return every[shuffle]
    return jax.vmap(one_block)(jax.random.split(rows_key, OWNERS)).astype(jnp.int32)


def set_ends(entries, stream_key, least, top_value):
    dims = entries.shape
    index_at = [jax.random.randint(jax.random.fold_in(stream_key, axis), (), 0, dims[axis]) for axis in range(len(dims))]
    entries = entries.at[tuple(index_at)].set(least)
    longest = dims.index(max(dims))
    index_at[longest] = (index_at[longest] + 1) % dims[longest]
    return entries.at[tuple(index_at)].set(top_value)


def block_scale(rng, shape, cuts, smallest, largest):
    def one(axis_at, shards_of):
        heights = jax.random.uniform(jax.random.fold_in(jax.random.fold_in(rng, 6), axis_at), (shards_of,), jnp.float32, smallest / len(cuts), largest / len(cuts))
        return jnp.repeat(jnp.exp(heights), shape[axis_at] // shards_of).reshape((-1,) + (1,) * (len(shape) - axis_at - 1))

    gain = one(*cuts[0])
    for cut in cuts[1:]:
        gain = gain * one(*cut)
    return gain


def different_ones(own_key, rows, number_of, top, lift):
    ranking = jax.random.permutation(jax.random.fold_in(own_key, 1), number_of)
    pull = ranking
    for power in range(3):
        pull = pull * pull // number_of
    pull = pull * lift // number_of
    lots = jax.random.randint(jax.random.fold_in(own_key, 2), (rows, number_of), 0, 4096) + pull
    holders = jax.random.permutation(jax.random.fold_in(own_key, 3), rows)[jnp.arange(number_of) % rows]
    lots = jnp.where(jnp.arange(rows)[:, None] == holders[None, :], 1 << 14, lots)
    merit = lots * number_of + jnp.arange(number_of)
    return lax.top_k(merit.astype(jnp.int32), top)[1].astype(jnp.int32)


def gaussian(rng, extent, spread, limit, cuts=(), kind=jnp.bfloat16):
    values = jax.random.normal(rng, extent, jnp.float32) * spread
    if len(cuts) > 0:
        values = block_scale(rng, extent, cuts, -0.22, 0.18) * values
    return jnp.clip(values, min=-limit, max=limit).astype(kind)


def setup_inputs(seed: int = 0) -> dict:
    seeds = jax.random.split(jax.random.key(seed), 8)
    pressure_start = gaussian(seeds[0], (S, NZ, NA, NC), 1.0, 6.0, ((0, 4), (2, 4), (3, 2)), jnp.float32)
    along_start = gaussian(seeds[1], (S, NZ, NA, NC), 1.0, 6.0, ((0, 4), (2, 4), (3, 2)), jnp.float32)
    cross_start = gaussian(seeds[2], (S, NZ, NA, NC), 1.0, 6.0, ((0, 4), (2, 4), (3, 2)), jnp.float32)
    depth_layers = set_ends(jax.random.randint(seeds[3], (NA, NC), 1, NZ + 1), jax.random.fold_in(seeds[3], 1), 1, NZ).astype(jnp.int32)
    stiffness = jnp.clip(jnp.exp(math.log(0.45) - 1.50407736 * jax.random.uniform(seeds[4], (NA, NC), jnp.float32) ** block_scale(seeds[4], (NA, NC), ((0, 4), (1, 2)), -0.2, 0.2)), 0.1, 0.45)
    patch_lists = different_ones(seeds[5], S, NPATCH, K, 0)
    owner_map = draw_owner_map(jax.random.fold_in(seeds[7], 71), 0)
    return dict(pressure_start=pressure_start, along_start=along_start, cross_start=cross_start, depth_layers=depth_layers, stiffness=stiffness, patch_lists=patch_lists, owner_map=owner_map)


def advance(fields, wet_mask, wet_upper, wet_lower, stiffness, onehot):
    pressure, flow_along, flow_cross = fields
    zero_row = jnp.zeros((NZ, 1, NC), jnp.float32)
    zero_col = jnp.zeros((NZ, NA, 1), jnp.float32)
    zero_layer = jnp.zeros((1, NA, NC), jnp.float32)
    traces = []
    for step_index in range(STEPS):
        ahead_row = jnp.concatenate([pressure[:, 1:, :], zero_row], 1)
        flow_along = wet_mask * (flow_along - (ahead_row - pressure))
        ahead_col = jnp.concatenate([pressure[:, :, 1:], zero_col], 2)
        flow_cross = wet_mask * (flow_cross - (ahead_col - pressure))
        behind = jnp.concatenate([zero_row, flow_along[:, :-1, :]], 1)
        before = jnp.concatenate([zero_col, flow_cross[:, :, :-1]], 2)
        upper_layer = jnp.concatenate([zero_layer, pressure[:-1]], 0)
        lower_layer = jnp.concatenate([pressure[1:], zero_layer], 0)
        vertical = wet_upper * (upper_layer - pressure) + wet_lower * (lower_layer - pressure)
        pressure = wet_mask * (pressure - stiffness * ((flow_along - behind) + (flow_cross - before)) + 0.5 * stiffness * vertical)
        traces.append(jnp.sum(pressure * onehot, axis=0))
    return pressure, jnp.stack(traces)


def reference(pressure_start, along_start, cross_start, depth_layers, stiffness, patch_lists, owner_map):
    layer_index = lax.broadcasted_iota(jnp.int32, (NZ, NA, NC), 0)
    wet_mask = (layer_index < depth_layers[None]).astype(jnp.float32)
    onehot = (layer_index == depth_layers[None] - 1).astype(jnp.float32)
    zero_layer = jnp.zeros((1, NA, NC), jnp.float32)
    wet_upper = jnp.concatenate([zero_layer, wet_mask[:-1]], 0)
    wet_lower = jnp.concatenate([wet_mask[1:], zero_layer], 0)

    def run_sensor(fields):
        return advance(fields, wet_mask, wet_upper, wet_lower, stiffness, onehot)

    adjoint_pressure, traces = lax.map(run_sensor, (pressure_start, along_start, cross_start))
    member = jnp.zeros((S, NPATCH), jnp.float32).at[jnp.arange(S, dtype=jnp.int32)[:, None], patch_lists].set(1.0)
    positions = jnp.arange(NP_DEV, dtype=jnp.int32)
    earlier = positions[None, :] < positions[:, None]

    def place_source(source, panel_store):
        source = source.astype(jnp.int32)
        along_block = source // N_CROSS
        cross_block = source % N_CROSS
        zero_index = jnp.zeros((), jnp.int32)
        trace_block = lax.dynamic_slice(traces, (zero_index, zero_index, along_block * A_DEV, cross_block * C_DEV), (S, STEPS, A_DEV, C_DEV))
        member_block = lax.dynamic_slice(member, (zero_index, source * NP_DEV), (S, NP_DEV))
        panels = trace_block.reshape(S, STEPS, NP_DEV, PC) * member_block[:, None, :, None]
        panels = jnp.transpose(panels, (2, 0, 1, 3)).reshape(NP_DEV, S, TP)
        owners = lax.dynamic_index_in_dim(owner_map, source, 0, keepdims=False)
        slot_rank = jnp.sum(((owners[:, None] == owners[None, :]) & earlier).astype(jnp.int32), axis=1)
        return panel_store.at[owners, source * CAP + slot_rank].set(panels)

    panel_store = lax.fori_loop(0, OWNERS, place_source, jnp.zeros((OWNERS, SLOTS, S, TP), jnp.float32))
    return adjoint_pressure, panel_store
```

```python
import functools

import jax
import jax.numpy as jnp
from jax import lax
from jax.experimental import pallas as pl
from jax.experimental.pallas import tpu as pltpu
from jax.sharding import PartitionSpec as P

STEPS = 8
SUB = 8
VMEM = pltpu.VMEM


def lanes_of(shape):
    return lax.broadcasted_iota(jnp.int32, shape, len(shape) - 1)


def edges_kernel(p_ref, fa_ref, fc_ref, depth_ref, stiff_ref, w_ref, strip_ref, up_ref, down_ref):
    layers, rows, cols = p_ref.shape
    core = lax.axis_index("cross")
    width = cols // layers
    last = rows - SUB
    lane = lanes_of((rows, cols))
    row = lax.broadcasted_iota(jnp.int32, (rows, cols), 0)
    row_sub = lax.broadcasted_iota(jnp.int32, (SUB, cols), 0)
    depth = depth_ref[...]
    stiff = stiff_ref[...]
    first_lane = lane == 0
    seam_first = jnp.logical_and(first_lane, core == 0)
    group = lane // width
    group_sub = lanes_of((SUB, cols)) // width
    strip_p = strip_w = strip_s = jnp.zeros((rows, cols), jnp.float32)
    strip_v = jnp.zeros((SUB, cols), jnp.float32)
    for z in range(layers):
        wet = depth > z
        p = p_ref[z]
        va = jnp.where(wet, fa_ref[z], 0.0)
        vc = jnp.where(wet, fc_ref[z], 0.0)
        behind = jnp.where(row == 0, 0.0, pltpu.roll(va, 1, 0))
        turned = pltpu.roll(vc, 1, 1)
        w = (va - behind) + (vc - jnp.where(first_lane, 0.0, turned))
        w_ref[z] = w
        base = 2 * SUB * z
        up_ref[base : base + SUB] = p[last:]
        up_ref[base + SUB : base + 2 * SUB] = jnp.where(
            row_sub == 0, pltpu.roll(va[last:], 1, 0), w[last:]
        )
        down_ref[base : base + SUB] = p[:SUB]
        down_ref[base + SUB : base + 2 * SUB] = w[:SUB]
        shift = (width * z + width * (1 - core)) % cols
        shift_w = (width * z + (width - 1) * (1 - core)) % cols
        here = group == z
        seam_w = jnp.where(seam_first, turned, w)
        strip_p = jnp.where(here, pltpu.roll(p, shift, 1), strip_p)
        strip_w = jnp.where(here, pltpu.roll(seam_w, shift_w, 1), strip_w)
        strip_s = jnp.where(here, pltpu.roll(jnp.where(wet, stiff, 0.0), shift, 1), strip_s)
        strip_v = jnp.where(
            group_sub == z, pltpu.roll(pltpu.roll(va[last:], 1, 0), shift_w, 1), strip_v
        )
    strip_v = jnp.where(row_sub == 0, strip_v, strip_w[last:])
    strip_ref[0:rows] = strip_p
    strip_ref[rows : 2 * rows] = strip_w
    strip_ref[2 * rows : 3 * rows] = strip_s
    strip_ref[3 * rows : 3 * rows + SUB] = strip_v
    base = 2 * SUB * layers
    for ref, part in ((up_ref, slice(last, rows)), (down_ref, slice(0, SUB))):
        ref[base : base + SUB] = depth[part].astype(jnp.float32)
        ref[base + SUB : base + 2 * SUB] = stiff[part]
        ref[base + 2 * SUB : base + 3 * SUB] = strip_p[part]
        ref[base + 4 * SUB : base + 5 * SUB] = strip_s[part]
    up_ref[base + 3 * SUB : base + 4 * SUB] = strip_v
    down_ref[base + 3 * SUB : base + 4 * SUB] = strip_w[:SUB]


def steps_kernel(
    p_ref,
    w_in_ref,
    depth_ref,
    stiff_ref,
    own_up_ref,
    own_ref,
    other_ref,
    above_ref,
    below_ref,
    place_ref,
    p_out_ref,
    panel_ref,
    p_buf,
    w_buf,
    g_buf,
    d_buf,
    s_buf,
    seam_p,
    seam_w,
    seam_s,
    seam_h,
    seam_g,
    v_buf,
    trace,
):
    layers, rows, cols = p_ref.shape
    core = lax.axis_index("cross")
    width = cols // layers
    wide = rows + 2 * SUB
    blocks = wide // SUB
    lane = lanes_of((SUB, cols))
    slot = lane % width
    low = core == 0
    base = 2 * SUB * layers

    for z in range(layers):
        at = 2 * SUB * z
        p_buf[z, 0:SUB] = above_ref[at : at + SUB]
        p_buf[z, SUB : SUB + rows] = p_ref[z]
        p_buf[z, SUB + rows : wide] = below_ref[at : at + SUB]
        p_buf[z, wide : wide + SUB] = jnp.zeros((SUB, cols), jnp.float32)
        w_buf[z, 0:SUB] = above_ref[at + SUB : at + 2 * SUB]
        w_buf[z, SUB : SUB + rows] = w_in_ref[z]
        w_buf[z, SUB + rows : wide] = below_ref[at + SUB : at + 2 * SUB]
        w_buf[z, SUB : SUB + 1] = w_buf[z, SUB : SUB + 1] - above_ref[at + SUB : at + SUB + 1]
        w_buf[z, SUB + rows : SUB + rows + 1] = (
            w_buf[z, SUB + rows : SUB + rows + 1] - own_up_ref[at + SUB : at + SUB + 1]
        )
        g_buf[z, 0:SUB] = jnp.zeros((SUB, cols), jnp.float32)
    d_buf[0:SUB] = above_ref[base : base + SUB]
    d_buf[SUB : SUB + rows] = depth_ref[...].astype(jnp.float32)
    d_buf[SUB + rows : wide] = below_ref[base : base + SUB]
    s_buf[0:SUB] = above_ref[base + SUB : base + 2 * SUB]
    s_buf[SUB : SUB + rows] = stiff_ref[...]
    s_buf[SUB + rows : wide] = below_ref[base + SUB : base + 2 * SUB]

    def sides(own, other):
        return jnp.where(low, own, other), jnp.where(low, other, own)

    for buf, part in ((seam_p, 0), (seam_w, 1), (seam_s, 2)):
        own_at = base + (2 + part) * SUB
        other_at = base + (5 + part) * SUB
        top = sides(above_ref[own_at : own_at + SUB], above_ref[other_at : other_at + SUB])
        end = sides(below_ref[own_at : own_at + SUB], below_ref[other_at : other_at + SUB])
        middle = sides(
            own_ref[part * rows : (part + 1) * rows], other_ref[part * rows : (part + 1) * rows]
        )
        for side in range(2):
            buf[side, 0:SUB] = top[side]
            buf[side, SUB : SUB + rows] = middle[side]
            buf[side, SUB + rows : wide] = end[side]
    for side in range(2):
        seam_p[side, wide : wide + SUB] = jnp.zeros((SUB, cols), jnp.float32)
        seam_g[side, 0:SUB] = jnp.zeros((SUB, cols), jnp.float32)
    raw = seam_w[0]
    wide_slot = lanes_of((wide, cols)) % width
    v_buf[...] = jnp.where(wide_slot == width - 1, raw, 0.0)
    seam_w[0] = pltpu.roll(raw, 1, 1)
    wide_row = lax.broadcasted_iota(jnp.int32, (wide, cols), 0)
    seam_w[1] = seam_w[1] - jnp.where(
        jnp.logical_and(wide_slot == 0, wide_row > 0), pltpu.roll(raw, cols - width + 1, 1), 0.0
    )
    last_own = own_ref[3 * rows : 3 * rows + 1]
    last_other = other_ref[3 * rows : 3 * rows + 1]
    last_sides = sides(last_own, last_other)
    for side in range(2):
        fix_end = pltpu.roll(last_sides[0], 1, 1) if side == 0 else last_sides[1]
        seam_w[side, SUB : SUB + 1] = seam_w[side, SUB : SUB + 1] - seam_w[side, 0:1]
        seam_w[side, SUB + rows : SUB + rows + 1] = (
            seam_w[side, SUB + rows : SUB + rows + 1] - fix_end
        )
        wet = jnp.where(seam_s[side] > 0.0, 0.5, 0.0)
        deeper = pltpu.roll(wet, cols - width, 1)
        seam_h[side] = jnp.where(lanes_of((wide, cols)) < cols - width, deeper, 0.0)

    last_lane = lane == cols - 1
    first_lane = lane == 0
    last_slot = slot == width - 1
    first_slot = slot == 0
    keep = slot == jnp.where(low, width - 2, width - 1)

    def step(t, carry):
        for r in range(blocks):
            at = r * SUB
            here = slice(at, at + SUB)
            ahead = slice(at + 1, at + 1 + SUB)
            g_here = slice(at + SUB, at + 2 * SUB)
            g_behind = slice(at + SUB - 1, at + 2 * SUB - 1)
            sp = [seam_p[0, here], seam_p[1, here]]
            ss = [seam_s[0, here], seam_s[1, here]]
            wet_s = [s > 0.0 for s in ss]
            right = [
                jnp.where(last_slot, pltpu.roll(sp[1], width - 1, 1), pltpu.roll(sp[0], cols - 1, 1)),
                pltpu.roll(sp[1], cols - 1, 1),
            ]
            gy = [jnp.where(wet_s[i], right[i] - sp[i], 0.0) for i in range(2)]
            left = [
                pltpu.roll(gy[0], 1, 1),
                jnp.where(
                    first_slot, pltpu.roll(gy[0], cols - width + 1, 1), pltpu.roll(gy[1], 1, 1)
                ),
            ]
            inject = jnp.where(low, pltpu.roll(sp[1], width - 2, 1), gy[0] - v_buf[here])
            inject = jnp.where(keep, inject, 0.0)
            v_buf[here] = jnp.zeros((SUB, cols), jnp.float32)
            for i in range(2):
                gx = jnp.where(wet_s[i], seam_p[i, ahead] - sp[i], 0.0)
                seam_g[i, g_here] = gx
                w = seam_w[i, here] - ((gx - seam_g[i, g_behind]) + (gy[i] - left[i]))
                seam_w[i, here] = w
                hz = seam_h[i, here] * (pltpu.roll(sp[i], cols - width, 1) - sp[i])
                flux = w - (hz - pltpu.roll(hz, width, 1))
                seam_p[i, here] = jnp.where(wet_s[i], sp[i] - ss[i] * flux, 0.0)
            depth = d_buf[here]
            stiff = s_buf[here]
            surface = jnp.zeros((SUB, cols), jnp.float32)
            hz_before = None
            p = p_buf[0, here]
            wet = depth > 0.0
            for z in range(layers):
                gx = jnp.where(wet, p_buf[z, ahead] - p, 0.0)
                g_buf[z, g_here] = gx
                edge = pltpu.roll(inject, (cols - width + 1 - width * z) % cols, 1)
                p_right = jnp.where(last_lane, edge, pltpu.roll(p, cols - 1, 1))
                gy = jnp.where(wet, p_right - p, 0.0)
                gy_left = jnp.where(first_lane, edge, pltpu.roll(gy, 1, 1))
                w = w_buf[z, here] - ((gx - g_buf[z, g_behind]) + (gy - gy_left))
                w_buf[z, here] = w
                flux = w
                if z < layers - 1:
                    p_next = p_buf[z + 1, here]
                    wet_next = depth > float(z + 1)
                    hz = jnp.where(wet_next, 0.5 * (p_next - p), 0.0)
                    flux = w - (hz if hz_before is None else hz - hz_before)
                    hz_before = hz
                else:
                    flux = w + hz_before
                p_new = jnp.where(wet, p - stiff * flux, 0.0)
                p_buf[z, here] = p_new
                surface = jnp.where(wet, p_new, surface)
                if z < layers - 1:
                    p, wet = p_next, wet_next
            if 0 < r < blocks - 1:
                trace[t, at - SUB : at] = surface
        return carry

    lax.fori_loop(0, STEPS, step, 0)
    for z in range(layers):
        p_out_ref[z] = p_buf[z, SUB : SUB + rows]

    half = cols // 2
    lane_rows = lanes_of((rows, cols))
    place = place_ref[...]
    for j in range(STEPS // 2):
        one = trace[2 * j]
        two = trace[2 * j + 1]
        near = jnp.where(lane_rows < half, one, pltpu.roll(two, half, 1))
        far = jnp.where(lane_rows < half, pltpu.roll(one, half, 1), two)
        both = jnp.concatenate([near, far], 0)
        part_a = both.astype(jnp.bfloat16)
        rest = both - part_a.astype(jnp.float32)
        part_b = rest.astype(jnp.bfloat16)
        part_c = (rest - part_b.astype(jnp.float32)).astype(jnp.bfloat16)
        total = jnp.dot(place, part_a, preferred_element_type=jnp.float32)
        total += jnp.dot(place, part_b, preferred_element_type=jnp.float32)
        total += jnp.dot(place, part_c, preferred_element_type=jnp.float32)
        panel_ref[pl.ds(j, place.shape[0], stride=STEPS // 2)] = total


def shards(
    pressure_start, along_start, cross_start, depth_layers, stiffness, patch_lists, owner_map
):
    sensors, layers, rows, cols = pressure_start.shape
    f32 = jnp.float32
    along_count = lax.axis_size("along")
    cross_count = lax.axis_size("cross")
    forward = [(i, i + 1) for i in range(along_count - 1)]
    backward = [(target, source) for source, target in forward]
    swap = [(0, 1), (1, 0)]
    wide = rows + 2 * SUB
    strip_rows = 3 * rows + SUB
    pack_rows = 2 * SUB * layers + 5 * SUB

    spec = pl.BlockSpec(memory_space=VMEM)
    w, strips, up, down = pl.pallas_call(
        edges_kernel,
        out_shape=[
            jax.ShapeDtypeStruct((layers, rows, cols), f32),
            jax.ShapeDtypeStruct((strip_rows, cols), f32),
            jax.ShapeDtypeStruct((pack_rows, cols), f32),
            jax.ShapeDtypeStruct((pack_rows, cols), f32),
        ],
        in_specs=[spec] * 5,
        out_specs=[spec] * 4,
        name="edges",
    )(pressure_start[0], along_start[0], cross_start[0], depth_layers, stiffness)

    other = lax.ppermute(strips, "cross", swap)
    last = rows - SUB
    up_rest = jnp.concatenate(
        [other[last:rows], other[3 * rows :], other[3 * rows - SUB : 3 * rows]], 0
    )
    down_rest = jnp.concatenate(
        [other[:SUB], other[rows : rows + SUB], other[2 * rows : 2 * rows + SUB]], 0
    )
    above = lax.ppermute(jnp.concatenate([up, up_rest], 0), "along", forward)
    below = lax.ppermute(jnp.concatenate([down, down_rest], 0), "along", backward)

    patch_count = 2 * rows
    owner_count = along_count * cross_count
    capacity = patch_count // owner_count + 1
    slots = owner_count * capacity
    first_patch = (lax.axis_index("along") * cross_count + lax.axis_index("cross")) * patch_count
    positions = jnp.arange(patch_count, dtype=jnp.int32)
    member = jnp.any((patch_lists[0] - first_patch)[:, None] == positions[None, :], axis=0)
    owners = owner_map[0]
    earlier = positions[None, :] < positions[:, None]
    rank = jnp.sum(((owners[:, None] == owners[None, :]) & earlier).astype(jnp.int32), axis=1)
    target = jnp.where(member, owners * capacity + rank, -1)
    target = target.reshape(rows, 2).T.reshape(patch_count)
    place = (jnp.arange(slots, dtype=jnp.int32)[:, None] == target[None, :]).astype(jnp.bfloat16)

    parts = STEPS // 2
    pressure, panels = pl.pallas_call(
        steps_kernel,
        out_shape=[
            jax.ShapeDtypeStruct((layers, rows, cols), f32),
            jax.ShapeDtypeStruct((slots * parts, cols), f32),
        ],
        in_specs=[spec] * 10,
        out_specs=[spec] * 2,
        scratch_shapes=[
            VMEM((layers, wide + SUB, cols), f32),
            VMEM((layers, wide, cols), f32),
            VMEM((layers, wide + SUB, cols), f32),
            VMEM((wide, cols), f32),
            VMEM((wide, cols), f32),
            VMEM((2, wide + SUB, cols), f32),
            VMEM((2, wide, cols), f32),
            VMEM((2, wide, cols), f32),
            VMEM((2, wide, cols), f32),
            VMEM((2, wide + SUB, cols), f32),
            VMEM((wide, cols), f32),
            VMEM((STEPS, rows, cols), f32),
        ],
        compiler_params=pltpu.CompilerParams(vmem_limit_bytes=32 * 1024 * 1024),
        name="steps",
    )(
        pressure_start[0],
        w,
        depth_layers,
        stiffness,
        up,
        strips,
        other,
        above,
        below,
        place,
    )
    outgoing = panels.reshape(slots, 1, parts * cols)
    received = lax.all_to_all(outgoing, ("along", "cross"), split_axis=0, concat_axis=0, tiled=True)
    return (pressure[None], received[None])


def solution(mesh):
    in_specs = (
        P("batch", None, "along", "cross"),
        P("batch", None, "along", "cross"),
        P("batch", None, "along", "cross"),
        P("along", "cross"),
        P("along", "cross"),
        P("batch", None),
        P(("along", "cross"), None),
    )
    out_specs = (P("batch", None, "along", "cross"), P(("along", "cross"), None, "batch", None))
    return jax.shard_map(shards, mesh=mesh, in_specs=in_specs, out_specs=out_specs, check_vma=False)
```

```python
import jax
import jax.numpy as jnp
from jax import lax
from jax.experimental import pallas as pl
from jax.experimental.pallas import tpu as pltpu
from jax.sharding import PartitionSpec as P

STEPS = 8
SUB = 8
VMEM = pltpu.VMEM


def lanes_of(shape):
    return lax.broadcasted_iota(jnp.int32, shape, len(shape) - 1)


def rows_of(shape):
    return lax.broadcasted_iota(jnp.int32, shape, len(shape) - 2)


def edges_kernel(p_ref, fa_ref, fc_ref, depth_ref, stiff_ref, keep_ref, send_ref, one_ref, two_ref):
    layers, rows, cols = p_ref.shape
    low = lax.axis_index("cross") == 0
    span = rows // 2 + SUB
    last = rows - SUB
    lane = lanes_of((rows, cols))
    row = rows_of((rows, cols))
    row_sub = rows_of((SUB, cols))
    depth = depth_ref[...]
    stiff = stiff_ref[...]
    first_lane = lane == 0
    slot_one = row_sub == jnp.where(low, 0, -1)
    slot_two = row_sub == jnp.where(low, -1, 0)
    base = 2 * span * layers
    base_z = 2 * SUB * layers
    velocity = jnp.zeros((rows, cols), jnp.float32)

    def halves(array):
        first, second = array[:span], array[rows - span :]
        return jnp.where(low, first, second), jnp.where(low, second, first)

    def ends(array):
        first, second = array[:SUB], array[last:]
        return jnp.where(low, second, first), jnp.where(low, first, second)

    for z in range(layers):
        wet = depth > z
        p = p_ref[z]
        va = jnp.where(wet, fa_ref[z], 0.0)
        vc = jnp.where(wet, fc_ref[z], 0.0)
        behind = jnp.where(row == 0, 0.0, pltpu.roll(va, 1, 0))
        before = jnp.where(first_lane, 0.0, pltpu.roll(vc, 1, 1))
        w = (va - behind) + (vc - before)
        velocity = jnp.where(lane == z, pltpu.roll(vc, z + 1, 1), velocity)
        at = 2 * span * z
        keep_ref[at : at + span], send_ref[at : at + span] = halves(p)
        at += span
        keep_ref[at : at + span], send_ref[at : at + span] = halves(w)
        final = va[rows - 1 : rows]
        at = base + 3 * span + z
        keep_ref[at : at + 1] = final
        send_ref[at : at + 1] = final
        at = 2 * SUB * z
        one_ref[at : at + SUB], two_ref[at : at + SUB] = ends(p)
        at += SUB
        one, two = ends(w)
        final = jnp.broadcast_to(final, (SUB, cols))
        one_ref[at : at + SUB] = jnp.where(slot_one, final, one)
        two_ref[at : at + SUB] = jnp.where(slot_two, final, two)
    for i, array in enumerate((depth.astype(jnp.float32), stiff, velocity)):
        at = base + span * i
        keep_ref[at : at + span], send_ref[at : at + span] = halves(array)
        at = base_z + SUB * i
        one_ref[at : at + SUB], two_ref[at : at + SUB] = ends(array)


def steps_kernel(
    keep_ref,
    other_ref,
    one_ref,
    two_ref,
    place_ref,
    p_keep_ref,
    p_send_ref,
    panel_keep_ref,
    panel_send_ref,
    p_buf,
    w_buf,
    d_buf,
    s_buf,
    trace,
    wet_buf,
    scale_buf,
    half_buf,
    p_two,
    w_two,
):
    layers, half_rows, cols = p_keep_ref.shape
    core = lax.axis_index("cross")
    low = core == 0
    span = half_rows + SUB
    wide = span + SUB
    blocks = wide // SUB
    base = 2 * span * layers
    base_z = 2 * SUB * layers
    lane = lanes_of((SUB, cols))
    row = rows_of((SUB, cols))
    middle = pl.multiple_of(SUB * (1 - core), SUB)
    halo = pl.multiple_of(span * core, SUB)

    def left(own, other):
        return jnp.where(low, own, other)

    seam_span = left(keep_ref[base + 2 * span : base + 3 * span], other_ref[base + 2 * span : base + 3 * span])
    seam_halo = left(one_ref[base_z + 2 * SUB : base_z + 3 * SUB], two_ref[base_z + 2 * SUB : base_z + 3 * SUB])
    top_row = row == jnp.where(low, 0, -1)
    end_row = row == jnp.where(low, -1, 0)
    zeros = jnp.zeros((SUB, cols), jnp.float32)
    for tile, main_ref, halo_ref, seam_core in ((core, keep_ref, one_ref, 1), (1 - core, other_ref, two_ref, 0)):
        seam_lane = jnp.where(core == seam_core, 0, -1)
        seam = lanes_of((span, cols)) == seam_lane
        seam_sub = lane == seam_lane
        for z in range(layers):
            at = 2 * span * z
            at_z = 2 * SUB * z
            p_buf[tile, z, :SUB] = zeros
            p_two[tile, z, :SUB] = zeros
            p_two[tile, z, SUB + wide :] = zeros
            p_buf[tile, z, pl.ds(middle + SUB, span)] = main_ref[at : at + span]
            p_buf[tile, z, pl.ds(halo + SUB, SUB)] = halo_ref[at_z : at_z + SUB]
            p_buf[tile, z, SUB + wide :] = zeros
            turn = (cols - z) % cols
            w = main_ref[at + span : at + 2 * span]
            w = w - jnp.where(seam, pltpu.roll(seam_span, turn, 1) if turn else seam_span, 0.0)
            w_halo = halo_ref[at_z + SUB : at_z + 2 * SUB]
            slot = jnp.broadcast_to(w_halo[0:1], (SUB, cols))
            final = jnp.broadcast_to(main_ref[base + 3 * span + z : base + 3 * span + z + 1], (SUB, cols))
            w_halo = w_halo - jnp.where(seam_sub, pltpu.roll(seam_halo, turn, 1) if turn else seam_halo, 0.0)
            w_halo = w_halo - jnp.where(end_row, final, 0.0)
            w_top = w[:SUB] - jnp.where(top_row, slot, 0.0)
            w_buf[tile, z, pl.ds(middle, SUB)] = w_top
            w_buf[tile, z, pl.ds(middle + SUB, span - SUB)] = w[SUB:]
            w_buf[tile, z, pl.ds(halo, SUB)] = w_halo
        d_buf[tile, :SUB] = zeros
        for buf, i, shift in ((d_buf, 0, SUB), (s_buf, 1, 0)):
            buf[tile, pl.ds(middle + shift, span)] = main_ref[base + i * span : base + (i + 1) * span]
            buf[tile, pl.ds(halo + shift, SUB)] = halo_ref[base_z + i * SUB : base_z + (i + 1) * SUB]

    zs = range(layers)
    for i in range(2):
        for z in zs:
            wet = d_buf[i, SUB:] > float(z)
            if True:
                wet_buf[i, z, :SUB] = zeros
                wet_buf[i, z, SUB:] = jnp.where(wet, 1.0, 0.0)
            if True:
                scale_buf[i, z] = jnp.where(wet, s_buf[i], 0.0)
            if True and z > 0:
                half_buf[i, z - 1] = jnp.where(wet, 0.5, 0.0)
    ZB = 4
    groups = layers // ZB
    lane = lanes_of((ZB, wide, cols))
    last_lane = lane == cols - 1
    first_lane = lane == 0
    here = slice(SUB, SUB + wide)
    ahead = slice(SUB + 1, SUB + 1 + wide)
    back_rows = slice(SUB - 1, SUB - 1 + wide)

    def step(t, first, p_buf, w_buf, p_out, w_out):
        def stage_a(g):
            zs = slice(g * ZB, (g + 1) * ZB)
            return [pltpu.roll(p_buf[i, zs, here], cols - 1, 2) for i in range(2)]

        def stage_b(g, turned):
            zs = slice(g * ZB, (g + 1) * ZB)
            right = [
                jnp.where(last_lane, turned[1], turned[0]),
                jnp.where(last_lane, 0.0, turned[1]),
            ]
            gy = [wet_buf[i, zs, SUB:] * (right[i] - p_buf[i, zs, here]) for i in range(2)]
            return gy, [pltpu.roll(gy[i], 1, 2) for i in range(2)]

        hz_last = [None, None]
        surface = [None, None]

        def stage_c(g, gy, back):
            zs = slice(g * ZB, (g + 1) * ZB)
            before = [
                jnp.where(first_lane, 0.0, back[0]),
                jnp.where(first_lane, back[0], back[1]),
            ]
            for i in range(2):
                p = p_buf[i, zs, here]
                w = w_buf[i, zs] - (gy[i] - before[i])
                gx = wet_buf[i, zs, SUB:] * (p_buf[i, zs, ahead] - p)
                behind = wet_buf[i, zs, SUB - 1 : SUB - 1 + wide] * (p - p_buf[i, zs, back_rows])
                w = w - (gx - behind)
                w_out[i, zs] = w
                if g + 1 < groups:
                    hz = half_buf[i, zs] * (p_buf[i, g * ZB + 1 : (g + 1) * ZB + 1, here] - p)
                elif ZB > 1:
                    hz = jnp.concatenate([half_buf[i, g * ZB :] * (p[1:] - p[:-1]), jnp.zeros((1, wide, cols), jnp.float32)], 0)
                else:
                    hz = jnp.zeros((1, wide, cols), jnp.float32)
                prev = jnp.zeros((1, wide, cols), jnp.float32) if g == 0 else hz_last[i]
                flux = w - (hz - (jnp.concatenate([prev, hz[:-1]], 0) if ZB > 1 else prev))
                hz_last[i] = hz[-1:]
                old = wet_buf[i, zs, SUB:] * p if first else p
                new = old - scale_buf[i, zs] * flux
                p_out[i, zs, here] = new
                for k in range(ZB):
                    part = new[k, SUB:span]
                    z = g * ZB + k
                    surface[i] = part if z == 0 else jnp.where(d_buf[i, 2 * SUB : SUB + span] > float(z), part, surface[i])

        turned = [stage_a(0), stage_a(1)]
        ready = stage_b(0, turned[0])
        for g in range(groups):
            if g + 2 < groups:
                turned.append(stage_a(g + 2))
            coming = stage_b(g + 1, turned[g + 1]) if g + 1 < groups else None
            stage_c(g, *ready)
            ready = coming
        for i in range(2):
            trace[t, i] = surface[i]

    def two(k, carry):
        step(2 * k, False, p_buf, w_buf, p_two, w_two)
        step(2 * k + 1, False, p_two, w_two, p_buf, w_buf)
        return carry

    step(0, True, p_buf, w_buf, p_two, w_two)
    step(1, False, p_two, w_two, p_buf, w_buf)
    lax.fori_loop(1, STEPS // 2, two, 0)
    for z in zs:
        p_keep_ref[z] = p_buf[core, z, 2 * SUB : 2 * SUB + half_rows]
        p_send_ref[z] = p_buf[1 - core, z, 2 * SUB : 2 * SUB + half_rows]

    width = cols // 2
    lane_rows = lanes_of((half_rows, cols))
    place = place_ref[...]
    count = place.shape[0] // 2
    parts = STEPS // 2
    for j in range(parts):
        pieces = []
        for i in range(2):
            one = trace[2 * j, i]
            two = trace[2 * j + 1, i]
            pieces.append(jnp.where(lane_rows < width, one, pltpu.roll(two, width, 1)))
            pieces.append(jnp.where(lane_rows < width, pltpu.roll(one, width, 1), two))
        both = jnp.concatenate(pieces, 0)
        part_a = both.astype(jnp.bfloat16)
        rest = both - part_a.astype(jnp.float32)
        part_b = rest.astype(jnp.bfloat16)
        part_c = (rest - part_b.astype(jnp.float32)).astype(jnp.bfloat16)
        total = jnp.dot(place, part_a, preferred_element_type=jnp.float32)
        total += jnp.dot(place, part_b, preferred_element_type=jnp.float32)
        total += jnp.dot(place, part_c, preferred_element_type=jnp.float32)
        panel_keep_ref[pl.ds(j, count, stride=parts)] = total[:count]
        panel_send_ref[pl.ds(j, count, stride=parts)] = total[count:]


def shards(
    pressure_start, along_start, cross_start, depth_layers, stiffness, patch_lists, owner_map
):
    sensors, layers, rows, cols = pressure_start.shape
    f32 = jnp.float32
    along_count = lax.axis_size("along")
    cross_count = lax.axis_size("cross")
    along = lax.axis_index("along")
    cross = lax.axis_index("cross")
    low = cross == 0
    swap = [(0, 1), (1, 0)]
    pair = ("along", "cross")
    steps_up = range(along_count - 1)
    route_one = [(2 * i, 2 * i + 2) for i in steps_up] + [(2 * i + 3, 2 * i + 1) for i in steps_up]
    route_two = [(2 * i + 1, 2 * i + 2) for i in steps_up] + [(2 * i + 2, 2 * i + 1) for i in steps_up]
    half_rows = rows // 2
    span = half_rows + SUB
    wide = span + SUB
    pack_rows = 2 * span * layers + 3 * span + layers
    end_rows = 2 * SUB * layers + 3 * SUB

    spec = pl.BlockSpec(memory_space=VMEM)
    keep, send, one, two = pl.pallas_call(
        edges_kernel,
        out_shape=[
            jax.ShapeDtypeStruct((pack_rows, cols), f32),
            jax.ShapeDtypeStruct((pack_rows, cols), f32),
            jax.ShapeDtypeStruct((end_rows, cols), f32),
            jax.ShapeDtypeStruct((end_rows, cols), f32),
        ],
        in_specs=[spec] * 5,
        out_specs=[spec] * 4,
        compiler_params=pltpu.CompilerParams(vmem_limit_bytes=32 * 1024 * 1024),
        name="edges",
    )(pressure_start[0], along_start[0], cross_start[0], depth_layers, stiffness)

    other_owners = lax.ppermute(owner_map, "cross", swap)
    other = lax.ppermute(send, "cross", swap)
    near = lax.ppermute(one, pair, route_one)
    far = lax.ppermute(two, pair, route_two)

    patch_count = 2 * rows
    capacity = patch_count // (along_count * cross_count) + 1
    owners = jnp.where(low, jnp.stack([owner_map[0], other_owners[0]]), jnp.stack([other_owners[0], owner_map[0]]))
    positions = jnp.arange(patch_count, dtype=jnp.int32)
    earlier = positions[None, :] < positions[:, None]
    rank = jnp.sum(((owners[:, :, None] == owners[:, None, :]) & earlier).astype(jnp.int32), axis=2)
    local_ids = patch_lists[0] - along * cross_count * patch_count
    member = jnp.any(local_ids[:, None] == jnp.arange(2 * patch_count, dtype=jnp.int32)[None, :], axis=0)
    to_chip = owners // cross_count
    rotate = along_count <= 4
    if rotate:
        to_chip = (to_chip - along) % along_count
    block = jnp.arange(2, dtype=jnp.int32)[:, None]
    count = along_count * 2 * capacity
    target = (to_chip * 2 + block) * capacity + rank + jnp.where(owners % cross_count == cross, 0, count)
    target = jnp.where(member.reshape(2, patch_count), target, -1).reshape(2, 2, half_rows, 2)
    target = jnp.where(low, target[:, 0], target[:, 1])
    target = jnp.swapaxes(target, 1, 2).reshape(patch_count)
    place = (jnp.arange(2 * count, dtype=jnp.int32)[:, None] == target[None, :]).astype(jnp.bfloat16)

    parts = STEPS // 2
    p_keep, p_send, panel_keep, panel_send = pl.pallas_call(
        steps_kernel,
        out_shape=[
            jax.ShapeDtypeStruct((layers, half_rows, cols), f32),
            jax.ShapeDtypeStruct((layers, half_rows, cols), f32),
            jax.ShapeDtypeStruct((count * parts, cols), f32),
            jax.ShapeDtypeStruct((count * parts, cols), f32),
        ],
        in_specs=[spec] * 5,
        out_specs=[spec] * 4,
        scratch_shapes=[
            VMEM((2, layers, wide + 2 * SUB, cols), f32),
            VMEM((2, layers, wide, cols), f32),
            VMEM((2, wide + SUB, cols), f32),
            VMEM((2, wide, cols), f32),
            VMEM((STEPS, 2, half_rows, cols), f32),
            VMEM((2, layers, wide + SUB, cols), f32),
            VMEM((2, layers, wide, cols), f32),
            VMEM((2, layers - 1, wide, cols), f32),
            VMEM((2, layers, wide + 2 * SUB, cols), f32),
            VMEM((2, layers, wide, cols), f32),
        ],
        compiler_params=pltpu.CompilerParams(vmem_limit_bytes=32 * 1024 * 1024),
        name="steps",
    )(keep, other, near, far, place)

    panels = panel_keep + lax.ppermute(panel_send, "cross", swap)
    panels = panels.reshape(along_count, 2 * capacity * parts, cols)
    if rotate:
        received = [panels[0]]
        for k in range(1, along_count):
            route = [(i, (i + k) % along_count) for i in range(along_count)]
            received.append(lax.ppermute(panels[k], "along", route))
        order = (along - jnp.arange(along_count, dtype=jnp.int32)) % along_count
        received = jnp.stack(received)[order]
    else:
        received = lax.all_to_all(panels, "along", split_axis=0, concat_axis=0, tiled=True)
    received = received.reshape(1, along_count * 2 * capacity, 1, parts * cols)

    p_other = lax.ppermute(p_send, "cross", swap)
    pressure = jnp.where(
        low, jnp.concatenate([p_keep, p_other], 1), jnp.concatenate([p_other, p_keep], 1)
    )
    return (pressure[None], received)


def solution(mesh):
    in_specs = (
        P("batch", None, "along", "cross"),
        P("batch", None, "along", "cross"),
        P("batch", None, "along", "cross"),
        P("along", "cross"),
        P("along", "cross"),
        P("batch", None),
        P(("along", "cross"), None),
    )
    out_specs = (P("batch", None, "along", "cross"), P(("along", "cross"), None, "batch", None))
    return jax.shard_map(shards, mesh=mesh, in_specs=in_specs, out_specs=out_specs, check_vma=False)
```

```python
import functools

import jax
import jax.numpy as jnp
from jax import lax
from jax.experimental import pallas as pl
from jax.experimental.pallas import tpu as pltpu
from jax.sharding import PartitionSpec as P

STEPS = 8
SUB = 8
VMEM = pltpu.VMEM


def lanes_of(shape):
    return lax.broadcasted_iota(jnp.int32, shape, len(shape) - 1)


def rows_of(shape):
    return lax.broadcasted_iota(jnp.int32, shape, len(shape) - 2)


def edges_kernel(
    p_hbm, fa_hbm, fc_hbm, depth_hbm, stiff_hbm, owner_hbm,
    keep_ref, send_ref, one_ref, two_ref,
    p_ref, fa_ref, fc_ref, depth_ref, stiff_ref, owner_ref, sems,
):
    copies = [
        pltpu.make_async_copy(source, target, sems.at[i])
        for i, (source, target) in enumerate(
            (
                (depth_hbm, depth_ref),
                (stiff_hbm, stiff_ref),
                (owner_hbm, owner_ref),
                (fa_hbm, fa_ref),
                (fc_hbm, fc_ref),
                (p_hbm, p_ref),
            )
        )
    ]
    for copy in copies:
        copy.start()
    for copy in copies:
        copy.wait()
    layers, rows, cols = p_ref.shape
    low = lax.axis_index("cross") == 0
    span = rows // 2 + SUB
    last = rows - SUB
    lane = lanes_of((rows, cols))
    row = rows_of((rows, cols))
    row_sub = rows_of((SUB, cols))
    depth = depth_ref[...]
    stiff = stiff_ref[...]
    first_lane = lane == 0
    slot_one = row_sub == jnp.where(low, 0, -1)
    slot_two = row_sub == jnp.where(low, -1, 0)
    base = 2 * span * layers
    base_z = 2 * SUB * layers
    velocity = jnp.zeros((rows, cols), jnp.float32)

    def halves(array):
        first, second = array[:span], array[rows - span :]
        return jnp.where(low, first, second), jnp.where(low, second, first)

    def ends(array):
        first, second = array[:SUB], array[last:]
        return jnp.where(low, second, first), jnp.where(low, first, second)

    for z in range(layers):
        wet = depth > z
        p = p_ref[z]
        va = jnp.where(wet, fa_ref[z], 0.0)
        vc = jnp.where(wet, fc_ref[z], 0.0)
        behind = jnp.where(row == 0, 0.0, pltpu.roll(va, 1, 0))
        before = jnp.where(first_lane, 0.0, pltpu.roll(vc, 1, 1))
        w = (va - behind) + (vc - before)
        velocity = jnp.where(lane == z, pltpu.roll(vc, z + 1, 1), velocity)
        at = 2 * span * z
        keep_ref[at : at + span], send_ref[at : at + span] = halves(p)
        at += span
        keep_ref[at : at + span], send_ref[at : at + span] = halves(w)
        final = va[rows - 1 : rows]
        at = base + 3 * span + z
        keep_ref[at : at + 1] = final
        send_ref[at : at + 1] = final
        at = 2 * SUB * z
        one_ref[at : at + SUB], two_ref[at : at + SUB] = ends(p)
        at += SUB
        one, two = ends(w)
        final = jnp.broadcast_to(final, (SUB, cols))
        one_ref[at : at + SUB] = jnp.where(slot_one, final, one)
        two_ref[at : at + SUB] = jnp.where(slot_two, final, two)
    for i, array in enumerate((depth.astype(jnp.float32), stiff, velocity)):
        at = base + span * i
        keep_ref[at : at + span], send_ref[at : at + span] = halves(array)
        at = base_z + SUB * i
        one_ref[at : at + SUB], two_ref[at : at + SUB] = ends(array)
    at = base + 3 * span + layers
    owners = owner_ref[...].astype(jnp.float32)
    send_ref[at : at + SUB] = jnp.broadcast_to(owners, (SUB, cols))


def place_kernel(ids_ref, own_ref, other_ref, place_ref, *, owner_count, chips, capacity):
    along = lax.axis_index("along")
    cross = lax.axis_index("cross")
    low = cross == 0
    cores = owner_count // chips
    patches = own_ref.shape[1]
    last = other_ref.shape[0] - SUB
    own = own_ref[...].astype(jnp.float32)
    other = other_ref[last : last + 1]
    owners = [jnp.where(low, own, other), jnp.where(low, other, own)]
    lane = lanes_of((patches, patches))
    half = patches // 2
    block = lane // half
    within = lane % half
    patch = half * cross + 2 * (within % (half // 2)) + within // (half // 2)
    source = rows_of((patches, patches))
    number = rows_of((owner_count, patches)).astype(jnp.float32)
    chosen = jnp.zeros((owner_count, patches), jnp.float32)
    counts = jnp.zeros((owner_count, patches), jnp.float32)
    for i in range(2):
        held = (number == owners[i]).astype(jnp.bfloat16)
        pick = jnp.where(block == i, jnp.where(source == patch, 1.0, 0.0), 0.0).astype(jnp.bfloat16)
        earlier = jnp.where(block == i, jnp.where(source < patch, 1.0, 0.0), 0.0).astype(jnp.bfloat16)
        chosen += jnp.dot(held, pick, preferred_element_type=jnp.float32)
        counts += jnp.dot(held, earlier, preferred_element_type=jnp.float32)
    rank = jnp.sum(chosen * counts, axis=0, keepdims=True).astype(jnp.int32)
    owner = jnp.sum(chosen * number, axis=0, keepdims=True).astype(jnp.int32)
    wanted = (along * cores + block) * patches + patch
    found = jnp.zeros((patches, patches), jnp.float32)
    for j in range(ids_ref.shape[1]):
        found = jnp.where(ids_ref[:, j : j + 1] == wanted, 1.0, found)
    member = jnp.sum(found, axis=0, keepdims=True)
    block = block[:1]
    chip = owner // cores
    owner_core = owner % cores
    some = 2 * capacity
    slot = block * capacity + rank
    if chips == 4:
        ahead = lax.rem(chip - along + chips, chips)
        near = lax.rem(ahead, 2) == 1
        handler = jnp.where(near, ahead // 2, owner_core)
        slot = slot + jnp.where(
            near, jnp.where(owner_core == handler, 0, some), jnp.where(ahead == 2, 2 * some, 3 * some)
        )
    else:
        handler = owner_core
        slot = slot + chip * some
    slot = jnp.where(handler == cross, slot, slot + chips * some)
    slot = jnp.where(member > 0.0, slot, -1)
    place_ref[...] = jnp.where(rows_of(place_ref.shape) == slot, 1.0, 0.0).astype(jnp.bfloat16)


def gather_kernel(own_ref, near_ref, far_ref, swapped_ref, out_ref, sems):
    chips = 4
    along = lax.axis_index("along")
    cross = lax.axis_index("cross")
    count = out_ref.shape[0] // chips
    copies = []
    for i, (ref, ahead) in enumerate(
        ((own_ref, 0), (near_ref, 3 - 2 * cross), (far_ref, 2), (swapped_ref, 1 + 2 * cross))
    ):
        at = pl.multiple_of(lax.rem(along + ahead, chips) * count, SUB)
        copies.append(pltpu.make_async_copy(ref, out_ref.at[pl.ds(at, count)], sems.at[i]))
    for copy in copies:
        copy.start()
    for copy in copies:
        copy.wait()


def steps_kernel(
    keep_ref,
    other_ref,
    halo_ref,
    place_ref,
    p_keep_ref,
    p_send_ref,
    panel_keep_ref,
    panel_send_ref,
    p_buf,
    w_buf,
    d_buf,
    s_buf,
    trace,
    wet_buf,
    scale_buf,
    half_buf,
    p_two,
    w_two,
):
    layers, half_rows, cols = p_keep_ref.shape
    core = lax.axis_index("cross")
    low = core == 0
    span = half_rows + SUB
    wide = span + SUB
    blocks = wide // SUB
    base = 2 * span * layers
    base_z = 2 * SUB * layers
    ends = halo_ref.shape[0] // 2
    one_ref = halo_ref.at[:ends]
    two_ref = halo_ref.at[ends:]
    lane = lanes_of((SUB, cols))
    row = rows_of((SUB, cols))
    middle = pl.multiple_of(SUB * (1 - core), SUB)
    halo = pl.multiple_of(span * core, SUB)

    def left(own, other):
        return jnp.where(low, own, other)

    seam_span = left(keep_ref[base + 2 * span : base + 3 * span], other_ref[base + 2 * span : base + 3 * span])
    seam_halo = left(one_ref[base_z + 2 * SUB : base_z + 3 * SUB], two_ref[base_z + 2 * SUB : base_z + 3 * SUB])
    top_row = row == jnp.where(low, 0, -1)
    end_row = row == jnp.where(low, -1, 0)
    zeros = jnp.zeros((SUB, cols), jnp.float32)
    for tile, main_ref, end_ref, seam_core in ((core, keep_ref, one_ref, 1), (1 - core, other_ref, two_ref, 0)):
        seam_lane = jnp.where(core == seam_core, 0, -1)
        seam = lanes_of((span, cols)) == seam_lane
        seam_sub = lane == seam_lane
        for z in range(layers):
            at = 2 * span * z
            at_z = 2 * SUB * z
            p_buf[tile, z, :SUB] = zeros
            p_two[tile, z, :SUB] = zeros
            p_two[tile, z, SUB + wide :] = zeros
            p_buf[tile, z, pl.ds(middle + SUB, span)] = main_ref[at : at + span]
            p_buf[tile, z, pl.ds(halo + SUB, SUB)] = end_ref[at_z : at_z + SUB]
            p_buf[tile, z, SUB + wide :] = zeros
            turn = (cols - z) % cols
            w = main_ref[at + span : at + 2 * span]
            w = w - jnp.where(seam, pltpu.roll(seam_span, turn, 1) if turn else seam_span, 0.0)
            w_halo = end_ref[at_z + SUB : at_z + 2 * SUB]
            slot = jnp.broadcast_to(w_halo[0:1], (SUB, cols))
            final = jnp.broadcast_to(main_ref[base + 3 * span + z : base + 3 * span + z + 1], (SUB, cols))
            w_halo = w_halo - jnp.where(seam_sub, pltpu.roll(seam_halo, turn, 1) if turn else seam_halo, 0.0)
            w_halo = w_halo - jnp.where(end_row, final, 0.0)
            w_top = w[:SUB] - jnp.where(top_row, slot, 0.0)
            w_buf[tile, z, pl.ds(middle, SUB)] = w_top
            w_buf[tile, z, pl.ds(middle + SUB, span - SUB)] = w[SUB:]
            w_buf[tile, z, pl.ds(halo, SUB)] = w_halo
        d_buf[tile, :SUB] = zeros
        for buf, i, shift in ((d_buf, 0, SUB), (s_buf, 1, 0)):
            buf[tile, pl.ds(middle + shift, span)] = main_ref[base + i * span : base + (i + 1) * span]
            buf[tile, pl.ds(halo + shift, SUB)] = end_ref[base_z + i * SUB : base_z + (i + 1) * SUB]

    zs = range(layers)
    for i in range(2):
        for z in zs:
            wet = d_buf[i, SUB:] > float(z)
            if True:
                wet_buf[i, z, :SUB] = zeros
                wet_buf[i, z, SUB:] = jnp.where(wet, 1.0, 0.0)
            if True:
                scale_buf[i, z] = jnp.where(wet, s_buf[i], 0.0)
            if True and z > 0:
                half_buf[i, z - 1] = jnp.where(wet, 0.5, 0.0)
    ZB = 4
    groups = layers // ZB
    lane = lanes_of((ZB, wide, cols))
    last_lane = lane == cols - 1
    first_lane = lane == 0
    here = slice(SUB, SUB + wide)
    ahead = slice(SUB + 1, SUB + 1 + wide)
    back_rows = slice(SUB - 1, SUB - 1 + wide)

    def step(t, first, p_buf, w_buf, p_out, w_out):
        def stage_a(g):
            zs = slice(g * ZB, (g + 1) * ZB)
            return [pltpu.roll(p_buf[i, zs, here], cols - 1, 2) for i in range(2)]

        def stage_b(g, turned):
            zs = slice(g * ZB, (g + 1) * ZB)
            right = [
                jnp.where(last_lane, turned[1], turned[0]),
                jnp.where(last_lane, 0.0, turned[1]),
            ]
            gy = [wet_buf[i, zs, SUB:] * (right[i] - p_buf[i, zs, here]) for i in range(2)]
            return gy, [pltpu.roll(gy[i], 1, 2) for i in range(2)]

        hz_last = [None, None]
        surface = [None, None]

        def stage_c(g, gy, back):
            zs = slice(g * ZB, (g + 1) * ZB)
            before = [
                jnp.where(first_lane, 0.0, back[0]),
                jnp.where(first_lane, back[0], back[1]),
            ]
            for i in range(2):
                p = p_buf[i, zs, here]
                w = w_buf[i, zs] - (gy[i] - before[i])
                gx = wet_buf[i, zs, SUB:] * (p_buf[i, zs, ahead] - p)
                behind = wet_buf[i, zs, SUB - 1 : SUB - 1 + wide] * (p - p_buf[i, zs, back_rows])
                w = w - (gx - behind)
                w_out[i, zs] = w
                if g + 1 < groups:
                    hz = half_buf[i, zs] * (p_buf[i, g * ZB + 1 : (g + 1) * ZB + 1, here] - p)
                elif ZB > 1:
                    hz = jnp.concatenate([half_buf[i, g * ZB :] * (p[1:] - p[:-1]), jnp.zeros((1, wide, cols), jnp.float32)], 0)
                else:
                    hz = jnp.zeros((1, wide, cols), jnp.float32)
                prev = jnp.zeros((1, wide, cols), jnp.float32) if g == 0 else hz_last[i]
                flux = w - (hz - (jnp.concatenate([prev, hz[:-1]], 0) if ZB > 1 else prev))
                hz_last[i] = hz[-1:]
                old = wet_buf[i, zs, SUB:] * p if first else p
                new = old - scale_buf[i, zs] * flux
                p_out[i, zs, here] = new
                for k in range(ZB):
                    part = new[k, SUB:span]
                    z = g * ZB + k
                    surface[i] = part if z == 0 else jnp.where(d_buf[i, 2 * SUB : SUB + span] > float(z), part, surface[i])

        turned = [stage_a(0), stage_a(1)]
        ready = stage_b(0, turned[0])
        for g in range(groups):
            if g + 2 < groups:
                turned.append(stage_a(g + 2))
            coming = stage_b(g + 1, turned[g + 1]) if g + 1 < groups else None
            stage_c(g, *ready)
            ready = coming
        for i in range(2):
            trace[t, i] = surface[i]

    def two(k, carry):
        step(2 * k, False, p_buf, w_buf, p_two, w_two)
        step(2 * k + 1, False, p_two, w_two, p_buf, w_buf)
        return carry

    step(0, True, p_buf, w_buf, p_two, w_two)
    step(1, False, p_two, w_two, p_buf, w_buf)
    lax.fori_loop(1, STEPS // 2, two, 0)
    for z in zs:
        p_keep_ref[z] = p_buf[core, z, 2 * SUB : 2 * SUB + half_rows]
        p_send_ref[z] = p_buf[1 - core, z, 2 * SUB : 2 * SUB + half_rows]

    width = cols // 2
    lane_rows = lanes_of((half_rows, cols))
    place = place_ref[...]
    count = place.shape[0] // 2
    parts = STEPS // 2
    for j in range(parts):
        pieces = []
        for i in range(2):
            one = trace[2 * j, i]
            two = trace[2 * j + 1, i]
            pieces.append(jnp.where(lane_rows < width, one, pltpu.roll(two, width, 1)))
            pieces.append(jnp.where(lane_rows < width, pltpu.roll(one, width, 1), two))
        both = jnp.concatenate(pieces, 0)
        part_a = both.astype(jnp.bfloat16)
        rest = both - part_a.astype(jnp.float32)
        part_b = rest.astype(jnp.bfloat16)
        part_c = (rest - part_b.astype(jnp.float32)).astype(jnp.bfloat16)
        total = jnp.dot(place, part_a, preferred_element_type=jnp.float32)
        total += jnp.dot(place, part_b, preferred_element_type=jnp.float32)
        total += jnp.dot(place, part_c, preferred_element_type=jnp.float32)
        panel_keep_ref[pl.ds(j, count, stride=parts)] = total[:count]
        panel_send_ref[pl.ds(j, count, stride=parts)] = total[count:]


def shards(
    pressure_start, along_start, cross_start, depth_layers, stiffness, patch_lists, owner_map
):
    sensors, layers, rows, cols = pressure_start.shape
    f32 = jnp.float32
    along_count = lax.axis_size("along")
    cross_count = lax.axis_size("cross")
    low = lax.axis_index("cross") == 0
    swap = [(0, 1), (1, 0)]
    pair = ("along", "cross")
    steps_up = range(along_count - 1)
    route = [(2 * i, 2 * i + 2) for i in steps_up] + [(2 * i + 3, 2 * i + 1) for i in steps_up]
    half_rows = rows // 2
    span = half_rows + SUB
    wide = span + SUB
    pack_rows = 2 * span * layers + 3 * span + layers
    end_rows = 2 * SUB * layers + 3 * SUB

    spec = pl.BlockSpec(memory_space=VMEM)
    hbm = pl.BlockSpec(memory_space=pltpu.HBM)
    params = pltpu.CompilerParams(vmem_limit_bytes=32 * 1024 * 1024)
    keep, send, one, two = pl.pallas_call(
        edges_kernel,
        out_shape=[
            jax.ShapeDtypeStruct((pack_rows, cols), f32),
            jax.ShapeDtypeStruct((pack_rows + SUB, cols), f32),
            jax.ShapeDtypeStruct((end_rows, cols), f32),
            jax.ShapeDtypeStruct((end_rows, cols), f32),
        ],
        in_specs=[hbm] * 6,
        out_specs=[spec] * 4,
        scratch_shapes=[
            VMEM((layers, rows, cols), f32),
            VMEM((layers, rows, cols), f32),
            VMEM((layers, rows, cols), f32),
            VMEM((rows, cols), jnp.int32),
            VMEM((rows, cols), f32),
            VMEM(owner_map.shape, jnp.int32),
            pltpu.SemaphoreType.DMA((6,)),
        ],
        compiler_params=params,
        name="edges",
    )(pressure_start[0], along_start[0], cross_start[0], depth_layers, stiffness, owner_map)

    halo = jnp.concatenate([one, lax.ppermute(two, "cross", swap)], 0)
    other = lax.ppermute(send, "cross", swap)
    halo = lax.ppermute(halo, pair, route)

    patch_count = 2 * rows
    owner_count = along_count * cross_count
    capacity = patch_count // owner_count + 1
    count = owner_count * capacity
    place = pl.pallas_call(
        functools.partial(
            place_kernel, owner_count=owner_count, chips=along_count, capacity=capacity
        ),
        out_shape=jax.ShapeDtypeStruct((2 * count, patch_count), jnp.bfloat16),
        in_specs=[spec] * 3,
        out_specs=spec,
        compiler_params=params,
        name="place",
    )(patch_lists.reshape(-1, patch_count).T, owner_map, other)

    parts = STEPS // 2
    p_keep, p_send, panel_keep, panel_send = pl.pallas_call(
        steps_kernel,
        out_shape=[
            jax.ShapeDtypeStruct((layers, half_rows, cols), f32),
            jax.ShapeDtypeStruct((layers, half_rows, cols), f32),
            jax.ShapeDtypeStruct((count * parts, cols), f32),
            jax.ShapeDtypeStruct((count * parts, cols), f32),
        ],
        in_specs=[spec] * 4,
        out_specs=[spec] * 4,
        scratch_shapes=[
            VMEM((2, layers, wide + 2 * SUB, cols), f32),
            VMEM((2, layers, wide, cols), f32),
            VMEM((2, wide + SUB, cols), f32),
            VMEM((2, wide, cols), f32),
            VMEM((STEPS, 2, half_rows, cols), f32),
            VMEM((2, layers, wide + SUB, cols), f32),
            VMEM((2, layers, wide, cols), f32),
            VMEM((2, layers - 1, wide, cols), f32),
            VMEM((2, layers, wide + 2 * SUB, cols), f32),
            VMEM((2, layers, wide, cols), f32),
        ],
        compiler_params=params,
        name="steps",
    )(keep, other, halo, place)

    panels = panel_keep + lax.ppermute(panel_send, "cross", swap)
    if along_count == 4:
        some = 2 * capacity * parts
        ring = range(along_count)
        near_route = [(2 * i, 2 * ((i + 1) % along_count)) for i in ring]
        near_route += [(2 * ((i + 1) % along_count) + 1, 2 * i + 1) for i in ring]
        near = lax.ppermute(panels[: 2 * some], pair, near_route)
        far = lax.ppermute(
            panels[2 * some : 3 * some], "along", [(i, (i + 2) % along_count) for i in ring]
        )
        swapped = lax.ppermute(near[some:], "cross", swap)
        received = pl.pallas_call(
            gather_kernel,
            out_shape=jax.ShapeDtypeStruct((count * parts, cols), f32),
            in_specs=[spec] * 4,
            out_specs=hbm,
            scratch_shapes=[pltpu.SemaphoreType.DMA((4,))],
            compiler_params=params,
            name="gather",
        )(panels[3 * some :], near[:some], far, swapped)
    else:
        panels = panels.reshape(along_count, 2 * capacity * parts, cols)
        received = lax.all_to_all(panels, "along", split_axis=0, concat_axis=0, tiled=True)
    received = received.reshape(1, count, 1, parts * cols)

    p_other = lax.ppermute(p_send, "cross", swap)
    pressure = jnp.where(
        low, jnp.concatenate([p_keep, p_other], 1), jnp.concatenate([p_other, p_keep], 1)
    )
    return (pressure[None], received)


def solution(mesh):
    in_specs = (
        P("batch", None, "along", "cross"),
        P("batch", None, "along", "cross"),
        P("batch", None, "along", "cross"),
        P("along", "cross"),
        P("along", "cross"),
        P("batch", None),
        P(("along", "cross"), None),
    )
    out_specs = (P("batch", None, "along", "cross"), P(("along", "cross"), None, "batch", None))
    return jax.shard_map(shards, mesh=mesh, in_specs=in_specs, out_specs=out_specs, check_vma=False)
```

```python
import functools

import jax
import jax.numpy as jnp
from jax import lax
from jax.experimental import pallas as pl
from jax.experimental.pallas import tpu as pltpu
from jax.sharding import PartitionSpec as P

STEPS = 8
SUB = 8
VMEM = pltpu.VMEM


def lanes_of(shape):
    return lax.broadcasted_iota(jnp.int32, shape, len(shape) - 1)


def rows_of(shape):
    return lax.broadcasted_iota(jnp.int32, shape, len(shape) - 2)


def edges_kernel(
    p_hbm, fa_hbm, fc_hbm, depth_hbm, stiff_hbm, owner_hbm,
    keep_ref, send_ref, one_ref, two_ref,
    p_ref, fa_ref, fc_ref, depth_ref, stiff_ref, owner_ref, sems,
):
    copies = [
        pltpu.make_async_copy(source, target, sems.at[i])
        for i, (source, target) in enumerate(
            (
                (depth_hbm, depth_ref),
                (stiff_hbm, stiff_ref),
                (owner_hbm, owner_ref),
                (fa_hbm, fa_ref),
                (fc_hbm, fc_ref),
                (p_hbm, p_ref),
            )
        )
    ]
    for copy in copies:
        copy.start()
    for copy in copies:
        copy.wait()
    layers, rows, cols = p_ref.shape
    low = lax.axis_index("cross") == 0
    span = rows // 2 + SUB
    last = rows - SUB
    lane = lanes_of((rows, cols))
    row = rows_of((rows, cols))
    row_sub = rows_of((SUB, cols))
    depth = depth_ref[...]
    stiff = stiff_ref[...]
    first_lane = lane == 0
    slot_one = row_sub == jnp.where(low, 0, -1)
    slot_two = row_sub == jnp.where(low, -1, 0)
    base = 2 * span * layers
    base_z = 2 * SUB * layers
    velocity = jnp.zeros((rows, cols), jnp.float32)

    def halves(array):
        first, second = array[:span], array[rows - span :]
        return jnp.where(low, first, second), jnp.where(low, second, first)

    def ends(array):
        first, second = array[:SUB], array[last:]
        return jnp.where(low, second, first), jnp.where(low, first, second)

    for z in range(layers):
        wet = depth > z
        p = p_ref[z]
        va = jnp.where(wet, fa_ref[z], 0.0)
        vc = jnp.where(wet, fc_ref[z], 0.0)
        behind = jnp.where(row == 0, 0.0, pltpu.roll(va, 1, 0))
        before = jnp.where(first_lane, 0.0, pltpu.roll(vc, 1, 1))
        w = (va - behind) + (vc - before)
        velocity = jnp.where(lane == z, pltpu.roll(vc, z + 1, 1), velocity)
        at = 2 * span * z
        keep_ref[at : at + span], send_ref[at : at + span] = halves(p)
        at += span
        keep_ref[at : at + span], send_ref[at : at + span] = halves(w)
        final = va[rows - 1 : rows]
        at = base + 3 * span + z
        keep_ref[at : at + 1] = final
        send_ref[at : at + 1] = final
        at = 2 * SUB * z
        one_ref[at : at + SUB], two_ref[at : at + SUB] = ends(p)
        at += SUB
        one, two = ends(w)
        final = jnp.broadcast_to(final, (SUB, cols))
        one_ref[at : at + SUB] = jnp.where(slot_one, final, one)
        two_ref[at : at + SUB] = jnp.where(slot_two, final, two)
    for i, array in enumerate((depth.astype(jnp.float32), stiff, velocity)):
        at = base + span * i
        keep_ref[at : at + span], send_ref[at : at + span] = halves(array)
        at = base_z + SUB * i
        one_ref[at : at + SUB], two_ref[at : at + SUB] = ends(array)
    at = base + 3 * span + layers
    owners = owner_ref[...].astype(jnp.float32)
    send_ref[at : at + SUB] = jnp.broadcast_to(owners, (SUB, cols))


def place_kernel(ids_ref, own_ref, other_ref, place_ref, *, owner_count, chips, capacity):
    along = lax.axis_index("along")
    cross = lax.axis_index("cross")
    low = cross == 0
    cores = owner_count // chips
    patches = own_ref.shape[1]
    last = other_ref.shape[0] - SUB
    own = own_ref[...].astype(jnp.float32)
    other = other_ref[last : last + 1]
    owners = [jnp.where(low, own, other), jnp.where(low, other, own)]
    lane = lanes_of((patches, patches))
    half = patches // 2
    block = lane // half
    within = lane % half
    patch = half * cross + 2 * (within % (half // 2)) + within // (half // 2)
    source = rows_of((patches, patches))
    number = rows_of((owner_count, patches)).astype(jnp.float32)
    chosen = jnp.zeros((owner_count, patches), jnp.float32)
    counts = jnp.zeros((owner_count, patches), jnp.float32)
    for i in range(2):
        held = (number == owners[i]).astype(jnp.bfloat16)
        pick = jnp.where(block == i, jnp.where(source == patch, 1.0, 0.0), 0.0).astype(jnp.bfloat16)
        earlier = jnp.where(block == i, jnp.where(source < patch, 1.0, 0.0), 0.0).astype(jnp.bfloat16)
        chosen += jnp.dot(held, pick, preferred_element_type=jnp.float32)
        counts += jnp.dot(held, earlier, preferred_element_type=jnp.float32)
    rank = jnp.sum(chosen * counts, axis=0, keepdims=True).astype(jnp.int32)
    owner = jnp.sum(chosen * number, axis=0, keepdims=True).astype(jnp.int32)
    wanted = (along * cores + block) * patches + patch
    found = jnp.zeros((patches, patches), jnp.float32)
    for j in range(ids_ref.shape[1]):
        found = jnp.where(ids_ref[:, j : j + 1] == wanted, 1.0, found)
    member = jnp.sum(found, axis=0, keepdims=True)
    block = block[:1]
    chip = owner // cores
    owner_core = owner % cores
    some = 2 * capacity
    slot = block * capacity + rank
    if chips == 4:
        ahead = lax.rem(chip - along + chips, chips)
        near = lax.rem(ahead, 2) == 1
        handler = jnp.where(near, ahead // 2, owner_core)
        slot = slot + jnp.where(
            near, jnp.where(owner_core == handler, 0, some), jnp.where(ahead == 2, 2 * some, 3 * some)
        )
    else:
        handler = owner_core
        slot = slot + chip * some
    slot = jnp.where(handler == cross, slot, slot + chips * some)
    slot = jnp.where(member > 0.0, slot, -1)
    place_ref[...] = jnp.where(rows_of(place_ref.shape) == slot, 1.0, 0.0).astype(jnp.bfloat16)


def gather_kernel(own_ref, near_ref, far_ref, swapped_ref, out_ref, sems):
    chips = 4
    along = lax.axis_index("along")
    cross = lax.axis_index("cross")
    count = out_ref.shape[0] // chips
    copies = []
    for i, (ref, ahead) in enumerate(
        ((own_ref, 0), (near_ref, 3 - 2 * cross), (far_ref, 2), (swapped_ref, 1 + 2 * cross))
    ):
        at = pl.multiple_of(lax.rem(along + ahead, chips) * count, SUB)
        copies.append(pltpu.make_async_copy(ref, out_ref.at[pl.ds(at, count)], sems.at[i]))
    for copy in copies:
        copy.start()
    for copy in copies:
        copy.wait()


def prepare_kernel(
    keep_ref, other_ref, two_in_ref,
    two_ref, p_buf, w_buf, d_buf, wet_buf, scale_buf, half_buf,
):
    layers = p_buf.shape[1]
    cols = p_buf.shape[3]
    core = lax.axis_index("cross")
    low = core == 0
    wide = w_buf.shape[2]
    span = wide - SUB
    base = 2 * span * layers
    lane = lanes_of((span, cols))
    middle = pl.multiple_of(SUB * (1 - core), SUB)
    zeros = jnp.zeros((SUB, cols), jnp.float32)
    two_ref[...] = two_in_ref[...]
    at = base + 2 * span
    seam = jnp.where(low, keep_ref[at : at + span], other_ref[at : at + span])
    for tile, main_ref, seam_core in ((core, keep_ref, 1), (1 - core, other_ref, 0)):
        seam_lane = lane == jnp.where(core == seam_core, 0, -1)
        depth = main_ref[base : base + span]
        stiff = main_ref[base + span : base + 2 * span]
        d_buf[tile, :SUB] = zeros
        d_buf[tile, pl.ds(middle + SUB, span)] = depth
        for z in range(layers):
            at = 2 * span * z
            p_buf[tile, z, :SUB] = zeros
            p_buf[tile, z, SUB + wide :] = zeros
            p_buf[tile, z, pl.ds(middle + SUB, span)] = main_ref[at : at + span]
            turned = pltpu.roll(seam, cols - z, 1) if z else seam
            w_buf[tile, z, pl.ds(middle, span)] = main_ref[at + span : at + 2 * span] - jnp.where(
                seam_lane, turned, 0.0
            )
            wet = depth > float(z)
            wet_buf[tile, z, :SUB] = zeros
            wet_buf[tile, z, pl.ds(middle + SUB, span)] = jnp.where(wet, 1.0, 0.0)
            scale_buf[tile, z, pl.ds(middle, span)] = jnp.where(wet, stiff, 0.0)
            if z > 0:
                half_buf[tile, z - 1, pl.ds(middle, span)] = jnp.where(wet, 0.5, 0.0)


def steps_kernel(
    keep_ref, other_ref, one_ref, two_ref, place_ref,
    p_in, w_in, d_in, wet_in, scale_in, half_in,
    p_keep_ref, p_send_ref, panel_keep_ref, panel_send_ref,
    p_buf, w_buf, d_buf, wet_buf, scale_buf, half_buf,
    trace, p_two, w_two,
):
    layers, half_rows, cols = p_keep_ref.shape
    core = lax.axis_index("cross")
    low = core == 0
    span = half_rows + SUB
    wide = span + SUB
    base = 2 * span * layers
    base_z = 2 * SUB * layers
    lane = lanes_of((SUB, cols))
    row = rows_of((SUB, cols))
    middle = pl.multiple_of(SUB * (1 - core), SUB)
    halo = pl.multiple_of(span * core, SUB)
    at = base_z + 2 * SUB
    seam = jnp.where(low, one_ref[at : at + SUB], two_ref[at : at + SUB])
    top_row = row == jnp.where(low, 0, -1)
    end_row = row == jnp.where(low, -1, 0)
    zeros = jnp.zeros((SUB, cols), jnp.float32)
    for tile, main_ref, end_ref, seam_core in (
        (core, keep_ref, one_ref, 1), (1 - core, other_ref, two_ref, 0)
    ):
        seam_lane = lane == jnp.where(core == seam_core, 0, -1)
        depth = end_ref[base_z : base_z + SUB]
        stiff = end_ref[base_z + SUB : base_z + 2 * SUB]
        d_buf[tile, pl.ds(halo + SUB, SUB)] = depth
        for z in range(layers):
            at = 2 * SUB * z
            p_two[tile, z, :SUB] = zeros
            p_two[tile, z, SUB + wide :] = zeros
            p_buf[tile, z, pl.ds(halo + SUB, SUB)] = end_ref[at : at + SUB]
            w = end_ref[at + SUB : at + 2 * SUB]
            slot = jnp.broadcast_to(w[0:1], (SUB, cols))
            final = base + 3 * span + z
            final = jnp.broadcast_to(main_ref[final : final + 1], (SUB, cols))
            turned = pltpu.roll(seam, cols - z, 1) if z else seam
            w = w - jnp.where(seam_lane, turned, 0.0) - jnp.where(end_row, final, 0.0)
            w_buf[tile, z, pl.ds(halo, SUB)] = w
            w_buf[tile, z, pl.ds(middle, SUB)] = w_buf[tile, z, pl.ds(middle, SUB)] - jnp.where(
                top_row, slot, 0.0
            )
            wet = depth > float(z)
            wet_buf[tile, z, pl.ds(halo + SUB, SUB)] = jnp.where(wet, 1.0, 0.0)
            scale_buf[tile, z, pl.ds(halo, SUB)] = jnp.where(wet, stiff, 0.0)
            if z > 0:
                half_buf[tile, z - 1, pl.ds(halo, SUB)] = jnp.where(wet, 0.5, 0.0)

    zs = range(layers)
    ZB = 4
    groups = layers // ZB
    lane = lanes_of((ZB, wide, cols))
    last_lane = lane == cols - 1
    first_lane = lane == 0
    here = slice(SUB, SUB + wide)
    ahead = slice(SUB + 1, SUB + 1 + wide)
    back_rows = slice(SUB - 1, SUB - 1 + wide)

    def step(t, first, p_buf, w_buf, p_out, w_out):
        def stage_a(g):
            zs = slice(g * ZB, (g + 1) * ZB)
            return [pltpu.roll(p_buf[i, zs, here], cols - 1, 2) for i in range(2)]

        def stage_b(g, turned):
            zs = slice(g * ZB, (g + 1) * ZB)
            right = [
                jnp.where(last_lane, turned[1], turned[0]),
                jnp.where(last_lane, 0.0, turned[1]),
            ]
            gy = [wet_buf[i, zs, SUB:] * (right[i] - p_buf[i, zs, here]) for i in range(2)]
            return gy, [pltpu.roll(gy[i], 1, 2) for i in range(2)]

        hz_last = [None, None]
        surface = [None, None]

        def stage_c(g, gy, back):
            zs = slice(g * ZB, (g + 1) * ZB)
            before = [
                jnp.where(first_lane, 0.0, back[0]),
                jnp.where(first_lane, back[0], back[1]),
            ]
            for i in range(2):
                p = p_buf[i, zs, here]
                w = w_buf[i, zs] - (gy[i] - before[i])
                gx = wet_buf[i, zs, SUB:] * (p_buf[i, zs, ahead] - p)
                behind = wet_buf[i, zs, SUB - 1 : SUB - 1 + wide] * (p - p_buf[i, zs, back_rows])
                w = w - (gx - behind)
                w_out[i, zs] = w
                if g + 1 < groups:
                    hz = half_buf[i, zs] * (p_buf[i, g * ZB + 1 : (g + 1) * ZB + 1, here] - p)
                elif ZB > 1:
                    hz = jnp.concatenate([half_buf[i, g * ZB :] * (p[1:] - p[:-1]), jnp.zeros((1, wide, cols), jnp.float32)], 0)
                else:
                    hz = jnp.zeros((1, wide, cols), jnp.float32)
                prev = jnp.zeros((1, wide, cols), jnp.float32) if g == 0 else hz_last[i]
                flux = w - (hz - (jnp.concatenate([prev, hz[:-1]], 0) if ZB > 1 else prev))
                hz_last[i] = hz[-1:]
                old = wet_buf[i, zs, SUB:] * p if first else p
                new = old - scale_buf[i, zs] * flux
                p_out[i, zs, here] = new
                for k in range(ZB):
                    part = new[k, SUB:span]
                    z = g * ZB + k
                    surface[i] = part if z == 0 else jnp.where(d_buf[i, 2 * SUB : SUB + span] > float(z), part, surface[i])

        turned = [stage_a(0), stage_a(1)]
        ready = stage_b(0, turned[0])
        for g in range(groups):
            if g + 2 < groups:
                turned.append(stage_a(g + 2))
            coming = stage_b(g + 1, turned[g + 1]) if g + 1 < groups else None
            stage_c(g, *ready)
            ready = coming
        for i in range(2):
            trace[t, i] = surface[i]

    def two(k, carry):
        step(2 * k, False, p_buf, w_buf, p_two, w_two)
        step(2 * k + 1, False, p_two, w_two, p_buf, w_buf)
        return carry

    step(0, True, p_buf, w_buf, p_two, w_two)
    step(1, False, p_two, w_two, p_buf, w_buf)
    lax.fori_loop(1, STEPS // 2, two, 0)
    for z in zs:
        p_keep_ref[z] = p_buf[core, z, 2 * SUB : 2 * SUB + half_rows]
        p_send_ref[z] = p_buf[1 - core, z, 2 * SUB : 2 * SUB + half_rows]

    width = cols // 2
    lane_rows = lanes_of((half_rows, cols))
    place = place_ref[...]
    count = place.shape[0] // 2
    parts = STEPS // 2
    for j in range(parts):
        pieces = []
        for i in range(2):
            one = trace[2 * j, i]
            two = trace[2 * j + 1, i]
            pieces.append(jnp.where(lane_rows < width, one, pltpu.roll(two, width, 1)))
            pieces.append(jnp.where(lane_rows < width, pltpu.roll(one, width, 1), two))
        both = jnp.concatenate(pieces, 0)
        part_a = both.astype(jnp.bfloat16)
        rest = both - part_a.astype(jnp.float32)
        part_b = rest.astype(jnp.bfloat16)
        part_c = (rest - part_b.astype(jnp.float32)).astype(jnp.bfloat16)
        total = jnp.dot(place, part_a, preferred_element_type=jnp.float32)
        total += jnp.dot(place, part_b, preferred_element_type=jnp.float32)
        total += jnp.dot(place, part_c, preferred_element_type=jnp.float32)
        panel_keep_ref[pl.ds(j, count, stride=parts)] = total[:count]
        panel_send_ref[pl.ds(j, count, stride=parts)] = total[count:]


def shards(
    pressure_start, along_start, cross_start, depth_layers, stiffness, patch_lists, owner_map
):
    sensors, layers, rows, cols = pressure_start.shape
    f32 = jnp.float32
    along_count = lax.axis_size("along")
    cross_count = lax.axis_size("cross")
    low = lax.axis_index("cross") == 0
    swap = [(0, 1), (1, 0)]
    pair = ("along", "cross")
    steps_up = range(along_count - 1)
    route_one = [(2 * i, 2 * i + 2) for i in steps_up] + [(2 * i + 3, 2 * i + 1) for i in steps_up]
    route_two = [(2 * i + 1, 2 * i + 2) for i in steps_up]
    route_two += [(2 * i + 2, 2 * i + 1) for i in steps_up]
    half_rows = rows // 2
    span = half_rows + SUB
    wide = span + SUB
    pack_rows = 2 * span * layers + 3 * span + layers
    end_rows = 2 * SUB * layers + 3 * SUB

    spec = pl.BlockSpec(memory_space=VMEM)
    hbm = pl.BlockSpec(memory_space=pltpu.HBM)
    params = pltpu.CompilerParams(vmem_limit_bytes=32 * 1024 * 1024)
    keep, send, one, two = pl.pallas_call(
        edges_kernel,
        out_shape=[
            jax.ShapeDtypeStruct((pack_rows, cols), f32),
            jax.ShapeDtypeStruct((pack_rows + SUB, cols), f32),
            jax.ShapeDtypeStruct((end_rows, cols), f32),
            jax.ShapeDtypeStruct((end_rows, cols), f32),
        ],
        in_specs=[hbm] * 6,
        out_specs=[spec] * 4,
        scratch_shapes=[
            VMEM((layers, rows, cols), f32),
            VMEM((layers, rows, cols), f32),
            VMEM((layers, rows, cols), f32),
            VMEM((rows, cols), jnp.int32),
            VMEM((rows, cols), f32),
            VMEM(owner_map.shape, jnp.int32),
            pltpu.SemaphoreType.DMA((6,)),
        ],
        compiler_params=params,
        name="edges",
    )(
        *(
            pltpu.with_memory_space_constraint(x, pltpu.HBM)
            for x in (
                pressure_start[0],
                along_start[0],
                cross_start[0],
                depth_layers,
                stiffness,
                owner_map,
            )
        )
    )

    other = lax.ppermute(send, "cross", swap)
    one = lax.ppermute(one, pair, route_one)
    state_shapes = [
        jax.ShapeDtypeStruct(shape, f32)
        for shape in (
            (2, layers, wide + 2 * SUB, cols),
            (2, layers, wide, cols),
            (2, wide + SUB, cols),
            (2, layers, wide + SUB, cols),
            (2, layers, wide, cols),
            (2, layers - 1, wide, cols),
        )
    ]
    two, *state = pl.pallas_call(
        prepare_kernel,
        out_shape=[jax.ShapeDtypeStruct((end_rows, cols), f32)] + state_shapes,
        in_specs=[spec] * 3,
        out_specs=[spec] * 7,
        compiler_params=params,
        name="prepare",
    )(keep, other, two)
    two = lax.ppermute(two, pair, route_two)

    patch_count = 2 * rows
    owner_count = along_count * cross_count
    capacity = patch_count // owner_count + 1
    count = owner_count * capacity
    place = pl.pallas_call(
        functools.partial(
            place_kernel, owner_count=owner_count, chips=along_count, capacity=capacity
        ),
        out_shape=jax.ShapeDtypeStruct((2 * count, patch_count), jnp.bfloat16),
        in_specs=[spec] * 3,
        out_specs=spec,
        compiler_params=params,
        name="place",
    )(patch_lists.reshape(-1, patch_count).T, owner_map, other)

    parts = STEPS // 2
    p_keep, p_send, panel_keep, panel_send, *state = pl.pallas_call(
        steps_kernel,
        out_shape=[
            jax.ShapeDtypeStruct((layers, half_rows, cols), f32),
            jax.ShapeDtypeStruct((layers, half_rows, cols), f32),
            jax.ShapeDtypeStruct((count * parts, cols), f32),
            jax.ShapeDtypeStruct((count * parts, cols), f32),
        ]
        + state_shapes,
        in_specs=[spec] * 11,
        out_specs=[spec] * 10,
        scratch_shapes=[
            VMEM((STEPS, 2, half_rows, cols), f32),
            VMEM((2, layers, wide + 2 * SUB, cols), f32),
            VMEM((2, layers, wide, cols), f32),
        ],
        input_output_aliases={5 + i: 4 + i for i in range(6)},
        compiler_params=params,
        name="steps",
    )(keep, other, one, two, place, *state)

    panels = panel_keep + lax.ppermute(panel_send, "cross", swap)
    if along_count == 4:
        some = 2 * capacity * parts
        ring = range(along_count)
        near_route = [(2 * i, 2 * ((i + 1) % along_count)) for i in ring]
        near_route += [(2 * ((i + 1) % along_count) + 1, 2 * i + 1) for i in ring]
        near = lax.ppermute(panels[: 2 * some], pair, near_route)
        far = lax.ppermute(
            panels[2 * some : 3 * some], "along", [(i, (i + 2) % along_count) for i in ring]
        )
        swapped = lax.ppermute(near[some:], "cross", swap)
        received = pl.pallas_call(
            gather_kernel,
            out_shape=jax.ShapeDtypeStruct((count * parts, cols), f32),
            in_specs=[spec] * 4,
            out_specs=hbm,
            scratch_shapes=[pltpu.SemaphoreType.DMA((4,))],
            compiler_params=params,
            name="gather",
        )(panels[3 * some :], near[:some], far, swapped)
    else:
        panels = panels.reshape(along_count, 2 * capacity * parts, cols)
        received = lax.all_to_all(panels, "along", split_axis=0, concat_axis=0, tiled=True)
    received = received.reshape(1, count, 1, parts * cols)

    p_other = lax.ppermute(p_send, "cross", swap)
    pressure = jnp.where(
        low, jnp.concatenate([p_keep, p_other], 1), jnp.concatenate([p_other, p_keep], 1)
    )
    return (pressure[None], received)


def solution(mesh):
    in_specs = (
        P("batch", None, "along", "cross"),
        P("batch", None, "along", "cross"),
        P("batch", None, "along", "cross"),
        P("along", "cross"),
        P("along", "cross"),
        P("batch", None),
        P(("along", "cross"), None),
    )
    out_specs = (P("batch", None, "along", "cross"), P(("along", "cross"), None, "batch", None))
    return jax.shard_map(shards, mesh=mesh, in_specs=in_specs, out_specs=out_specs, check_vma=False)
```

```python
import functools

import jax
import jax.numpy as jnp
from jax import lax
from jax.experimental import pallas as pl
from jax.experimental.pallas import tpu as pltpu
from jax.sharding import PartitionSpec as P

STEPS = 8
SUB = 8
VMEM = pltpu.VMEM


def lanes_of(shape):
    return lax.broadcasted_iota(jnp.int32, shape, len(shape) - 1)


def rows_of(shape):
    return lax.broadcasted_iota(jnp.int32, shape, len(shape) - 2)


def edges_kernel(
    p_hbm, fa_hbm, fc_hbm, depth_hbm, stiff_hbm, owner_hbm,
    keep_ref, send_ref, one_ref, two_ref,
    p_ref, fa_ref, fc_ref, depth_ref, stiff_ref, owner_ref, sems,
):
    copies = [
        pltpu.make_async_copy(source, target, sems.at[i])
        for i, (source, target) in enumerate(
            (
                (depth_hbm, depth_ref),
                (stiff_hbm, stiff_ref),
                (owner_hbm, owner_ref),
                (fa_hbm, fa_ref),
                (fc_hbm, fc_ref),
                (p_hbm, p_ref),
            )
        )
    ]
    for copy in copies:
        copy.start()
    for copy in copies:
        copy.wait()
    layers, rows, cols = p_ref.shape
    low = lax.axis_index("cross") == 0
    span = rows // 2 + SUB
    last = rows - SUB
    lane = lanes_of((rows, cols))
    row = rows_of((rows, cols))
    row_sub = rows_of((SUB, cols))
    depth = depth_ref[...]
    stiff = stiff_ref[...]
    first_lane = lane == 0
    slot_one = row_sub == jnp.where(low, 0, -1)
    slot_two = row_sub == jnp.where(low, -1, 0)
    base = 2 * span * layers
    base_z = 2 * SUB * layers
    velocity = jnp.zeros((rows, cols), jnp.float32)

    def halves(array):
        first, second = array[:span], array[rows - span :]
        return jnp.where(low, first, second), jnp.where(low, second, first)

    def ends(array):
        first, second = array[:SUB], array[last:]
        return jnp.where(low, second, first), jnp.where(low, first, second)

    for z in range(layers):
        wet = depth > z
        p = p_ref[z]
        va = jnp.where(wet, fa_ref[z], 0.0)
        vc = jnp.where(wet, fc_ref[z], 0.0)
        behind = jnp.where(row == 0, 0.0, pltpu.roll(va, 1, 0))
        before = jnp.where(first_lane, 0.0, pltpu.roll(vc, 1, 1))
        w = (va - behind) + (vc - before)
        velocity = jnp.where(lane == z, pltpu.roll(vc, z + 1, 1), velocity)
        at = 2 * span * z
        keep_ref[at : at + span], send_ref[at : at + span] = halves(p)
        at += span
        keep_ref[at : at + span], send_ref[at : at + span] = halves(w)
        final = va[rows - 1 : rows]
        at = base + 3 * span + z
        keep_ref[at : at + 1] = final
        send_ref[at : at + 1] = final
        at = 2 * SUB * z
        one_ref[at : at + SUB], two_ref[at : at + SUB] = ends(p)
        at += SUB
        one, two = ends(w)
        final = jnp.broadcast_to(final, (SUB, cols))
        one_ref[at : at + SUB] = jnp.where(slot_one, final, one)
        two_ref[at : at + SUB] = jnp.where(slot_two, final, two)
    for i, array in enumerate((depth.astype(jnp.float32), stiff, velocity)):
        at = base + span * i
        keep_ref[at : at + span], send_ref[at : at + span] = halves(array)
        at = base_z + SUB * i
        one_ref[at : at + SUB], two_ref[at : at + SUB] = ends(array)
    at = base + 3 * span + layers
    owners = owner_ref[...].astype(jnp.float32)
    send_ref[at : at + SUB] = jnp.broadcast_to(owners, (SUB, cols))


def place_kernel(ids_ref, own_ref, other_ref, place_ref, *, owner_count, chips, capacity):
    along = lax.axis_index("along")
    cross = lax.axis_index("cross")
    low = cross == 0
    cores = owner_count // chips
    patches = own_ref.shape[1]
    last = other_ref.shape[0] - SUB
    own = own_ref[...].astype(jnp.float32)
    other = other_ref[last : last + 1]
    owners = [jnp.where(low, own, other), jnp.where(low, other, own)]
    lane = lanes_of((patches, patches))
    half = patches // 2
    block = lane // half
    within = lane % half
    patch = half * cross + 2 * (within % (half // 2)) + within // (half // 2)
    source = rows_of((patches, patches))
    number = rows_of((owner_count, patches)).astype(jnp.float32)
    chosen = jnp.zeros((owner_count, patches), jnp.float32)
    counts = jnp.zeros((owner_count, patches), jnp.float32)
    for i in range(2):
        held = (number == owners[i]).astype(jnp.bfloat16)
        pick = jnp.where(block == i, jnp.where(source == patch, 1.0, 0.0), 0.0).astype(jnp.bfloat16)
        earlier = jnp.where(block == i, jnp.where(source < patch, 1.0, 0.0), 0.0).astype(jnp.bfloat16)
        chosen += jnp.dot(held, pick, preferred_element_type=jnp.float32)
        counts += jnp.dot(held, earlier, preferred_element_type=jnp.float32)
    rank = jnp.sum(chosen * counts, axis=0, keepdims=True).astype(jnp.int32)
    owner = jnp.sum(chosen * number, axis=0, keepdims=True).astype(jnp.int32)
    wanted = (along * cores + block) * patches + patch
    found = jnp.zeros((patches, patches), jnp.float32)
    for j in range(ids_ref.shape[1]):
        found = jnp.where(ids_ref[:, j : j + 1] == wanted, 1.0, found)
    member = jnp.sum(found, axis=0, keepdims=True)
    block = block[:1]
    chip = owner // cores
    owner_core = owner % cores
    some = 2 * capacity
    slot = block * capacity + rank
    if chips == 4:
        ahead = lax.rem(chip - along + chips, chips)
        near = lax.rem(ahead, 2) == 1
        handler = jnp.where(near, ahead // 2, owner_core)
        slot = slot + jnp.where(
            near, jnp.where(owner_core == handler, 0, some), jnp.where(ahead == 2, 2 * some, 3 * some)
        )
    else:
        handler = owner_core
        slot = slot + chip * some
    slot = jnp.where(handler == cross, slot, slot + chips * some)
    slot = jnp.where(member > 0.0, slot, -1)
    place_ref[...] = jnp.where(rows_of(place_ref.shape) == slot, 1.0, 0.0).astype(jnp.bfloat16)


def gather_kernel(own_ref, near_ref, far_ref, swapped_ref, out_ref, sems):
    chips = 4
    along = lax.axis_index("along")
    cross = lax.axis_index("cross")
    count = out_ref.shape[0] // chips
    copies = []
    for i, (ref, ahead) in enumerate(
        ((own_ref, 0), (near_ref, 3 - 2 * cross), (far_ref, 2), (swapped_ref, 1 + 2 * cross))
    ):
        at = pl.multiple_of(lax.rem(along + ahead, chips) * count, SUB)
        copies.append(pltpu.make_async_copy(ref, out_ref.at[pl.ds(at, count)], sems.at[i]))
    for copy in copies:
        copy.start()
    for copy in copies:
        copy.wait()


def steps_kernel(
    keep_ref,
    other_ref,
    one_ref,
    two_ref,
    place_ref,
    p_keep_ref,
    p_send_ref,
    panel_keep_ref,
    panel_send_ref,
    p_buf,
    w_buf,
    d_buf,
    s_buf,
    trace,
    wet_buf,
    scale_buf,
    half_buf,
    p_two,
    w_two,
):
    layers, half_rows, cols = p_keep_ref.shape
    core = lax.axis_index("cross")
    low = core == 0
    span = half_rows + SUB
    wide = span + SUB
    blocks = wide // SUB
    base = 2 * span * layers
    base_z = 2 * SUB * layers
    lane = lanes_of((SUB, cols))
    row = rows_of((SUB, cols))
    middle = pl.multiple_of(SUB * (1 - core), SUB)
    halo = pl.multiple_of(span * core, SUB)

    def left(own, other):
        return jnp.where(low, own, other)

    seam_span = left(keep_ref[base + 2 * span : base + 3 * span], other_ref[base + 2 * span : base + 3 * span])
    seam_halo = left(one_ref[base_z + 2 * SUB : base_z + 3 * SUB], two_ref[base_z + 2 * SUB : base_z + 3 * SUB])
    top_row = row == jnp.where(low, 0, -1)
    end_row = row == jnp.where(low, -1, 0)
    zeros = jnp.zeros((SUB, cols), jnp.float32)
    for tile, main_ref, end_ref, seam_core in ((core, keep_ref, one_ref, 1), (1 - core, other_ref, two_ref, 0)):
        seam_lane = jnp.where(core == seam_core, 0, -1)
        seam = lanes_of((span, cols)) == seam_lane
        seam_sub = lane == seam_lane
        for z in range(layers):
            at = 2 * span * z
            at_z = 2 * SUB * z
            p_buf[tile, z, :SUB] = zeros
            p_two[tile, z, :SUB] = zeros
            p_two[tile, z, SUB + wide :] = zeros
            p_buf[tile, z, pl.ds(middle + SUB, span)] = main_ref[at : at + span]
            p_buf[tile, z, pl.ds(halo + SUB, SUB)] = end_ref[at_z : at_z + SUB]
            p_buf[tile, z, SUB + wide :] = zeros
            turn = (cols - z) % cols
            w = main_ref[at + span : at + 2 * span]
            w = w - jnp.where(seam, pltpu.roll(seam_span, turn, 1) if turn else seam_span, 0.0)
            w_halo = end_ref[at_z + SUB : at_z + 2 * SUB]
            slot = jnp.broadcast_to(w_halo[0:1], (SUB, cols))
            final = jnp.broadcast_to(main_ref[base + 3 * span + z : base + 3 * span + z + 1], (SUB, cols))
            w_halo = w_halo - jnp.where(seam_sub, pltpu.roll(seam_halo, turn, 1) if turn else seam_halo, 0.0)
            w_halo = w_halo - jnp.where(end_row, final, 0.0)
            w_top = w[:SUB] - jnp.where(top_row, slot, 0.0)
            w_buf[tile, z, pl.ds(middle, SUB)] = w_top
            w_buf[tile, z, pl.ds(middle + SUB, span - SUB)] = w[SUB:]
            w_buf[tile, z, pl.ds(halo, SUB)] = w_halo
        d_buf[tile, :SUB] = zeros
        for buf, i, shift in ((d_buf, 0, SUB), (s_buf, 1, 0)):
            buf[tile, pl.ds(middle + shift, span)] = main_ref[base + i * span : base + (i + 1) * span]
            buf[tile, pl.ds(halo + shift, SUB)] = end_ref[base_z + i * SUB : base_z + (i + 1) * SUB]

    zs = range(layers)
    for i in range(2):
        for z in zs:
            wet = d_buf[i, SUB:] > float(z)
            if True:
                wet_buf[i, z, :SUB] = zeros
                wet_buf[i, z, SUB:] = jnp.where(wet, 1.0, 0.0)
            if True:
                scale_buf[i, z] = jnp.where(wet, s_buf[i], 0.0)
            if True and z > 0:
                half_buf[i, z - 1] = jnp.where(wet, 0.5, 0.0)
    ZB = 4
    groups = layers // ZB
    lane = lanes_of((ZB, wide, cols))
    last_lane = lane == cols - 1
    first_lane = lane == 0
    here = slice(SUB, SUB + wide)
    ahead = slice(SUB + 1, SUB + 1 + wide)
    back_rows = slice(SUB - 1, SUB - 1 + wide)

    def step(t, first, p_buf, w_buf, p_out, w_out):
        def stage_a(g):
            zs = slice(g * ZB, (g + 1) * ZB)
            return [pltpu.roll(p_buf[i, zs, here], cols - 1, 2) for i in range(2)]

        def stage_b(g, turned):
            zs = slice(g * ZB, (g + 1) * ZB)
            right = [
                jnp.where(last_lane, turned[1], turned[0]),
                jnp.where(last_lane, 0.0, turned[1]),
            ]
            gy = [wet_buf[i, zs, SUB:] * (right[i] - p_buf[i, zs, here]) for i in range(2)]
            return gy, [pltpu.roll(gy[i], 1, 2) for i in range(2)]

        hz_last = [None, None]
        surface = [None, None]

        def stage_c(g, gy, back):
            zs = slice(g * ZB, (g + 1) * ZB)
            before = [
                jnp.where(first_lane, 0.0, back[0]),
                jnp.where(first_lane, back[0], back[1]),
            ]
            for i in range(2):
                p = p_buf[i, zs, here]
                w = w_buf[i, zs] - (gy[i] - before[i])
                gx = wet_buf[i, zs, SUB:] * (p_buf[i, zs, ahead] - p)
                behind = wet_buf[i, zs, SUB - 1 : SUB - 1 + wide] * (p - p_buf[i, zs, back_rows])
                w = w - (gx - behind)
                w_out[i, zs] = w
                if g + 1 < groups:
                    hz = half_buf[i, zs] * (p_buf[i, g * ZB + 1 : (g + 1) * ZB + 1, here] - p)
                elif ZB > 1:
                    hz = jnp.concatenate([half_buf[i, g * ZB :] * (p[1:] - p[:-1]), jnp.zeros((1, wide, cols), jnp.float32)], 0)
                else:
                    hz = jnp.zeros((1, wide, cols), jnp.float32)
                prev = jnp.zeros((1, wide, cols), jnp.float32) if g == 0 else hz_last[i]
                flux = w - (hz - (jnp.concatenate([prev, hz[:-1]], 0) if ZB > 1 else prev))
                hz_last[i] = hz[-1:]
                old = wet_buf[i, zs, SUB:] * p if first else p
                new = old - scale_buf[i, zs] * flux
                p_out[i, zs, here] = new
                for k in range(ZB):
                    part = new[k, SUB:span]
                    z = g * ZB + k
                    surface[i] = part if z == 0 else jnp.where(d_buf[i, 2 * SUB : SUB + span] > float(z), part, surface[i])

        turned = [stage_a(0), stage_a(1)]
        ready = stage_b(0, turned[0])
        for g in range(groups):
            if g + 2 < groups:
                turned.append(stage_a(g + 2))
            coming = stage_b(g + 1, turned[g + 1]) if g + 1 < groups else None
            stage_c(g, *ready)
            ready = coming
        for i in range(2):
            trace[t, i] = surface[i]

    def two(k, carry):
        step(2 * k, False, p_buf, w_buf, p_two, w_two)
        step(2 * k + 1, False, p_two, w_two, p_buf, w_buf)
        return carry

    step(0, True, p_buf, w_buf, p_two, w_two)
    step(1, False, p_two, w_two, p_buf, w_buf)
    lax.fori_loop(1, STEPS // 2, two, 0)
    for z in zs:
        p_keep_ref[z] = p_buf[core, z, 2 * SUB : 2 * SUB + half_rows]
        p_send_ref[z] = p_buf[1 - core, z, 2 * SUB : 2 * SUB + half_rows]

    width = cols // 2
    lane_rows = lanes_of((half_rows, cols))
    place = place_ref[...]
    count = place.shape[0] // 2
    parts = STEPS // 2
    for j in range(parts):
        pieces = []
        for i in range(2):
            one = trace[2 * j, i]
            two = trace[2 * j + 1, i]
            pieces.append(jnp.where(lane_rows < width, one, pltpu.roll(two, width, 1)))
            pieces.append(jnp.where(lane_rows < width, pltpu.roll(one, width, 1), two))
        both = jnp.concatenate(pieces, 0)
        part_a = both.astype(jnp.bfloat16)
        rest = both - part_a.astype(jnp.float32)
        part_b = rest.astype(jnp.bfloat16)
        part_c = (rest - part_b.astype(jnp.float32)).astype(jnp.bfloat16)
        total = jnp.dot(place, part_a, preferred_element_type=jnp.float32)
        total += jnp.dot(place, part_b, preferred_element_type=jnp.float32)
        total += jnp.dot(place, part_c, preferred_element_type=jnp.float32)
        panel_keep_ref[pl.ds(j, count, stride=parts)] = total[:count]
        panel_send_ref[pl.ds(j, count, stride=parts)] = total[count:]


def shards(
    pressure_start, along_start, cross_start, depth_layers, stiffness, patch_lists, owner_map
):
    sensors, layers, rows, cols = pressure_start.shape
    f32 = jnp.float32
    along_count = lax.axis_size("along")
    cross_count = lax.axis_size("cross")
    low = lax.axis_index("cross") == 0
    swap = [(0, 1), (1, 0)]
    pair = ("along", "cross")
    steps_up = range(along_count - 1)
    route_one = [(2 * i, 2 * i + 2) for i in steps_up] + [(2 * i + 3, 2 * i + 1) for i in steps_up]
    route_two = [(2 * i + 1, 2 * i + 2) for i in steps_up]
    route_two += [(2 * i + 2, 2 * i + 1) for i in steps_up]
    half_rows = rows // 2
    span = half_rows + SUB
    wide = span + SUB
    pack_rows = 2 * span * layers + 3 * span + layers
    end_rows = 2 * SUB * layers + 3 * SUB

    spec = pl.BlockSpec(memory_space=VMEM)
    hbm = pl.BlockSpec(memory_space=pltpu.HBM)
    params = pltpu.CompilerParams(vmem_limit_bytes=32 * 1024 * 1024)
    keep, send, one, two = pl.pallas_call(
        edges_kernel,
        out_shape=[
            jax.ShapeDtypeStruct((pack_rows, cols), f32),
            jax.ShapeDtypeStruct((pack_rows + SUB, cols), f32),
            jax.ShapeDtypeStruct((end_rows, cols), f32),
            jax.ShapeDtypeStruct((end_rows, cols), f32),
        ],
        in_specs=[hbm] * 6,
        out_specs=[spec] * 4,
        scratch_shapes=[
            VMEM((layers, rows, cols), f32),
            VMEM((layers, rows, cols), f32),
            VMEM((layers, rows, cols), f32),
            VMEM((rows, cols), jnp.int32),
            VMEM((rows, cols), f32),
            VMEM(owner_map.shape, jnp.int32),
            pltpu.SemaphoreType.DMA((6,)),
        ],
        compiler_params=params,
        name="edges",
    )(
        *(
            pltpu.with_memory_space_constraint(x, pltpu.HBM)
            for x in (
                pressure_start[0],
                along_start[0],
                cross_start[0],
                depth_layers,
                stiffness,
                owner_map,
            )
        )
    )

    other = lax.ppermute(send, "cross", swap)
    one = lax.ppermute(one, pair, route_one)
    two = lax.ppermute(two, pair, route_two)

    patch_count = 2 * rows
    owner_count = along_count * cross_count
    capacity = patch_count // owner_count + 1
    count = owner_count * capacity
    place = pl.pallas_call(
        functools.partial(
            place_kernel, owner_count=owner_count, chips=along_count, capacity=capacity
        ),
        out_shape=jax.ShapeDtypeStruct((2 * count, patch_count), jnp.bfloat16),
        in_specs=[spec] * 3,
        out_specs=spec,
        compiler_params=params,
        name="place",
    )(patch_lists.reshape(-1, patch_count).T, owner_map, other)

    parts = STEPS // 2
    p_keep, p_send, panel_keep, panel_send = pl.pallas_call(
        steps_kernel,
        out_shape=[
            jax.ShapeDtypeStruct((layers, half_rows, cols), f32),
            jax.ShapeDtypeStruct((layers, half_rows, cols), f32),
            jax.ShapeDtypeStruct((count * parts, cols), f32),
            jax.ShapeDtypeStruct((count * parts, cols), f32),
        ],
        in_specs=[spec] * 5,
        out_specs=[spec] * 4,
        scratch_shapes=[
            VMEM((2, layers, wide + 2 * SUB, cols), f32),
            VMEM((2, layers, wide, cols), f32),
            VMEM((2, wide + SUB, cols), f32),
            VMEM((2, wide, cols), f32),
            VMEM((STEPS, 2, half_rows, cols), f32),
            VMEM((2, layers, wide + SUB, cols), f32),
            VMEM((2, layers, wide, cols), f32),
            VMEM((2, layers - 1, wide, cols), f32),
            VMEM((2, layers, wide + 2 * SUB, cols), f32),
            VMEM((2, layers, wide, cols), f32),
        ],
        compiler_params=params,
        name="steps",
    )(keep, other, one, two, place)

    panels = panel_keep + lax.ppermute(panel_send, "cross", swap)
    if along_count == 4:
        some = 2 * capacity * parts
        ring = range(along_count)
        near_route = [(2 * i, 2 * ((i + 1) % along_count)) for i in ring]
        near_route += [(2 * ((i + 1) % along_count) + 1, 2 * i + 1) for i in ring]
        near = lax.ppermute(panels[: 2 * some], pair, near_route)
        far = lax.ppermute(
            panels[2 * some : 3 * some], "along", [(i, (i + 2) % along_count) for i in ring]
        )
        swapped = lax.ppermute(near[some:], "cross", swap)
        received = pl.pallas_call(
            gather_kernel,
            out_shape=jax.ShapeDtypeStruct((count * parts, cols), f32),
            in_specs=[spec] * 4,
            out_specs=hbm,
            scratch_shapes=[pltpu.SemaphoreType.DMA((4,))],
            compiler_params=params,
            name="gather",
        )(panels[3 * some :], near[:some], far, swapped)
    else:
        panels = panels.reshape(along_count, 2 * capacity * parts, cols)
        received = lax.all_to_all(panels, "along", split_axis=0, concat_axis=0, tiled=True)
    received = received.reshape(1, count, 1, parts * cols)

    p_other = lax.ppermute(p_send, "cross", swap)
    pressure = jnp.where(
        low, jnp.concatenate([p_keep, p_other], 1), jnp.concatenate([p_other, p_keep], 1)
    )
    return (pressure[None], received)


def solution(mesh):
    in_specs = (
        P("batch", None, "along", "cross"),
        P("batch", None, "along", "cross"),
        P("batch", None, "along", "cross"),
        P("along", "cross"),
        P("along", "cross"),
        P("batch", None),
        P(("along", "cross"), None),
    )
    out_specs = (P("batch", None, "along", "cross"), P(("along", "cross"), None, "batch", None))
    return jax.shard_map(shards, mesh=mesh, in_specs=in_specs, out_specs=out_specs, check_vma=False)
```

```python
import functools

import jax
import jax.numpy as jnp
from jax import lax
from jax.experimental import pallas as pl
from jax.experimental.pallas import tpu as pltpu
from jax.sharding import PartitionSpec as P

STEPS = 8
SUB = 8
VMEM = pltpu.VMEM


def lanes_of(shape):
    return lax.broadcasted_iota(jnp.int32, shape, len(shape) - 1)


def rows_of(shape):
    return lax.broadcasted_iota(jnp.int32, shape, len(shape) - 2)


def edges_kernel(
    p_hbm, fa_hbm, fc_hbm, depth_hbm, stiff_hbm, owner_hbm, ids_hbm,
    keep_ref, send_ref, one_ref, two_ref, ids_ref, owners_ref,
    p_ref, fa_ref, fc_ref, depth_ref, stiff_ref, owner_ref, sems,
):
    copies = [
        pltpu.make_async_copy(source, target, sems.at[i])
        for i, (source, target) in enumerate(
            (
                (depth_hbm, depth_ref),
                (stiff_hbm, stiff_ref),
                (owner_hbm, owner_ref),
                (ids_hbm, ids_ref),
                (fa_hbm, fa_ref),
                (fc_hbm, fc_ref),
                (p_hbm, p_ref),
            )
        )
    ]
    for copy in copies:
        copy.start()
    for copy in copies:
        copy.wait()
    layers, rows, cols = p_ref.shape
    low = lax.axis_index("cross") == 0
    span = rows // 2 + SUB
    last = rows - SUB
    lane = lanes_of((rows, cols))
    row = rows_of((rows, cols))
    row_sub = rows_of((SUB, cols))
    depth = depth_ref[...]
    stiff = stiff_ref[...]
    first_lane = lane == 0
    slot_one = row_sub == jnp.where(low, 0, -1)
    slot_two = row_sub == jnp.where(low, -1, 0)
    base = 2 * span * layers
    base_z = 2 * SUB * layers
    velocity = jnp.zeros((rows, cols), jnp.float32)

    def halves(array):
        first, second = array[:span], array[rows - span :]
        return jnp.where(low, first, second), jnp.where(low, second, first)

    def ends(array):
        first, second = array[:SUB], array[last:]
        return jnp.where(low, second, first), jnp.where(low, first, second)

    for z in range(layers):
        wet = depth > z
        p = p_ref[z]
        va = jnp.where(wet, fa_ref[z], 0.0)
        vc = jnp.where(wet, fc_ref[z], 0.0)
        behind = jnp.where(row == 0, 0.0, pltpu.roll(va, 1, 0))
        before = jnp.where(first_lane, 0.0, pltpu.roll(vc, 1, 1))
        w = (va - behind) + (vc - before)
        velocity = jnp.where(lane == z, pltpu.roll(vc, z + 1, 1), velocity)
        at = 2 * span * z
        keep_ref[at : at + span], send_ref[at : at + span] = halves(p)
        at += span
        keep_ref[at : at + span], send_ref[at : at + span] = halves(w)
        final = va[rows - 1 : rows]
        at = base + 3 * span + z
        keep_ref[at : at + 1] = final
        send_ref[at : at + 1] = final
        at = 2 * SUB * z
        one_ref[at : at + SUB], two_ref[at : at + SUB] = ends(p)
        at += SUB
        one, two = ends(w)
        final = jnp.broadcast_to(final, (SUB, cols))
        one_ref[at : at + SUB] = jnp.where(slot_one, final, one)
        two_ref[at : at + SUB] = jnp.where(slot_two, final, two)
    for i, array in enumerate((depth.astype(jnp.float32), stiff, velocity)):
        at = base + span * i
        keep_ref[at : at + span], send_ref[at : at + span] = halves(array)
        at = base_z + SUB * i
        one_ref[at : at + SUB], two_ref[at : at + SUB] = ends(array)
    at = base + 3 * span + layers
    owners = jnp.broadcast_to(owner_ref[...].astype(jnp.float32), (SUB, cols))
    owners_ref[...] = owners
    send_ref[at : at + SUB] = owners


def place_kernel(ids_ref, own_ref, other_ref, place_ref, *, owner_count, chips, capacity):
    along = lax.axis_index("along")
    cross = lax.axis_index("cross")
    low = cross == 0
    cores = owner_count // chips
    patches = own_ref.shape[1]
    last = other_ref.shape[0] - SUB
    own = own_ref[0:1]
    other = other_ref[last : last + 1]
    owners = [jnp.where(low, own, other), jnp.where(low, other, own)]
    lane = lanes_of((patches, patches))
    half = patches // 2
    block = lane // half
    within = lane % half
    held = half // 2
    turn = (held - SUB) * cross
    patch = half * cross + 2 * lax.rem(within % held + turn, held) + within // held
    source = rows_of((patches, patches))
    number = rows_of((owner_count, patches)).astype(jnp.float32)
    chosen = jnp.zeros((owner_count, patches), jnp.float32)
    counts = jnp.zeros((owner_count, patches), jnp.float32)
    for i in range(2):
        owned = (number == owners[i]).astype(jnp.bfloat16)
        pick = jnp.where(block == i, jnp.where(source == patch, 1.0, 0.0), 0.0).astype(jnp.bfloat16)
        earlier = jnp.where(block == i, jnp.where(source < patch, 1.0, 0.0), 0.0).astype(jnp.bfloat16)
        chosen += jnp.dot(owned, pick, preferred_element_type=jnp.float32)
        counts += jnp.dot(owned, earlier, preferred_element_type=jnp.float32)
    rank = jnp.sum(chosen * counts, axis=0, keepdims=True).astype(jnp.int32)
    owner = jnp.sum(chosen * number, axis=0, keepdims=True).astype(jnp.int32)
    wanted = (along * cores + block) * patches + patch
    found = jnp.zeros((patches, patches), jnp.float32)
    for j in range(ids_ref.shape[1]):
        found = jnp.where(ids_ref[:, j : j + 1] == wanted, 1.0, found)
    member = jnp.sum(found, axis=0, keepdims=True)
    block = block[:1]
    chip = owner // cores
    owner_core = owner % cores
    some = 2 * capacity
    slot = block * capacity + rank
    if chips == 4:
        ahead = lax.rem(chip - along + chips, chips)
        slot = slot + ahead * some
    else:
        slot = slot + chip * some
    handler = owner_core
    slot = jnp.where(handler == cross, slot, slot + chips * some)
    slot = jnp.where(member > 0.0, slot, -1)
    place_ref[...] = jnp.where(rows_of(place_ref.shape) == slot, 1.0, 0.0).astype(jnp.bfloat16)


def gather_kernel(own_ref, one_ref, two_ref, three_ref, out_ref, sems):
    chips = 4
    along = lax.axis_index("along")
    count = out_ref.shape[0] // chips
    copies = []
    for i, (ref, ahead) in enumerate(
        ((own_ref, 0), (one_ref, 3), (two_ref, 2), (three_ref, 1))
    ):
        at = pl.multiple_of(lax.rem(along + ahead, chips) * count, SUB)
        copies.append(pltpu.make_async_copy(ref, out_ref.at[pl.ds(at, count)], sems.at[i]))
    for copy in copies:
        copy.start()
    for copy in copies:
        copy.wait()


ZB = 4


def masks(depth, stiff, d_buf, wet_buf, scale_buf, half_buf, tile):
    layers = wet_buf.shape[1]
    zeros = jnp.zeros((SUB, depth.shape[1]), jnp.float32)
    d_buf[tile] = depth
    for z in range(layers):
        wet = depth > float(z)
        wet_buf[tile, z, :SUB] = zeros
        wet_buf[tile, z, SUB:] = jnp.where(wet, 1.0, 0.0)
        scale_buf[tile, z] = jnp.where(wet, stiff, 0.0)
        if z > 0:
            half_buf[tile, z - 1] = jnp.where(wet, 0.5, 0.0)


def advance(p_buf, w_buf, d_buf, wet_buf, scale_buf, half_buf, p_two, w_two, trace, kept):
    layers = p_buf.shape[1]
    wide, cols = w_buf.shape[2:]
    groups = layers // ZB
    lane = lanes_of((ZB, wide, cols))
    last_lane = lane == cols - 1
    first_lane = lane == 0
    zeros = jnp.zeros((SUB, cols), jnp.float32)
    for tile in range(2):
        for z in range(layers):
            for buf in (p_buf, p_two):
                buf[tile, z, :SUB] = zeros
                buf[tile, z, SUB + wide :] = zeros
    here = slice(SUB, SUB + wide)
    ahead = slice(SUB + 1, SUB + 1 + wide)
    back_rows = slice(SUB - 1, SUB - 1 + wide)

    def step(t, first, p_buf, w_buf, p_out, w_out):
        def stage_a(g):
            zs = slice(g * ZB, (g + 1) * ZB)
            return [pltpu.roll(p_buf[i, zs, here], cols - 1, 2) for i in range(2)]

        def stage_b(g, turned):
            zs = slice(g * ZB, (g + 1) * ZB)
            right = [
                jnp.where(last_lane, turned[1], turned[0]),
                jnp.where(last_lane, 0.0, turned[1]),
            ]
            gy = [wet_buf[i, zs, SUB:] * (right[i] - p_buf[i, zs, here]) for i in range(2)]
            return gy, [pltpu.roll(gy[i], 1, 2) for i in range(2)]

        hz_last = [None, None]
        surface = [None, None]

        def stage_c(g, gy, back):
            zs = slice(g * ZB, (g + 1) * ZB)
            before = [
                jnp.where(first_lane, 0.0, back[0]),
                jnp.where(first_lane, back[0], back[1]),
            ]
            for i in range(2):
                p = p_buf[i, zs, here]
                w = w_buf[i, zs] - (gy[i] - before[i])
                gx = wet_buf[i, zs, SUB:] * (p_buf[i, zs, ahead] - p)
                behind = wet_buf[i, zs, SUB - 1 : SUB - 1 + wide] * (p - p_buf[i, zs, back_rows])
                w = w - (gx - behind)
                w_out[i, zs] = w
                if g + 1 < groups:
                    hz = half_buf[i, zs] * (p_buf[i, g * ZB + 1 : (g + 1) * ZB + 1, here] - p)
                elif ZB > 1:
                    hz = jnp.concatenate([half_buf[i, g * ZB :] * (p[1:] - p[:-1]), jnp.zeros((1, wide, cols), jnp.float32)], 0)
                else:
                    hz = jnp.zeros((1, wide, cols), jnp.float32)
                prev = jnp.zeros((1, wide, cols), jnp.float32) if g == 0 else hz_last[i]
                flux = w - (hz - (jnp.concatenate([prev, hz[:-1]], 0) if ZB > 1 else prev))
                hz_last[i] = hz[-1:]
                old = wet_buf[i, zs, SUB:] * p if first else p
                new = old - scale_buf[i, zs] * flux
                p_out[i, zs, here] = new
                for k in range(ZB):
                    part = new[k, kept]
                    z = g * ZB + k
                    surface[i] = part if z == 0 else jnp.where(d_buf[i, kept] > float(z), part, surface[i])

        turned = [stage_a(0), stage_a(1)]
        ready = stage_b(0, turned[0])
        for g in range(groups):
            if g + 2 < groups:
                turned.append(stage_a(g + 2))
            coming = stage_b(g + 1, turned[g + 1]) if g + 1 < groups else None
            stage_c(g, *ready)
            ready = coming
        for i in range(2):
            trace[t, i] = surface[i]

    def two(k, carry):
        step(2 * k, False, p_buf, w_buf, p_two, w_two)
        step(2 * k + 1, False, p_two, w_two, p_buf, w_buf)
        return carry

    step(0, True, p_buf, w_buf, p_two, w_two)
    step(1, False, p_two, w_two, p_buf, w_buf)
    lax.fori_loop(1, STEPS // 2, two, 0)


def state_buffers(layers, wide, cols):
    return [
        VMEM(shape, jnp.float32)
        for shape in (
            (2, layers, wide + 2 * SUB, cols),
            (2, layers, wide, cols),
            (2, wide, cols),
            (2, layers, wide + SUB, cols),
            (2, layers, wide, cols),
            (2, layers - 1, wide, cols),
            (2, layers, wide + 2 * SUB, cols),
            (2, layers, wide, cols),
        )
    ]


def inner_kernel(keep_ref, other_ref, p_keep_ref, p_send_ref, trace_ref, *state):
    layers, inner_rows, cols = p_keep_ref.shape
    core = lax.axis_index("cross")
    low = core == 0
    span = inner_rows + 2 * SUB
    base = 2 * span * layers
    p_buf, w_buf, d_buf, wet_buf, scale_buf, half_buf, p_two, w_two = state
    lane = lanes_of((span, cols))
    at = base + 2 * span
    seam = jnp.where(low, keep_ref[at : at + span], other_ref[at : at + span])
    for tile, main_ref, seam_core in ((core, keep_ref, 1), (1 - core, other_ref, 0)):
        seam_lane = lane == jnp.where(core == seam_core, 0, -1)
        masks(
            main_ref[base : base + span],
            main_ref[base + span : base + 2 * span],
            d_buf, wet_buf, scale_buf, half_buf, tile,
        )
        for z in range(layers):
            at = 2 * span * z
            p_buf[tile, z, SUB : SUB + span] = main_ref[at : at + span]
            turned = pltpu.roll(seam, cols - z, 1) if z else seam
            w_buf[tile, z] = main_ref[at + span : at + 2 * span] - jnp.where(seam_lane, turned, 0.0)
    kept = slice(SUB, SUB + inner_rows)
    advance(p_buf, w_buf, d_buf, wet_buf, scale_buf, half_buf, p_two, w_two, trace_ref, kept)
    for z in range(layers):
        p_keep_ref[z] = p_buf[core, z, 2 * SUB : 2 * SUB + inner_rows]
        p_send_ref[z] = p_buf[1 - core, z, 2 * SUB : 2 * SUB + inner_rows]


def outer_kernel(
    keep_ref, other_ref, halo_ref, place_ref, inner_ref,
    p_keep_ref, p_send_ref, panel_keep_ref, panel_send_ref, trace, *state,
):
    layers, cols = p_keep_ref.shape[0], p_keep_ref.shape[2]
    inner_rows = inner_ref.shape[2]
    core = lax.axis_index("cross")
    low = core == 0
    span = inner_rows + 2 * SUB
    near = 2 * SUB
    base = 2 * span * layers
    base_z = 2 * SUB * layers
    ends = halo_ref.shape[0] // 2
    p_buf, w_buf, d_buf, wet_buf, scale_buf, half_buf, p_two, w_two = state
    lane = lanes_of((SUB, cols))
    row = rows_of((SUB, cols))
    offset = (span - near) * core

    def main_rows(ref, at):
        return ref[pl.ds(pl.multiple_of(at + offset, SUB), near)]

    def joined(main, halo):
        return jnp.where(
            low, jnp.concatenate([halo, main], 0), jnp.concatenate([main, halo], 0)
        )

    seam_at = base_z + 2 * SUB
    seam_halo = jnp.where(
        low, halo_ref[seam_at : seam_at + SUB], halo_ref[ends + seam_at : ends + seam_at + SUB]
    )
    seam_main = jnp.where(
        low, main_rows(keep_ref, base + 2 * span), main_rows(other_ref, base + 2 * span)
    )
    seam = joined(seam_main, seam_halo)
    top_row = row == jnp.where(low, 0, -1)
    end_row = row == jnp.where(low, -1, 0)
    wide_lane = lanes_of((near + SUB, cols))
    for tile, main_ref, end, seam_core in ((core, keep_ref, 0, 1), (1 - core, other_ref, ends, 0)):
        seam_lane = wide_lane == jnp.where(core == seam_core, 0, -1)

        def end_rows(at):
            return halo_ref[end + at : end + at + SUB]

        masks(
            joined(main_rows(main_ref, base), end_rows(base_z)),
            joined(main_rows(main_ref, base + span), end_rows(base_z + SUB)),
            d_buf, wet_buf, scale_buf, half_buf, tile,
        )
        for z in range(layers):
            at = 2 * span * z
            at_z = 2 * SUB * z
            p_buf[tile, z, SUB : 2 * SUB + near] = joined(main_rows(main_ref, at), end_rows(at_z))
            w = main_rows(main_ref, at + span)
            w_end = end_rows(at_z + SUB)
            slot = jnp.broadcast_to(w_end[0:1], (SUB, cols))
            final = base + 3 * span + z
            final = jnp.broadcast_to(main_ref[final : final + 1], (SUB, cols))
            w = jnp.concatenate([w[:SUB] - jnp.where(top_row, slot, 0.0), w[SUB:]], 0)
            w = joined(w, w_end - jnp.where(end_row, final, 0.0))
            turned = pltpu.roll(seam, cols - z, 1) if z else seam
            w_buf[tile, z] = w - jnp.where(seam_lane, turned, 0.0)
    kept = slice(SUB, 2 * SUB)
    advance(p_buf, w_buf, d_buf, wet_buf, scale_buf, half_buf, p_two, w_two, trace, kept)
    for z in range(layers):
        p_keep_ref[z] = p_buf[core, z, 2 * SUB : 3 * SUB]
        p_send_ref[z] = p_buf[1 - core, z, 2 * SUB : 3 * SUB]

    width = cols // 2
    lane_rows = lanes_of((inner_rows + SUB, cols))
    place = place_ref[...]
    count = place.shape[0] // 2
    parts = STEPS // 2
    for j in range(parts):
        pieces = []
        for i in range(2):
            one = jnp.concatenate([trace[2 * j, i], inner_ref[2 * j, i]], 0)
            two = jnp.concatenate([trace[2 * j + 1, i], inner_ref[2 * j + 1, i]], 0)
            pieces.append(jnp.where(lane_rows < width, one, pltpu.roll(two, width, 1)))
            pieces.append(jnp.where(lane_rows < width, pltpu.roll(one, width, 1), two))
        both = jnp.concatenate(pieces, 0)
        part_a = both.astype(jnp.bfloat16)
        rest = both - part_a.astype(jnp.float32)
        part_b = rest.astype(jnp.bfloat16)
        part_c = (rest - part_b.astype(jnp.float32)).astype(jnp.bfloat16)
        total = jnp.dot(place, part_a, preferred_element_type=jnp.float32)
        total += jnp.dot(place, part_b, preferred_element_type=jnp.float32)
        total += jnp.dot(place, part_c, preferred_element_type=jnp.float32)
        panel_keep_ref[pl.ds(j, count, stride=parts)] = total[:count]
        panel_send_ref[pl.ds(j, count, stride=parts)] = total[count:]


def shards(
    pressure_start, along_start, cross_start, depth_layers, stiffness, patch_lists, owner_map
):
    sensors, layers, rows, cols = pressure_start.shape
    f32 = jnp.float32
    along_count = lax.axis_size("along")
    cross_count = lax.axis_size("cross")
    low = lax.axis_index("cross") == 0
    swap = [(0, 1), (1, 0)]
    pair = ("along", "cross")
    steps_up = range(along_count - 1)
    route = [(2 * i, 2 * i + 2) for i in steps_up] + [(2 * i + 3, 2 * i + 1) for i in steps_up]
    half_rows = rows // 2
    span = half_rows + SUB
    pack_rows = 2 * span * layers + 3 * span + layers
    end_rows = 2 * SUB * layers + 3 * SUB

    spec = pl.BlockSpec(memory_space=VMEM)
    hbm = pl.BlockSpec(memory_space=pltpu.HBM)
    params = pltpu.CompilerParams(vmem_limit_bytes=32 * 1024 * 1024)
    keep, send, one, two, ids, owners = pl.pallas_call(
        edges_kernel,
        out_shape=[
            jax.ShapeDtypeStruct((pack_rows, cols), f32),
            jax.ShapeDtypeStruct((pack_rows + SUB, cols), f32),
            jax.ShapeDtypeStruct((end_rows, cols), f32),
            jax.ShapeDtypeStruct((end_rows, cols), f32),
            jax.ShapeDtypeStruct(patch_lists.shape, jnp.int32),
            jax.ShapeDtypeStruct((SUB, cols), f32),
        ],
        in_specs=[hbm] * 7,
        out_specs=[spec] * 6,
        scratch_shapes=[
            VMEM((layers, rows, cols), f32),
            VMEM((layers, rows, cols), f32),
            VMEM((layers, rows, cols), f32),
            VMEM((rows, cols), jnp.int32),
            VMEM((rows, cols), f32),
            VMEM(owner_map.shape, jnp.int32),
            pltpu.SemaphoreType.DMA((7,)),
        ],
        compiler_params=params,
        name="edges",
    )(
        *(
            pltpu.with_memory_space_constraint(x, pltpu.HBM)
            for x in (
                pressure_start[0],
                along_start[0],
                cross_start[0],
                depth_layers,
                stiffness,
                owner_map,
                patch_lists,
            )
        )
    )

    two = lax.ppermute(two, "cross", swap)
    halo = jnp.concatenate([one, two], 0)
    send = lax.optimization_barrier((send, two))[0]
    other = lax.ppermute(send, "cross", swap)
    halo = lax.ppermute(halo, pair, route)

    patch_count = 2 * rows
    owner_count = along_count * cross_count
    capacity = patch_count // owner_count + 1
    count = owner_count * capacity
    place = pl.pallas_call(
        functools.partial(
            place_kernel, owner_count=owner_count, chips=along_count, capacity=capacity
        ),
        out_shape=jax.ShapeDtypeStruct((2 * count, patch_count), jnp.bfloat16),
        in_specs=[spec] * 3,
        out_specs=spec,
        compiler_params=params,
        name="place",
    )(ids.reshape(-1, patch_count).T, owners, other)

    parts = STEPS // 2
    inner_rows = half_rows - SUB
    inner_shape = jax.ShapeDtypeStruct((layers, inner_rows, cols), f32)
    inner_keep, inner_send, inner_trace = pl.pallas_call(
        inner_kernel,
        out_shape=[
            inner_shape,
            inner_shape,
            jax.ShapeDtypeStruct((STEPS, 2, inner_rows, cols), f32),
        ],
        in_specs=[spec] * 2,
        out_specs=[spec] * 3,
        scratch_shapes=state_buffers(layers, span, cols),
        compiler_params=params,
        cost_estimate=pl.CostEstimate(
            flops=400 * layers * span * cols,
            bytes_accessed=200 * layers * span * cols,
            transcendentals=0,
        ),
        name="inner",
    )(keep, other)
    outer_shape = jax.ShapeDtypeStruct((layers, SUB, cols), f32)
    panel_shape = jax.ShapeDtypeStruct((count * parts, cols), f32)
    outer_keep, outer_send, panel_keep, panel_send = pl.pallas_call(
        outer_kernel,
        out_shape=[outer_shape, outer_shape, panel_shape, panel_shape],
        in_specs=[spec] * 5,
        out_specs=[spec] * 4,
        scratch_shapes=[VMEM((STEPS, 2, SUB, cols), f32)] + state_buffers(layers, 3 * SUB, cols),
        compiler_params=params,
        name="outer",
    )(keep, other, halo, place, inner_trace)

    panels = panel_keep + lax.ppermute(panel_send, "cross", swap)
    if along_count == 4:
        some = 2 * capacity * parts
        ring = range(along_count)
        pieces = [panels[:some]]
        for k in range(1, along_count):
            pieces.append(
                lax.ppermute(
                    panels[k * some : (k + 1) * some],
                    "along",
                    [(i, (i + k) % along_count) for i in ring],
                )
            )
        received = pl.pallas_call(
            gather_kernel,
            out_shape=jax.ShapeDtypeStruct((count * parts, cols), f32),
            in_specs=[spec] * 4,
            out_specs=hbm,
            scratch_shapes=[pltpu.SemaphoreType.DMA((4,))],
            compiler_params=params,
            name="gather",
        )(*pieces)
    else:
        panels = panels.reshape(along_count, 2 * capacity * parts, cols)
        received = lax.all_to_all(panels, "along", split_axis=0, concat_axis=0, tiled=True)
    received = received.reshape(1, count, 1, parts * cols)

    inner_other = lax.ppermute(inner_send, "cross", swap)
    outer_other = lax.ppermute(outer_send, "cross", swap)
    pressure = jnp.where(
        low,
        jnp.concatenate([outer_keep, inner_keep, inner_other, outer_other], 1),
        jnp.concatenate([outer_other, inner_other, inner_keep, outer_keep], 1),
    )
    return (pressure[None], received)


def solution(mesh):
    in_specs = (
        P("batch", None, "along", "cross"),
        P("batch", None, "along", "cross"),
        P("batch", None, "along", "cross"),
        P("along", "cross"),
        P("along", "cross"),
        P("batch", None),
        P(("along", "cross"), None),
    )
    out_specs = (P("batch", None, "along", "cross"), P(("along", "cross"), None, "batch", None))
    return jax.shard_map(shards, mesh=mesh, in_specs=in_specs, out_specs=out_specs, check_vma=False)
```

```python
import functools

import jax
import jax.numpy as jnp
from jax import lax
from jax.experimental import pallas as pl
from jax.experimental.pallas import tpu as pltpu
from jax.sharding import PartitionSpec as P

STEPS = 8
SUB = 8
VMEM = pltpu.VMEM


def lanes_of(shape):
    return lax.broadcasted_iota(jnp.int32, shape, len(shape) - 1)


def rows_of(shape):
    return lax.broadcasted_iota(jnp.int32, shape, len(shape) - 2)


def edges_kernel(
    p_hbm, fa_hbm, fc_hbm, depth_hbm, stiff_hbm, owner_hbm, ids_hbm,
    keep_ref, send_ref, one_ref, two_ref, ids_ref, owners_ref,
    p_ref, fa_ref, fc_ref, depth_ref, stiff_ref, owner_ref, sems,
):
    copies = [
        pltpu.make_async_copy(source, target, sems.at[i])
        for i, (source, target) in enumerate(
            (
                (depth_hbm, depth_ref),
                (stiff_hbm, stiff_ref),
                (owner_hbm, owner_ref),
                (ids_hbm, ids_ref),
                (fa_hbm, fa_ref),
                (fc_hbm, fc_ref),
                (p_hbm, p_ref),
            )
        )
    ]
    for copy in copies:
        copy.start()
    for copy in copies:
        copy.wait()
    layers, rows, cols = p_ref.shape
    low = lax.axis_index("cross") == 0
    span = rows // 2 + SUB
    last = rows - SUB
    lane = lanes_of((rows, cols))
    row = rows_of((rows, cols))
    row_sub = rows_of((SUB, cols))
    depth = depth_ref[...]
    stiff = stiff_ref[...]
    first_lane = lane == 0
    slot_one = row_sub == jnp.where(low, 0, -1)
    slot_two = row_sub == jnp.where(low, -1, 0)
    base = 2 * span * layers
    base_z = 2 * SUB * layers
    velocity = jnp.zeros((rows, cols), jnp.float32)

    def halves(array):
        first, second = array[:span], array[rows - span :]
        return jnp.where(low, first, second), jnp.where(low, second, first)

    def ends(array):
        first, second = array[:SUB], array[last:]
        return jnp.where(low, second, first), jnp.where(low, first, second)

    for z in range(layers):
        wet = depth > z
        p = p_ref[z]
        va = jnp.where(wet, fa_ref[z], 0.0)
        vc = jnp.where(wet, fc_ref[z], 0.0)
        behind = jnp.where(row == 0, 0.0, pltpu.roll(va, 1, 0))
        before = jnp.where(first_lane, 0.0, pltpu.roll(vc, 1, 1))
        w = (va - behind) + (vc - before)
        velocity = jnp.where(lane == z, pltpu.roll(vc, z + 1, 1), velocity)
        at = 2 * span * z
        keep_ref[at : at + span], send_ref[at : at + span] = halves(p)
        at += span
        keep_ref[at : at + span], send_ref[at : at + span] = halves(w)
        final = va[rows - 1 : rows]
        at = base + 3 * span + z
        keep_ref[at : at + 1] = final
        send_ref[at : at + 1] = final
        at = 2 * SUB * z
        one_ref[at : at + SUB], two_ref[at : at + SUB] = ends(p)
        at += SUB
        one, two = ends(w)
        final = jnp.broadcast_to(final, (SUB, cols))
        one_ref[at : at + SUB] = jnp.where(slot_one, final, one)
        two_ref[at : at + SUB] = jnp.where(slot_two, final, two)
    for i, array in enumerate((depth.astype(jnp.float32), stiff, velocity)):
        at = base + span * i
        keep_ref[at : at + span], send_ref[at : at + span] = halves(array)
        at = base_z + SUB * i
        one_ref[at : at + SUB], two_ref[at : at + SUB] = ends(array)
    at = base + 3 * span + layers
    owners = jnp.broadcast_to(owner_ref[...].astype(jnp.float32), (SUB, cols))
    owners_ref[...] = owners
    send_ref[at : at + SUB] = owners


def place_kernel(ids_ref, own_ref, other_ref, place_ref, *, owner_count, chips, capacity):
    along = lax.axis_index("along")
    cross = lax.axis_index("cross")
    low = cross == 0
    cores = owner_count // chips
    patches = own_ref.shape[1]
    last = other_ref.shape[0] - SUB
    own = own_ref[0:1]
    other = other_ref[last : last + 1]
    owners = [jnp.where(low, own, other), jnp.where(low, other, own)]
    lane = lanes_of((patches, patches))
    half = patches // 2
    block = lane // half
    within = lane % half
    held = half // 2
    turn = (held - SUB) * cross
    patch = half * cross + 2 * lax.rem(within % held + turn, held) + within // held
    source = rows_of((patches, patches))
    number = rows_of((owner_count, patches)).astype(jnp.float32)
    chosen = jnp.zeros((owner_count, patches), jnp.float32)
    counts = jnp.zeros((owner_count, patches), jnp.float32)
    for i in range(2):
        owned = (number == owners[i]).astype(jnp.bfloat16)
        pick = jnp.where(block == i, jnp.where(source == patch, 1.0, 0.0), 0.0).astype(jnp.bfloat16)
        earlier = jnp.where(block == i, jnp.where(source < patch, 1.0, 0.0), 0.0).astype(jnp.bfloat16)
        chosen += jnp.dot(owned, pick, preferred_element_type=jnp.float32)
        counts += jnp.dot(owned, earlier, preferred_element_type=jnp.float32)
    rank = jnp.sum(chosen * counts, axis=0, keepdims=True).astype(jnp.int32)
    owner = jnp.sum(chosen * number, axis=0, keepdims=True).astype(jnp.int32)
    wanted = (along * cores + block) * patches + patch
    found = jnp.zeros((patches, patches), jnp.float32)
    for j in range(ids_ref.shape[1]):
        found = jnp.where(ids_ref[:, j : j + 1] == wanted, 1.0, found)
    member = jnp.sum(found, axis=0, keepdims=True)
    block = block[:1]
    chip = owner // cores
    owner_core = owner % cores
    some = 2 * capacity
    slot = block * capacity + rank
    if chips == 4:
        ahead = lax.rem(chip - along + chips, chips)
        slot = slot + ahead * some
    else:
        slot = slot + chip * some
    handler = owner_core
    slot = jnp.where(handler == cross, slot, slot + chips * some)
    slot = jnp.where(member > 0.0, slot, -1)
    place_ref[...] = jnp.where(rows_of(place_ref.shape) == slot, 1.0, 0.0).astype(jnp.bfloat16)


def gather_kernel(own_ref, one_ref, two_ref, three_ref, out_ref, sems):
    chips = 4
    along = lax.axis_index("along")
    count = out_ref.shape[0] // chips
    copies = []
    for i, (ref, ahead) in enumerate(
        ((own_ref, 0), (one_ref, 3), (two_ref, 2), (three_ref, 1))
    ):
        at = pl.multiple_of(lax.rem(along + ahead, chips) * count, SUB)
        copies.append(pltpu.make_async_copy(ref, out_ref.at[pl.ds(at, count)], sems.at[i]))
    for copy in copies:
        copy.start()
    for copy in copies:
        copy.wait()


def masks(depth, stiff, d_buf, wet_buf, scale_buf, half_buf, tile):
    layers = wet_buf.shape[1]
    zeros = jnp.zeros((SUB, depth.shape[1]), jnp.float32)
    d_buf[tile] = depth
    for z in range(layers):
        wet = depth > float(z)
        wet_buf[tile, z, :SUB] = zeros
        wet_buf[tile, z, SUB:] = jnp.where(wet, 1.0, 0.0)
        scale_buf[tile, z] = jnp.where(wet, stiff, 0.0)
        if z > 0:
            half_buf[tile, z - 1] = jnp.where(wet, 0.5, 0.0)


def advance(state, before_step, after_step, ZB):
    p_buf, w_buf, d_buf, wet_buf, scale_buf, half_buf, p_two, w_two = state
    layers = p_buf.shape[1]
    wide, cols = w_buf.shape[2:]
    groups = layers // ZB
    lane = lanes_of((ZB, wide, cols))
    last_lane = lane == cols - 1
    first_lane = lane == 0
    zeros = jnp.zeros((SUB, cols), jnp.float32)
    for tile in range(2):
        for z in range(layers):
            for buf in (p_buf, p_two):
                buf[tile, z, :SUB] = zeros
                buf[tile, z, SUB + wide :] = zeros
    here = slice(SUB, SUB + wide)
    ahead = slice(SUB + 1, SUB + 1 + wide)
    back_rows = slice(SUB - 1, SUB - 1 + wide)

    def step(t, first, p_buf, w_buf, p_out, w_out):
        before_step(t, p_buf)

        def stage_a(g):
            zs = slice(g * ZB, (g + 1) * ZB)
            return [pltpu.roll(p_buf[i, zs, here], cols - 1, 2) for i in range(2)]

        def stage_b(g, turned):
            zs = slice(g * ZB, (g + 1) * ZB)
            right = [
                jnp.where(last_lane, turned[1], turned[0]),
                jnp.where(last_lane, 0.0, turned[1]),
            ]
            gy = [wet_buf[i, zs, SUB:] * (right[i] - p_buf[i, zs, here]) for i in range(2)]
            return gy, [pltpu.roll(gy[i], 1, 2) for i in range(2)]

        hz_last = [None, None]
        surface = [None, None]

        def stage_c(g, gy, back):
            zs = slice(g * ZB, (g + 1) * ZB)
            before = [
                jnp.where(first_lane, 0.0, back[0]),
                jnp.where(first_lane, back[0], back[1]),
            ]
            for i in range(2):
                p = p_buf[i, zs, here]
                w = w_buf[i, zs] - (gy[i] - before[i])
                gx = wet_buf[i, zs, SUB:] * (p_buf[i, zs, ahead] - p)
                behind = wet_buf[i, zs, SUB - 1 : SUB - 1 + wide] * (p - p_buf[i, zs, back_rows])
                w = w - (gx - behind)
                w_out[i, zs] = w
                if g + 1 < groups:
                    hz = half_buf[i, zs] * (p_buf[i, g * ZB + 1 : (g + 1) * ZB + 1, here] - p)
                elif ZB > 1:
                    hz = jnp.concatenate([half_buf[i, g * ZB :] * (p[1:] - p[:-1]), jnp.zeros((1, wide, cols), jnp.float32)], 0)
                else:
                    hz = jnp.zeros((1, wide, cols), jnp.float32)
                prev = jnp.zeros((1, wide, cols), jnp.float32) if g == 0 else hz_last[i]
                flux = w - (hz - (jnp.concatenate([prev, hz[:-1]], 0) if ZB > 1 else prev))
                hz_last[i] = hz[-1:]
                old = wet_buf[i, zs, SUB:] * p if first else p
                new = old - scale_buf[i, zs] * flux
                p_out[i, zs, here] = new
                for k in range(ZB):
                    part = new[k]
                    z = g * ZB + k
                    surface[i] = part if z == 0 else jnp.where(d_buf[i] > float(z), part, surface[i])

        turned = [stage_a(0), stage_a(1)]
        ready = stage_b(0, turned[0])
        for g in range(groups):
            if g + 2 < groups:
                turned.append(stage_a(g + 2))
            coming = stage_b(g + 1, turned[g + 1]) if g + 1 < groups else None
            stage_c(g, *ready)
            ready = coming
        for i in range(2):
            after_step(t, i, surface[i])

    def two(k, carry):
        step(2 * k, False, p_buf, w_buf, p_two, w_two)
        step(2 * k + 1, False, p_two, w_two, p_buf, w_buf)
        return carry

    step(0, True, p_buf, w_buf, p_two, w_two)
    step(1, False, p_two, w_two, p_buf, w_buf)
    lax.fori_loop(1, STEPS // 2, two, 0)


def state_buffers(layers, wide, cols):
    return [
        VMEM(shape, jnp.float32)
        for shape in (
            (2, layers, wide + 2 * SUB, cols),
            (2, layers, wide, cols),
            (2, wide, cols),
            (2, layers, wide + SUB, cols),
            (2, layers, wide, cols),
            (2, layers - 1, wide, cols),
            (2, layers, wide + 2 * SUB, cols),
            (2, layers, wide, cols),
        )
    ]


def inner_kernel(keep_ref, other_ref, p_keep_ref, p_send_ref, trace_ref, border_ref, *state):
    layers, inner_rows, cols = p_keep_ref.shape
    core = lax.axis_index("cross")
    low = core == 0
    span = inner_rows + 2 * SUB
    base = 2 * span * layers
    p_buf, w_buf, d_buf, wet_buf, scale_buf, half_buf, p_two, w_two = state
    lane = lanes_of((span, cols))
    at = base + 2 * span
    seam = jnp.where(low, keep_ref[at : at + span], other_ref[at : at + span])
    for tile, main_ref, seam_core in ((core, keep_ref, 1), (1 - core, other_ref, 0)):
        seam_lane = lane == jnp.where(core == seam_core, 0, -1)
        masks(
            main_ref[base : base + span],
            main_ref[base + span : base + 2 * span],
            d_buf, wet_buf, scale_buf, half_buf, tile,
        )
        for z in range(layers):
            at = 2 * span * z
            p_buf[tile, z, SUB : SUB + span] = main_ref[at : at + span]
            turned = pltpu.roll(seam, cols - z, 1) if z else seam
            w_buf[tile, z] = main_ref[at + span : at + 2 * span] - jnp.where(seam_lane, turned, 0.0)

    def before_step(t, p_now):
        for i in range(2):
            for z in range(layers):
                first, second = 2 * SUB, span - 1
                border_ref[t, i, z : z + 1] = jnp.where(
                    low, p_now[i, z, first : first + 1], p_now[i, z, second : second + 1]
                )

    def after_step(t, i, surface):
        trace_ref[t, i] = surface[SUB : SUB + inner_rows]

    advance(state, before_step, after_step, 4)
    for z in range(layers):
        p_keep_ref[z] = p_buf[core, z, 2 * SUB : 2 * SUB + inner_rows]
        p_send_ref[z] = p_buf[1 - core, z, 2 * SUB : 2 * SUB + inner_rows]


def outer_kernel(
    keep_ref, other_ref, halo_ref, place_ref, inner_ref, border_ref,
    p_keep_ref, p_send_ref, panel_keep_ref, panel_send_ref, trace, *state,
):
    layers, cols = p_keep_ref.shape[0], p_keep_ref.shape[2]
    inner_rows = inner_ref.shape[2]
    core = lax.axis_index("cross")
    low = core == 0
    span = inner_rows + 2 * SUB
    near = SUB
    base = 2 * span * layers
    base_z = 2 * SUB * layers
    ends = halo_ref.shape[0] // 2
    p_buf, w_buf, d_buf, wet_buf, scale_buf, half_buf, p_two, w_two = state
    lane = lanes_of((SUB, cols))
    row = rows_of((SUB, cols))
    offset = (span - near) * core

    def main_rows(ref, at):
        return ref[pl.ds(pl.multiple_of(at + offset, SUB), near)]

    def joined(main, halo):
        return jnp.where(
            low, jnp.concatenate([halo, main], 0), jnp.concatenate([main, halo], 0)
        )

    seam_at = base_z + 2 * SUB
    seam_halo = jnp.where(
        low, halo_ref[seam_at : seam_at + SUB], halo_ref[ends + seam_at : ends + seam_at + SUB]
    )
    seam_main = jnp.where(
        low, main_rows(keep_ref, base + 2 * span), main_rows(other_ref, base + 2 * span)
    )
    seam = joined(seam_main, seam_halo)
    top_row = row == jnp.where(low, 0, -1)
    end_row = row == jnp.where(low, -1, 0)
    wide_lane = lanes_of((near + SUB, cols))
    for tile, main_ref, end, seam_core in ((core, keep_ref, 0, 1), (1 - core, other_ref, ends, 0)):
        seam_lane = wide_lane == jnp.where(core == seam_core, 0, -1)

        def end_rows(at):
            return halo_ref[end + at : end + at + SUB]

        masks(
            joined(main_rows(main_ref, base), end_rows(base_z)),
            joined(main_rows(main_ref, base + span), end_rows(base_z + SUB)),
            d_buf, wet_buf, scale_buf, half_buf, tile,
        )
        for z in range(layers):
            at = 2 * span * z
            at_z = 2 * SUB * z
            p_buf[tile, z, SUB : 2 * SUB + near] = joined(main_rows(main_ref, at), end_rows(at_z))
            w = main_rows(main_ref, at + span)
            w_end = end_rows(at_z + SUB)
            slot = jnp.broadcast_to(w_end[0:1], (SUB, cols))
            final = base + 3 * span + z
            final = jnp.broadcast_to(main_ref[final : final + 1], (SUB, cols))
            w = joined(w - jnp.where(top_row, slot, 0.0), w_end - jnp.where(end_row, final, 0.0))
            turned = pltpu.roll(seam, cols - z, 1) if z else seam
            w_buf[tile, z] = w - jnp.where(seam_lane, turned, 0.0)
        for z in range(layers):
            first, second = base + SUB, base + span - SUB - 1
            depth = jnp.where(
                low, main_ref[first : first + 1], main_ref[second : second + 1]
            )
            wet_buf[tile, z, SUB - 1 : SUB] = jnp.where(depth > float(z), 1.0, 0.0)

    def before_step(t, p_now):
        for i in range(2):
            for z in range(layers):
                value = border_ref[t, i, z : z + 1]
                p_now[i, z, SUB - 1 : SUB] = value
                p_now[i, z, 2 * SUB + near : 2 * SUB + near + 1] = value

    def after_step(t, i, surface):
        trace[t, i] = jnp.where(low, surface[SUB:], surface[:SUB])

    advance(state, before_step, after_step, 8)
    own = pl.multiple_of(SUB + SUB * (1 - core), SUB)
    for z in range(layers):
        p_keep_ref[z] = p_buf[core, z, pl.ds(own, SUB)]
        p_send_ref[z] = p_buf[1 - core, z, pl.ds(own, SUB)]

    width = cols // 2
    lane_rows = lanes_of((inner_rows + SUB, cols))
    place = place_ref[...]
    count = place.shape[0] // 2
    parts = STEPS // 2
    for j in range(parts):
        pieces = []
        for i in range(2):
            one = jnp.concatenate([trace[2 * j, i], inner_ref[2 * j, i]], 0)
            two = jnp.concatenate([trace[2 * j + 1, i], inner_ref[2 * j + 1, i]], 0)
            pieces.append(jnp.where(lane_rows < width, one, pltpu.roll(two, width, 1)))
            pieces.append(jnp.where(lane_rows < width, pltpu.roll(one, width, 1), two))
        both = jnp.concatenate(pieces, 0)
        part_a = both.astype(jnp.bfloat16)
        rest = both - part_a.astype(jnp.float32)
        part_b = rest.astype(jnp.bfloat16)
        part_c = (rest - part_b.astype(jnp.float32)).astype(jnp.bfloat16)
        total = jnp.dot(place, part_a, preferred_element_type=jnp.float32)
        total += jnp.dot(place, part_b, preferred_element_type=jnp.float32)
        total += jnp.dot(place, part_c, preferred_element_type=jnp.float32)
        panel_keep_ref[pl.ds(j, count, stride=parts)] = total[:count]
        panel_send_ref[pl.ds(j, count, stride=parts)] = total[count:]


def shards(
    pressure_start, along_start, cross_start, depth_layers, stiffness, patch_lists, owner_map
):
    sensors, layers, rows, cols = pressure_start.shape
    f32 = jnp.float32
    along_count = lax.axis_size("along")
    cross_count = lax.axis_size("cross")
    low = lax.axis_index("cross") == 0
    swap = [(0, 1), (1, 0)]
    pair = ("along", "cross")
    steps_up = range(along_count - 1)
    route = [(2 * i, 2 * i + 2) for i in steps_up] + [(2 * i + 3, 2 * i + 1) for i in steps_up]
    half_rows = rows // 2
    span = half_rows + SUB
    pack_rows = 2 * span * layers + 3 * span + layers
    end_rows = 2 * SUB * layers + 3 * SUB

    spec = pl.BlockSpec(memory_space=VMEM)
    hbm = pl.BlockSpec(memory_space=pltpu.HBM)
    params = pltpu.CompilerParams(vmem_limit_bytes=32 * 1024 * 1024)
    keep, send, one, two, ids, owners = pl.pallas_call(
        edges_kernel,
        out_shape=[
            jax.ShapeDtypeStruct((pack_rows, cols), f32),
            jax.ShapeDtypeStruct((pack_rows + SUB, cols), f32),
            jax.ShapeDtypeStruct((end_rows, cols), f32),
            jax.ShapeDtypeStruct((end_rows, cols), f32),
            jax.ShapeDtypeStruct(patch_lists.shape, jnp.int32),
            jax.ShapeDtypeStruct((SUB, cols), f32),
        ],
        in_specs=[hbm] * 7,
        out_specs=[spec] * 6,
        scratch_shapes=[
            VMEM((layers, rows, cols), f32),
            VMEM((layers, rows, cols), f32),
            VMEM((layers, rows, cols), f32),
            VMEM((rows, cols), jnp.int32),
            VMEM((rows, cols), f32),
            VMEM(owner_map.shape, jnp.int32),
            pltpu.SemaphoreType.DMA((7,)),
        ],
        compiler_params=params,
        name="edges",
    )(
        *(
            pltpu.with_memory_space_constraint(x, pltpu.HBM)
            for x in (
                pressure_start[0],
                along_start[0],
                cross_start[0],
                depth_layers,
                stiffness,
                owner_map,
                patch_lists,
            )
        )
    )

    two = lax.ppermute(two, "cross", swap)
    halo = jnp.concatenate([one, two], 0)
    send = lax.optimization_barrier((send, two))[0]
    other = lax.ppermute(send, "cross", swap)
    halo = lax.ppermute(halo, pair, route)

    patch_count = 2 * rows
    owner_count = along_count * cross_count
    capacity = patch_count // owner_count + 1
    count = owner_count * capacity
    place = pl.pallas_call(
        functools.partial(
            place_kernel, owner_count=owner_count, chips=along_count, capacity=capacity
        ),
        out_shape=jax.ShapeDtypeStruct((2 * count, patch_count), jnp.bfloat16),
        in_specs=[spec] * 3,
        out_specs=spec,
        compiler_params=params,
        name="place",
    )(ids.reshape(-1, patch_count).T, owners, other)

    parts = STEPS // 2
    inner_rows = half_rows - SUB
    inner_shape = jax.ShapeDtypeStruct((layers, inner_rows, cols), f32)
    inner_keep, inner_send, inner_trace, border = pl.pallas_call(
        inner_kernel,
        out_shape=[
            inner_shape,
            inner_shape,
            jax.ShapeDtypeStruct((STEPS, 2, inner_rows, cols), f32),
            jax.ShapeDtypeStruct((STEPS, 2, layers, cols), f32),
        ],
        in_specs=[spec] * 2,
        out_specs=[spec] * 4,
        scratch_shapes=state_buffers(layers, span, cols),
        compiler_params=params,
        cost_estimate=pl.CostEstimate(
            flops=400 * layers * span * cols,
            bytes_accessed=200 * layers * span * cols,
            transcendentals=0,
        ),
        name="inner",
    )(keep, other)
    outer_shape = jax.ShapeDtypeStruct((layers, SUB, cols), f32)
    panel_shape = jax.ShapeDtypeStruct((count * parts, cols), f32)
    outer_keep, outer_send, panel_keep, panel_send = pl.pallas_call(
        outer_kernel,
        out_shape=[outer_shape, outer_shape, panel_shape, panel_shape],
        in_specs=[spec] * 6,
        out_specs=[spec] * 4,
        scratch_shapes=[VMEM((STEPS, 2, SUB, cols), f32)] + state_buffers(layers, 2 * SUB, cols),
        compiler_params=params,
        name="outer",
    )(keep, other, halo, place, inner_trace, border)

    panels = panel_keep + lax.ppermute(panel_send, "cross", swap)
    if along_count == 4:
        some = 2 * capacity * parts
        ring = range(along_count)
        pieces = [panels[:some]]
        for k in range(1, along_count):
            pieces.append(
                lax.ppermute(
                    panels[k * some : (k + 1) * some],
                    "along",
                    [(i, (i + k) % along_count) for i in ring],
                )
            )
        received = pl.pallas_call(
            gather_kernel,
            out_shape=jax.ShapeDtypeStruct((count * parts, cols), f32),
            in_specs=[spec] * 4,
            out_specs=hbm,
            scratch_shapes=[pltpu.SemaphoreType.DMA((4,))],
            compiler_params=params,
            name="gather",
        )(*pieces)
    else:
        panels = panels.reshape(along_count, 2 * capacity * parts, cols)
        received = lax.all_to_all(panels, "along", split_axis=0, concat_axis=0, tiled=True)
    received = received.reshape(1, count, 1, parts * cols)

    inner_other = lax.ppermute(inner_send, "cross", swap)
    outer_other = lax.ppermute(outer_send, "cross", swap)
    pressure = jnp.where(
        low,
        jnp.concatenate([outer_keep, inner_keep, inner_other, outer_other], 1),
        jnp.concatenate([outer_other, inner_other, inner_keep, outer_keep], 1),
    )
    return (pressure[None], received)


def solution(mesh):
    in_specs = (
        P("batch", None, "along", "cross"),
        P("batch", None, "along", "cross"),
        P("batch", None, "along", "cross"),
        P("along", "cross"),
        P("along", "cross"),
        P("batch", None),
        P(("along", "cross"), None),
    )
    out_specs = (P("batch", None, "along", "cross"), P(("along", "cross"), None, "batch", None))
    return jax.shard_map(shards, mesh=mesh, in_specs=in_specs, out_specs=out_specs, check_vma=False)
```

```python
import functools

import jax
import jax.numpy as jnp
from jax import lax
from jax.experimental import pallas as pl
from jax.experimental.pallas import tpu as pltpu
from jax.sharding import PartitionSpec as P

STEPS = 8
SUB = 8
VMEM = pltpu.VMEM


def lanes_of(shape):
    return lax.broadcasted_iota(jnp.int32, shape, len(shape) - 1)


def rows_of(shape):
    return lax.broadcasted_iota(jnp.int32, shape, len(shape) - 2)


def edges_kernel(
    p_hbm, fa_hbm, fc_hbm, depth_hbm, stiff_hbm, owner_hbm, ids_hbm,
    keep_ref, send_ref, one_ref, two_ref, ids_ref, owners_ref,
    p_ref, fa_ref, fc_ref, depth_ref, stiff_ref, owner_ref, sems,
):
    copies = [
        pltpu.make_async_copy(source, target, sems.at[i])
        for i, (source, target) in enumerate(
            (
                (depth_hbm, depth_ref),
                (stiff_hbm, stiff_ref),
                (owner_hbm, owner_ref),
                (ids_hbm, ids_ref),
                (fa_hbm, fa_ref),
                (fc_hbm, fc_ref),
                (p_hbm, p_ref),
            )
        )
    ]
    for copy in copies:
        copy.start()
    for copy in copies:
        copy.wait()
    layers, rows, cols = p_ref.shape
    low = lax.axis_index("cross") == 0
    span = rows // 2 + SUB
    last = rows - SUB
    lane = lanes_of((rows, cols))
    row = rows_of((rows, cols))
    row_sub = rows_of((SUB, cols))
    depth = depth_ref[...]
    stiff = stiff_ref[...]
    first_lane = lane == 0
    slot_one = row_sub == jnp.where(low, 0, -1)
    slot_two = row_sub == jnp.where(low, -1, 0)
    base = 2 * span * layers
    base_z = 2 * SUB * layers
    velocity = jnp.zeros((rows, cols), jnp.float32)

    def halves(array):
        first, second = array[:span], array[rows - span :]
        return jnp.where(low, first, second), jnp.where(low, second, first)

    def ends(array):
        first, second = array[:SUB], array[last:]
        return jnp.where(low, second, first), jnp.where(low, first, second)

    for z in range(layers):
        wet = depth > z
        p = p_ref[z]
        va = jnp.where(wet, fa_ref[z], 0.0)
        vc = jnp.where(wet, fc_ref[z], 0.0)
        behind = jnp.where(row == 0, 0.0, pltpu.roll(va, 1, 0))
        before = jnp.where(first_lane, 0.0, pltpu.roll(vc, 1, 1))
        w = (va - behind) + (vc - before)
        velocity = jnp.where(lane == z, pltpu.roll(vc, z + 1, 1), velocity)
        at = 2 * span * z
        keep_ref[at : at + span], send_ref[at : at + span] = halves(p)
        at += span
        keep_ref[at : at + span], send_ref[at : at + span] = halves(w)
        final = va[rows - 1 : rows]
        at = base + 3 * span + z
        keep_ref[at : at + 1] = final
        send_ref[at : at + 1] = final
        at = 2 * SUB * z
        one_ref[at : at + SUB], two_ref[at : at + SUB] = ends(p)
        at += SUB
        one, two = ends(w)
        final = jnp.broadcast_to(final, (SUB, cols))
        one_ref[at : at + SUB] = jnp.where(slot_one, final, one)
        two_ref[at : at + SUB] = jnp.where(slot_two, final, two)
    for i, array in enumerate((depth.astype(jnp.float32), stiff, velocity)):
        at = base + span * i
        keep_ref[at : at + span], send_ref[at : at + span] = halves(array)
        at = base_z + SUB * i
        one_ref[at : at + SUB], two_ref[at : at + SUB] = ends(array)
    at = base + 3 * span + layers
    owners = jnp.broadcast_to(owner_ref[...].astype(jnp.float32), (SUB, cols))
    owners_ref[...] = owners
    send_ref[at : at + SUB] = owners


def place_kernel(ids_ref, own_ref, other_ref, place_ref, *, owner_count, chips, capacity):
    along = lax.axis_index("along")
    cross = lax.axis_index("cross")
    low = cross == 0
    cores = owner_count // chips
    patches = own_ref.shape[1]
    last = other_ref.shape[0] - SUB
    own = own_ref[0:1]
    other = other_ref[last : last + 1]
    owners = [jnp.where(low, own, other), jnp.where(low, other, own)]
    lane = lanes_of((patches, patches))
    half = patches // 2
    block = lane // half
    within = lane % half
    held = half // 2
    turn = (held - SUB) * cross
    patch = half * cross + 2 * lax.rem(within % held + turn, held) + within // held
    source = rows_of((patches, patches))
    number = rows_of((owner_count, patches)).astype(jnp.float32)
    chosen = jnp.zeros((owner_count, patches), jnp.float32)
    counts = jnp.zeros((owner_count, patches), jnp.float32)
    for i in range(2):
        owned = (number == owners[i]).astype(jnp.bfloat16)
        pick = jnp.where(block == i, jnp.where(source == patch, 1.0, 0.0), 0.0).astype(jnp.bfloat16)
        earlier = jnp.where(block == i, jnp.where(source < patch, 1.0, 0.0), 0.0).astype(jnp.bfloat16)
        chosen += jnp.dot(owned, pick, preferred_element_type=jnp.float32)
        counts += jnp.dot(owned, earlier, preferred_element_type=jnp.float32)
    rank = jnp.sum(chosen * counts, axis=0, keepdims=True).astype(jnp.int32)
    owner = jnp.sum(chosen * number, axis=0, keepdims=True).astype(jnp.int32)
    wanted = (along * cores + block) * patches + patch
    found = jnp.zeros((patches, patches), jnp.float32)
    for j in range(ids_ref.shape[1]):
        found = jnp.where(ids_ref[:, j : j + 1] == wanted, 1.0, found)
    member = jnp.sum(found, axis=0, keepdims=True)
    block = block[:1]
    chip = owner // cores
    owner_core = owner % cores
    some = 2 * capacity
    slot = block * capacity + rank
    if chips == 4:
        slot = slot + lax.rem(chip - along + 2 * chips - 1, chips) * some
    else:
        slot = slot + chip * some
    handler = owner_core
    slot = jnp.where(handler == cross, slot, slot + chips * some)
    slot = jnp.where(member > 0.0, slot, -1)
    place_ref[...] = jnp.where(rows_of(place_ref.shape) == slot, 1.0, 0.0).astype(jnp.bfloat16)


def gather_kernel(own_ref, one_ref, two_ref, three_ref, out_ref, sems):
    chips = 4
    along = lax.axis_index("along")
    count = out_ref.shape[0] // chips
    copies = []
    for i, (ref, ahead) in enumerate(
        ((own_ref, 0), (one_ref, 3), (two_ref, 2), (three_ref, 1))
    ):
        at = pl.multiple_of(lax.rem(along + ahead, chips) * count, SUB)
        copies.append(pltpu.make_async_copy(ref, out_ref.at[pl.ds(at, count)], sems.at[i]))
    for copy in copies:
        copy.start()
    for copy in copies:
        copy.wait()


def masks(depth, stiff, d_buf, wet_buf, scale_buf, half_buf, tile):
    layers = wet_buf.shape[1]
    zeros = jnp.zeros((SUB, depth.shape[1]), jnp.float32)
    d_buf[tile] = depth
    for z in range(layers):
        wet = depth > float(z)
        wet_buf[tile, z, :SUB] = zeros
        wet_buf[tile, z, SUB:] = jnp.where(wet, 1.0, 0.0)
        scale_buf[tile, z] = jnp.where(wet, stiff, 0.0)
        if z > 0:
            half_buf[tile, z - 1] = jnp.where(wet, 0.5, 0.0)


def advance(state, before_step, after_step, ZB, low_row=0, high_row=None):
    p_buf, w_buf, d_buf, wet_buf, scale_buf, half_buf, p_two, w_two = state
    layers = p_buf.shape[1]
    wide, cols = w_buf.shape[2:]
    groups = layers // ZB
    zeros = jnp.zeros((SUB, cols), jnp.float32)
    for tile in range(2):
        for z in range(layers):
            for buf in (p_buf, p_two):
                buf[tile, z, :SUB] = zeros
                buf[tile, z, SUB + wide :] = zeros
    def step(t, first, p_buf, w_buf, p_out, w_out, low_row=0, high_row=wide):
        rows = slice(low_row, high_row)
        here = slice(SUB + low_row, SUB + high_row)
        ahead = slice(SUB + low_row + 1, SUB + high_row + 1)
        back_rows = slice(SUB + low_row - 1, SUB + high_row - 1)
        lane = lanes_of((ZB, high_row - low_row, cols))
        last_lane = lane == cols - 1
        first_lane = lane == 0
        zero_layer = jnp.zeros((1, high_row - low_row, cols), jnp.float32)
        before_step(t, p_buf)

        def stage_a(g):
            zs = slice(g * ZB, (g + 1) * ZB)
            return [pltpu.roll(p_buf[i, zs, here], cols - 1, 2) for i in range(2)]

        def stage_b(g, turned):
            zs = slice(g * ZB, (g + 1) * ZB)
            right = [
                jnp.where(last_lane, turned[1], turned[0]),
                jnp.where(last_lane, 0.0, turned[1]),
            ]
            gy = [wet_buf[i, zs, here] * (right[i] - p_buf[i, zs, here]) for i in range(2)]
            return gy, [pltpu.roll(gy[i], 1, 2) for i in range(2)]

        hz_last = [None, None]
        surface = [None, None]

        def stage_c(g, gy, back):
            zs = slice(g * ZB, (g + 1) * ZB)
            before = [
                jnp.where(first_lane, 0.0, back[0]),
                jnp.where(first_lane, back[0], back[1]),
            ]
            for i in range(2):
                p = p_buf[i, zs, here]
                w = w_buf[i, zs, rows] - (gy[i] - before[i])
                gx = wet_buf[i, zs, here] * (p_buf[i, zs, ahead] - p)
                behind = wet_buf[i, zs, back_rows] * (p - p_buf[i, zs, back_rows])
                w = w - (gx - behind)
                w_out[i, zs, rows] = w
                if g + 1 < groups:
                    hz = half_buf[i, zs, rows] * (p_buf[i, g * ZB + 1 : (g + 1) * ZB + 1, here] - p)
                elif ZB > 1:
                    hz = jnp.concatenate([half_buf[i, g * ZB :, rows] * (p[1:] - p[:-1]), zero_layer], 0)
                else:
                    hz = zero_layer
                prev = zero_layer if g == 0 else hz_last[i]
                flux = w - (hz - (jnp.concatenate([prev, hz[:-1]], 0) if ZB > 1 else prev))
                hz_last[i] = hz[-1:]
                old = wet_buf[i, zs, here] * p if first else p
                new = old - scale_buf[i, zs, rows] * flux
                p_out[i, zs, here] = new
                for k in range(ZB):
                    part = new[k]
                    z = g * ZB + k
                    surface[i] = part if z == 0 else jnp.where(d_buf[i, rows] > float(z), part, surface[i])

        turned = [stage_a(0), stage_a(1)]
        ready = stage_b(0, turned[0])
        for g in range(groups):
            if g + 2 < groups:
                turned.append(stage_a(g + 2))
            coming = stage_b(g + 1, turned[g + 1]) if g + 1 < groups else None
            stage_c(g, *ready)
            ready = coming
        for i in range(2):
            after_step(t, i, surface[i])

    def two(k, carry):
        step(2 * k, False, p_buf, w_buf, p_two, w_two)
        step(2 * k + 1, False, p_two, w_two, p_buf, w_buf)
        return carry

    step(0, True, p_buf, w_buf, p_two, w_two)
    step(1, False, p_two, w_two, p_buf, w_buf)
    lax.fori_loop(1, STEPS // 2 - 1, two, 0)
    step(STEPS - 2, False, p_buf, w_buf, p_two, w_two)
    step(STEPS - 1, False, p_two, w_two, p_buf, w_buf, low_row, high_row or wide)


def state_buffers(layers, wide, cols):
    return [
        VMEM(shape, jnp.float32)
        for shape in (
            (2, layers, wide + 2 * SUB, cols),
            (2, layers, wide, cols),
            (2, wide, cols),
            (2, layers, wide + SUB, cols),
            (2, layers, wide, cols),
            (2, layers - 1, wide, cols),
            (2, layers, wide + 2 * SUB, cols),
            (2, layers, wide, cols),
        )
    ]


def inner_kernel(keep_ref, other_ref, p_keep_ref, p_send_ref, trace_ref, border_ref, *state):
    layers, inner_rows, cols = p_keep_ref.shape
    core = lax.axis_index("cross")
    low = core == 0
    span = inner_rows + 2 * SUB
    base = 2 * span * layers
    p_buf, w_buf, d_buf, wet_buf, scale_buf, half_buf, p_two, w_two = state
    lane = lanes_of((span, cols))
    at = base + 2 * span
    seam = jnp.where(low, keep_ref[at : at + span], other_ref[at : at + span])
    for tile, main_ref, seam_core in ((core, keep_ref, 1), (1 - core, other_ref, 0)):
        seam_lane = lane == jnp.where(core == seam_core, 0, -1)
        masks(
            main_ref[base : base + span],
            main_ref[base + span : base + 2 * span],
            d_buf, wet_buf, scale_buf, half_buf, tile,
        )
        for z in range(layers):
            at = 2 * span * z
            p_buf[tile, z, SUB : SUB + span] = main_ref[at : at + span]
            turned = pltpu.roll(seam, cols - z, 1) if z else seam
            w_buf[tile, z] = main_ref[at + span : at + 2 * span] - jnp.where(seam_lane, turned, 0.0)

    def before_step(t, p_now):
        for i in range(2):
            for z in range(layers):
                first, second = 2 * SUB, span - 1
                border_ref[t, i, z : z + 1] = jnp.where(
                    low, p_now[i, z, first : first + 1], p_now[i, z, second : second + 1]
                )

    def after_step(t, i, surface):
        trace_ref[t, i] = surface if surface.shape[0] == inner_rows else surface[SUB : SUB + inner_rows]

    advance(state, before_step, after_step, 4, SUB, SUB + inner_rows)
    for z in range(layers):
        p_keep_ref[z] = p_buf[core, z, 2 * SUB : 2 * SUB + inner_rows]
        p_send_ref[z] = p_buf[1 - core, z, 2 * SUB : 2 * SUB + inner_rows]


def outer_kernel(
    keep_ref, other_ref, halo_ref, place_ref, inner_ref, border_ref,
    p_keep_ref, p_send_ref, panel_keep_ref, panel_send_ref, panel_rest_ref, trace, *state,
):
    layers, cols = p_keep_ref.shape[0], p_keep_ref.shape[2]
    inner_rows = inner_ref.shape[2]
    core = lax.axis_index("cross")
    low = core == 0
    span = inner_rows + 2 * SUB
    near = SUB
    base = 2 * span * layers
    base_z = 2 * SUB * layers
    ends = halo_ref.shape[0] // 2
    p_buf, w_buf, d_buf, wet_buf, scale_buf, half_buf, p_two, w_two = state
    lane = lanes_of((SUB, cols))
    row = rows_of((SUB, cols))
    offset = (span - near) * core

    def main_rows(ref, at):
        return ref[pl.ds(pl.multiple_of(at + offset, SUB), near)]

    def joined(main, halo):
        return jnp.where(
            low, jnp.concatenate([halo, main], 0), jnp.concatenate([main, halo], 0)
        )

    seam_at = base_z + 2 * SUB
    seam_halo = jnp.where(
        low, halo_ref[seam_at : seam_at + SUB], halo_ref[ends + seam_at : ends + seam_at + SUB]
    )
    seam_main = jnp.where(
        low, main_rows(keep_ref, base + 2 * span), main_rows(other_ref, base + 2 * span)
    )
    seam = joined(seam_main, seam_halo)
    top_row = row == jnp.where(low, 0, -1)
    end_row = row == jnp.where(low, -1, 0)
    wide_lane = lanes_of((near + SUB, cols))
    for tile, main_ref, end, seam_core in ((core, keep_ref, 0, 1), (1 - core, other_ref, ends, 0)):
        seam_lane = wide_lane == jnp.where(core == seam_core, 0, -1)

        def end_rows(at):
            return halo_ref[end + at : end + at + SUB]

        masks(
            joined(main_rows(main_ref, base), end_rows(base_z)),
            joined(main_rows(main_ref, base + span), end_rows(base_z + SUB)),
            d_buf, wet_buf, scale_buf, half_buf, tile,
        )
        for z in range(layers):
            at = 2 * span * z
            at_z = 2 * SUB * z
            p_buf[tile, z, SUB : 2 * SUB + near] = joined(main_rows(main_ref, at), end_rows(at_z))
            w = main_rows(main_ref, at + span)
            w_end = end_rows(at_z + SUB)
            slot = jnp.broadcast_to(w_end[0:1], (SUB, cols))
            final = base + 3 * span + z
            final = jnp.broadcast_to(main_ref[final : final + 1], (SUB, cols))
            w = joined(w - jnp.where(top_row, slot, 0.0), w_end - jnp.where(end_row, final, 0.0))
            turned = pltpu.roll(seam, cols - z, 1) if z else seam
            w_buf[tile, z] = w - jnp.where(seam_lane, turned, 0.0)
        for z in range(layers):
            first, second = base + SUB, base + span - SUB - 1
            depth = jnp.where(
                low, main_ref[first : first + 1], main_ref[second : second + 1]
            )
            wet_buf[tile, z, SUB - 1 : SUB] = jnp.where(depth > float(z), 1.0, 0.0)

    def before_step(t, p_now):
        for i in range(2):
            for z in range(layers):
                value = border_ref[t, i, z : z + 1]
                p_now[i, z, SUB - 1 : SUB] = value
                p_now[i, z, 2 * SUB + near : 2 * SUB + near + 1] = value

    def after_step(t, i, surface):
        trace[t, i] = jnp.where(low, surface[SUB:], surface[:SUB])

    advance(state, before_step, after_step, 8)
    own = pl.multiple_of(SUB + SUB * (1 - core), SUB)
    for z in range(layers):
        p_keep_ref[z] = p_buf[core, z, pl.ds(own, SUB)]
        p_send_ref[z] = p_buf[1 - core, z, pl.ds(own, SUB)]

    width = cols // 2
    lane_rows = lanes_of((inner_rows + SUB, cols))
    parts = STEPS // 2
    wholes = []
    for j in range(parts):
        pieces = []
        for i in range(2):
            one = jnp.concatenate([trace[2 * j, i], inner_ref[2 * j, i]], 0)
            two = jnp.concatenate([trace[2 * j + 1, i], inner_ref[2 * j + 1, i]], 0)
            pieces.append(jnp.where(lane_rows < width, one, pltpu.roll(two, width, 1)))
            pieces.append(jnp.where(lane_rows < width, pltpu.roll(one, width, 1), two))
        wholes.append(jnp.concatenate(pieces, 0))
    both = jnp.concatenate(wholes, 1)
    part_a = both.astype(jnp.bfloat16)
    rest = both - part_a.astype(jnp.float32)
    part_b = rest.astype(jnp.bfloat16)
    part_c = (rest - part_b.astype(jnp.float32)).astype(jnp.bfloat16)
    total = jnp.dot(
        jnp.concatenate([place_ref[...]] * 3, 1),
        jnp.concatenate([part_a, part_b, part_c], 0),
        preferred_element_type=jnp.float32,
    )
    for j in range(parts):
        piece = total[:, j * cols : (j + 1) * cols]
        at = 0
        for ref in (panel_keep_ref, panel_send_ref, panel_rest_ref):
            count = ref.shape[0] // parts
            ref[pl.ds(j, count, stride=parts)] = piece[at : at + count]
            at += count


def shards(
    pressure_start, along_start, cross_start, depth_layers, stiffness, patch_lists, owner_map
):
    sensors, layers, rows, cols = pressure_start.shape
    f32 = jnp.float32
    along_count = lax.axis_size("along")
    cross_count = lax.axis_size("cross")
    low = lax.axis_index("cross") == 0
    swap = [(0, 1), (1, 0)]
    pair = ("along", "cross")
    steps_up = range(along_count - 1)
    route = [(2 * i, 2 * i + 2) for i in steps_up] + [(2 * i + 3, 2 * i + 1) for i in steps_up]
    half_rows = rows // 2
    span = half_rows + SUB
    pack_rows = 2 * span * layers + 3 * span + layers
    end_rows = 2 * SUB * layers + 3 * SUB

    spec = pl.BlockSpec(memory_space=VMEM)
    hbm = pl.BlockSpec(memory_space=pltpu.HBM)
    params = pltpu.CompilerParams(vmem_limit_bytes=32 * 1024 * 1024)
    keep, send, one, two, ids, owners = pl.pallas_call(
        edges_kernel,
        out_shape=[
            jax.ShapeDtypeStruct((pack_rows, cols), f32),
            jax.ShapeDtypeStruct((pack_rows + SUB, cols), f32),
            jax.ShapeDtypeStruct((end_rows, cols), f32),
            jax.ShapeDtypeStruct((end_rows, cols), f32),
            jax.ShapeDtypeStruct(patch_lists.shape, jnp.int32),
            jax.ShapeDtypeStruct((SUB, cols), f32),
        ],
        in_specs=[hbm] * 7,
        out_specs=[spec] * 6,
        scratch_shapes=[
            VMEM((layers, rows, cols), f32),
            VMEM((layers, rows, cols), f32),
            VMEM((layers, rows, cols), f32),
            VMEM((rows, cols), jnp.int32),
            VMEM((rows, cols), f32),
            VMEM(owner_map.shape, jnp.int32),
            pltpu.SemaphoreType.DMA((7,)),
        ],
        compiler_params=params,
        name="edges",
    )(
        *(
            pltpu.with_memory_space_constraint(x, pltpu.HBM)
            for x in (
                pressure_start[0],
                along_start[0],
                cross_start[0],
                depth_layers,
                stiffness,
                owner_map,
                patch_lists,
            )
        )
    )

    two = lax.ppermute(two, "cross", swap)
    halo = jnp.concatenate([one, two], 0)
    send = lax.optimization_barrier((send, two))[0]
    other = lax.ppermute(send, "cross", swap)
    halo = lax.ppermute(halo, pair, route)

    patch_count = 2 * rows
    owner_count = along_count * cross_count
    capacity = patch_count // owner_count + 1
    count = owner_count * capacity
    place = pl.pallas_call(
        functools.partial(
            place_kernel, owner_count=owner_count, chips=along_count, capacity=capacity
        ),
        out_shape=jax.ShapeDtypeStruct((2 * count, patch_count), jnp.bfloat16),
        in_specs=[spec] * 3,
        out_specs=spec,
        compiler_params=params,
        name="place",
    )(ids.reshape(-1, patch_count).T, owners, other)

    parts = STEPS // 2
    inner_rows = half_rows - SUB
    inner_shape = jax.ShapeDtypeStruct((layers, inner_rows, cols), f32)
    inner_keep, inner_send, inner_trace, border = pl.pallas_call(
        inner_kernel,
        out_shape=[
            inner_shape,
            inner_shape,
            jax.ShapeDtypeStruct((STEPS, 2, inner_rows, cols), f32),
            jax.ShapeDtypeStruct((STEPS, 2, layers, cols), f32),
        ],
        in_specs=[spec] * 2,
        out_specs=[spec] * 4,
        scratch_shapes=state_buffers(layers, span, cols),
        compiler_params=params,
        cost_estimate=pl.CostEstimate(
            flops=400 * layers * span * cols,
            bytes_accessed=200 * layers * span * cols,
            transcendentals=0,
        ),
        name="inner",
    )(keep, other)
    outer_shape = jax.ShapeDtypeStruct((layers, SUB, cols), f32)
    some = 2 * capacity * parts
    outer_keep, outer_send, panel_keep, panel_send, panel_rest = pl.pallas_call(
        outer_kernel,
        out_shape=[outer_shape, outer_shape]
        + [
            jax.ShapeDtypeStruct((number, cols), f32)
            for number in (along_count * some, some, (along_count - 1) * some)
        ],
        in_specs=[spec] * 6,
        out_specs=[spec] * 5,
        scratch_shapes=[VMEM((STEPS, 2, SUB, cols), f32)] + state_buffers(layers, 2 * SUB, cols),
        compiler_params=params,
        name="outer",
    )(keep, other, halo, place, inner_trace, border)

    panel_first = panel_keep[:some] + lax.ppermute(panel_send, "cross", swap)
    rest_other = lax.ppermute(panel_rest, "cross", swap)
    panel_rest = panel_keep[some:] + rest_other
    if along_count == 4:
        pieces = [panel_rest[2 * some :]]
        for k in range(1, along_count):
            piece = panel_first if k == 1 else panel_rest[(k - 2) * some : (k - 1) * some]
            route = [(i, (i + k) % along_count) for i in range(along_count)]
            pieces.append(lax.ppermute(piece, "along", route))
        received = pl.pallas_call(
            gather_kernel,
            out_shape=jax.ShapeDtypeStruct((count * parts, cols), f32),
            in_specs=[spec] * 4,
            out_specs=hbm,
            scratch_shapes=[pltpu.SemaphoreType.DMA((4,))],
            compiler_params=params,
            name="gather",
        )(*pieces)
    else:
        panels = jnp.concatenate([panel_first, panel_rest], 0).reshape(along_count, some, cols)
        received = lax.all_to_all(panels, "along", split_axis=0, concat_axis=0, tiled=True)
    received = received.reshape(1, count, 1, parts * cols)

    inner_other = lax.ppermute(inner_send, "cross", swap)
    outer_other = lax.ppermute(outer_send, "cross", swap)
    pressure = jnp.where(
        low,
        jnp.concatenate([outer_keep, inner_keep, inner_other, outer_other], 1),
        jnp.concatenate([outer_other, inner_other, inner_keep, outer_keep], 1),
    )
    return (pressure[None], received)


def solution(mesh):
    in_specs = (
        P("batch", None, "along", "cross"),
        P("batch", None, "along", "cross"),
        P("batch", None, "along", "cross"),
        P("along", "cross"),
        P("along", "cross"),
        P("batch", None),
        P(("along", "cross"), None),
    )
    out_specs = (P("batch", None, "along", "cross"), P(("along", "cross"), None, "batch", None))
    return jax.shard_map(shards, mesh=mesh, in_specs=in_specs, out_specs=out_specs, check_vma=False)
```

```python
import functools

import jax
import jax.numpy as jnp
from jax import lax
from jax.experimental import pallas as pl
from jax.experimental.pallas import tpu as pltpu
from jax.sharding import PartitionSpec as P

STEPS = 8
SUB = 8
VMEM = pltpu.VMEM


def lanes_of(shape):
    return lax.broadcasted_iota(jnp.int32, shape, len(shape) - 1)


def rows_of(shape):
    return lax.broadcasted_iota(jnp.int32, shape, len(shape) - 2)


def edges_kernel(
    p_hbm, fa_hbm, fc_hbm, depth_hbm, stiff_hbm, owner_hbm, ids_hbm,
    keep_ref, send_ref, one_ref, two_ref, ids_ref, owners_ref,
    p_ref, fa_ref, fc_ref, depth_ref, stiff_ref, owner_ref, sems,
):
    layers, rows, cols = p_ref.shape
    half = layers // 2
    pairs = []
    for part in (slice(0, half), slice(half, layers)):
        for source, target in ((fa_hbm, fa_ref), (fc_hbm, fc_ref), (p_hbm, p_ref)):
            pairs.append((source.at[part], target.at[part]))
        if not part.start:
            pairs += [
                (depth_hbm, depth_ref), (stiff_hbm, stiff_ref), (owner_hbm, owner_ref), (ids_hbm, ids_ref)
            ]
    copies = [
        pltpu.make_async_copy(source, target, sems.at[i]) for i, (source, target) in enumerate(pairs)
    ]
    for copy in copies:
        copy.start()
    for copy in copies[:7]:
        copy.wait()
    low = lax.axis_index("cross") == 0
    span = rows // 2 + SUB
    last = rows - SUB
    lane = lanes_of((rows, cols))
    row = rows_of((rows, cols))
    row_sub = rows_of((SUB, cols))
    depth = depth_ref[...]
    stiff = stiff_ref[...]
    first_lane = lane == 0
    slot_one = row_sub == jnp.where(low, 0, -1)
    slot_two = row_sub == jnp.where(low, -1, 0)
    base = 2 * span * layers
    base_z = 2 * SUB * layers
    velocity = jnp.zeros((rows, cols), jnp.float32)

    def halves(array):
        first, second = array[:span], array[rows - span :]
        return jnp.where(low, first, second), jnp.where(low, second, first)

    def ends(array):
        first, second = array[:SUB], array[last:]
        return jnp.where(low, second, first), jnp.where(low, first, second)

    for z in range(layers):
        if z == half:
            for copy in copies[7:]:
                copy.wait()
        wet = depth > z
        p = p_ref[z]
        va = jnp.where(wet, fa_ref[z], 0.0)
        vc = jnp.where(wet, fc_ref[z], 0.0)
        behind = jnp.where(row == 0, 0.0, pltpu.roll(va, 1, 0))
        before = jnp.where(first_lane, 0.0, pltpu.roll(vc, 1, 1))
        w = (va - behind) + (vc - before)
        velocity = jnp.where(lane == z, pltpu.roll(vc, z + 1, 1), velocity)
        at = 2 * span * z
        keep_ref[at : at + span], send_ref[at : at + span] = halves(p)
        at += span
        keep_ref[at : at + span], send_ref[at : at + span] = halves(w)
        final = va[rows - 1 : rows]
        at = base + 3 * span + z
        keep_ref[at : at + 1] = final
        send_ref[at : at + 1] = final
        at = 2 * SUB * z
        one_ref[at : at + SUB], two_ref[at : at + SUB] = ends(p)
        at += SUB
        one, two = ends(w)
        final = jnp.broadcast_to(final, (SUB, cols))
        one_ref[at : at + SUB] = jnp.where(slot_one, final, one)
        two_ref[at : at + SUB] = jnp.where(slot_two, final, two)
    for i, array in enumerate((depth.astype(jnp.float32), stiff, velocity)):
        at = base + span * i
        keep_ref[at : at + span], send_ref[at : at + span] = halves(array)
        at = base_z + SUB * i
        one_ref[at : at + SUB], two_ref[at : at + SUB] = ends(array)
    at = base + 3 * span + layers
    owners = jnp.broadcast_to(owner_ref[...].astype(jnp.float32), (SUB, cols))
    owners_ref[...] = owners
    send_ref[at : at + SUB] = owners


def place_kernel(ids_ref, own_ref, other_ref, place_ref, *, owner_count, chips, capacity):
    along = lax.axis_index("along")
    cross = lax.axis_index("cross")
    low = cross == 0
    cores = owner_count // chips
    patches = own_ref.shape[1]
    last = other_ref.shape[0] - SUB
    own = own_ref[0:1]
    other = other_ref[last : last + 1]
    owners = [jnp.where(low, own, other), jnp.where(low, other, own)]
    lane = lanes_of((patches, patches))
    half = patches // 2
    block = lane // half
    within = lane % half
    held = half // 2
    turn = (held - SUB) * cross
    patch = half * cross + 2 * lax.rem(within % held + turn, held) + within // held
    source = rows_of((patches, patches))
    number = rows_of((owner_count, patches)).astype(jnp.float32)
    chosen = jnp.zeros((owner_count, patches), jnp.float32)
    counts = jnp.zeros((owner_count, patches), jnp.float32)
    for i in range(2):
        owned = (number == owners[i]).astype(jnp.bfloat16)
        pick = jnp.where(block == i, jnp.where(source == patch, 1.0, 0.0), 0.0).astype(jnp.bfloat16)
        earlier = jnp.where(block == i, jnp.where(source < patch, 1.0, 0.0), 0.0).astype(jnp.bfloat16)
        chosen += jnp.dot(owned, pick, preferred_element_type=jnp.float32)
        counts += jnp.dot(owned, earlier, preferred_element_type=jnp.float32)
    rank = jnp.sum(chosen * counts, axis=0, keepdims=True).astype(jnp.int32)
    owner = jnp.sum(chosen * number, axis=0, keepdims=True).astype(jnp.int32)
    wanted = (along * cores + block) * patches + patch
    found = jnp.zeros((patches, patches), jnp.float32)
    for j in range(ids_ref.shape[1]):
        found = jnp.where(ids_ref[:, j : j + 1] == wanted, 1.0, found)
    member = jnp.sum(found, axis=0, keepdims=True)
    block = block[:1]
    chip = owner // cores
    owner_core = owner % cores
    some = 2 * capacity
    slot = block * capacity + rank
    if chips == 4:
        slot = slot + lax.rem(chip - along + 2 * chips - 1, chips) * some
    else:
        slot = slot + chip * some
    handler = owner_core
    slot = jnp.where(handler == cross, slot, slot + chips * some)
    slot = jnp.where(member > 0.0, slot, -1)
    place_ref[...] = jnp.where(rows_of(place_ref.shape) == slot, 1.0, 0.0).astype(jnp.bfloat16)


def gather_kernel(own_ref, one_ref, two_ref, three_ref, out_ref, sems):
    chips = 4
    along = lax.axis_index("along")
    count = out_ref.shape[0] // chips
    copies = []
    for i, (ref, ahead) in enumerate(
        ((own_ref, 0), (one_ref, 3), (two_ref, 2), (three_ref, 1))
    ):
        at = pl.multiple_of(lax.rem(along + ahead, chips) * count, SUB)
        copies.append(pltpu.make_async_copy(ref, out_ref.at[pl.ds(at, count)], sems.at[i]))
    for copy in copies:
        copy.start()
    for copy in copies:
        copy.wait()


def masks(depth, stiff, d_buf, wet_buf, scale_buf, half_buf, tile):
    layers = wet_buf.shape[1]
    zeros = jnp.zeros((SUB, depth.shape[1]), jnp.float32)
    d_buf[tile] = depth
    for z in range(layers):
        wet = depth > float(z)
        wet_buf[tile, z, :SUB] = zeros
        wet_buf[tile, z, SUB:] = jnp.where(wet, 1.0, 0.0)
        scale_buf[tile, z] = jnp.where(wet, stiff, 0.0)
        if z > 0:
            half_buf[tile, z - 1] = jnp.where(wet, 0.5, 0.0)


def advance(state, before_step, after_step, ZB, low_row=0, high_row=None):
    p_buf, w_buf, d_buf, wet_buf, scale_buf, half_buf, p_two, w_two = state
    layers = p_buf.shape[1]
    wide, cols = w_buf.shape[2:]
    groups = layers // ZB
    zeros = jnp.zeros((SUB, cols), jnp.float32)
    for tile in range(2):
        for z in range(layers):
            for buf in (p_buf, p_two):
                buf[tile, z, :SUB] = zeros
                buf[tile, z, SUB + wide :] = zeros
    def step(t, first, p_buf, w_buf, p_out, w_out, low_row=0, high_row=wide):
        rows = slice(low_row, high_row)
        here = slice(SUB + low_row, SUB + high_row)
        ahead = slice(SUB + low_row + 1, SUB + high_row + 1)
        back_rows = slice(SUB + low_row - 1, SUB + high_row - 1)
        lane = lanes_of((ZB, high_row - low_row, cols))
        last_lane = lane == cols - 1
        first_lane = lane == 0
        zero_layer = jnp.zeros((1, high_row - low_row, cols), jnp.float32)
        before_step(t, p_buf)

        def stage_a(g):
            zs = slice(g * ZB, (g + 1) * ZB)
            return [pltpu.roll(p_buf[i, zs, here], cols - 1, 2) for i in range(2)]

        def stage_b(g, turned):
            zs = slice(g * ZB, (g + 1) * ZB)
            right = [
                jnp.where(last_lane, turned[1], turned[0]),
                jnp.where(last_lane, 0.0, turned[1]),
            ]
            gy = [wet_buf[i, zs, here] * (right[i] - p_buf[i, zs, here]) for i in range(2)]
            return gy, [pltpu.roll(gy[i], 1, 2) for i in range(2)]

        hz_last = [None, None]
        surface = [None, None]

        def stage_c(g, gy, back):
            zs = slice(g * ZB, (g + 1) * ZB)
            before = [
                jnp.where(first_lane, 0.0, back[0]),
                jnp.where(first_lane, back[0], back[1]),
            ]
            for i in range(2):
                p = p_buf[i, zs, here]
                w = w_buf[i, zs, rows] - (gy[i] - before[i])
                gx = wet_buf[i, zs, here] * (p_buf[i, zs, ahead] - p)
                behind = wet_buf[i, zs, back_rows] * (p - p_buf[i, zs, back_rows])
                w = w - (gx - behind)
                w_out[i, zs, rows] = w
                if g + 1 < groups:
                    hz = half_buf[i, zs, rows] * (p_buf[i, g * ZB + 1 : (g + 1) * ZB + 1, here] - p)
                elif ZB > 1:
                    hz = jnp.concatenate([half_buf[i, g * ZB :, rows] * (p[1:] - p[:-1]), zero_layer], 0)
                else:
                    hz = zero_layer
                prev = zero_layer if g == 0 else hz_last[i]
                flux = w - (hz - (jnp.concatenate([prev, hz[:-1]], 0) if ZB > 1 else prev))
                hz_last[i] = hz[-1:]
                old = wet_buf[i, zs, here] * p if first else p
                new = old - scale_buf[i, zs, rows] * flux
                p_out[i, zs, here] = new
                for k in range(ZB):
                    part = new[k]
                    z = g * ZB + k
                    surface[i] = part if z == 0 else jnp.where(d_buf[i, rows] > float(z), part, surface[i])

        turned = [stage_a(0), stage_a(1)]
        ready = stage_b(0, turned[0])
        for g in range(groups):
            if g + 2 < groups:
                turned.append(stage_a(g + 2))
            coming = stage_b(g + 1, turned[g + 1]) if g + 1 < groups else None
            stage_c(g, *ready)
            ready = coming
        for i in range(2):
            after_step(t, i, surface[i])

    def two(k, carry):
        step(2 * k, False, p_buf, w_buf, p_two, w_two)
        step(2 * k + 1, False, p_two, w_two, p_buf, w_buf)
        return carry

    step(0, True, p_buf, w_buf, p_two, w_two)
    step(1, False, p_two, w_two, p_buf, w_buf)
    lax.fori_loop(1, STEPS // 2 - 1, two, 0)
    step(STEPS - 2, False, p_buf, w_buf, p_two, w_two)
    step(STEPS - 1, False, p_two, w_two, p_buf, w_buf, low_row, high_row or wide)


def state_buffers(layers, wide, cols):
    return [
        VMEM(shape, jnp.float32)
        for shape in (
            (2, layers, wide + 2 * SUB, cols),
            (2, layers, wide, cols),
            (2, wide, cols),
            (2, layers, wide + SUB, cols),
            (2, layers, wide, cols),
            (2, layers - 1, wide, cols),
            (2, layers, wide + 2 * SUB, cols),
            (2, layers, wide, cols),
        )
    ]


def inner_kernel(keep_ref, other_ref, p_keep_ref, p_send_ref, trace_ref, border_ref, *state):
    layers, inner_rows, cols = p_keep_ref.shape
    core = lax.axis_index("cross")
    low = core == 0
    span = inner_rows + 2 * SUB
    base = 2 * span * layers
    p_buf, w_buf, d_buf, wet_buf, scale_buf, half_buf, p_two, w_two = state
    lane = lanes_of((span, cols))
    at = base + 2 * span
    seam = jnp.where(low, keep_ref[at : at + span], other_ref[at : at + span])
    for tile, main_ref, seam_core in ((core, keep_ref, 1), (1 - core, other_ref, 0)):
        seam_lane = lane == jnp.where(core == seam_core, 0, -1)
        masks(
            main_ref[base : base + span],
            main_ref[base + span : base + 2 * span],
            d_buf, wet_buf, scale_buf, half_buf, tile,
        )
        for z in range(layers):
            at = 2 * span * z
            p_buf[tile, z, SUB : SUB + span] = main_ref[at : at + span]
            turned = pltpu.roll(seam, cols - z, 1) if z else seam
            w_buf[tile, z] = main_ref[at + span : at + 2 * span] - jnp.where(seam_lane, turned, 0.0)

    def before_step(t, p_now):
        for i in range(2):
            for z in range(layers):
                first, second = 2 * SUB, span - 1
                border_ref[t, i, z : z + 1] = jnp.where(
                    low, p_now[i, z, first : first + 1], p_now[i, z, second : second + 1]
                )

    def after_step(t, i, surface):
        trace_ref[t, i] = surface if surface.shape[0] == inner_rows else surface[SUB : SUB + inner_rows]

    advance(state, before_step, after_step, 4, SUB, SUB + inner_rows)
    for z in range(layers):
        p_keep_ref[z] = p_buf[core, z, 2 * SUB : 2 * SUB + inner_rows]
        p_send_ref[z] = p_buf[1 - core, z, 2 * SUB : 2 * SUB + inner_rows]


def outer_kernel(
    keep_ref, other_ref, halo_ref, place_ref, inner_ref, border_ref,
    p_keep_ref, p_send_ref, panel_keep_ref, panel_send_ref, panel_rest_ref, trace, *state,
):
    layers, cols = p_keep_ref.shape[0], p_keep_ref.shape[2]
    inner_rows = inner_ref.shape[2]
    core = lax.axis_index("cross")
    low = core == 0
    span = inner_rows + 2 * SUB
    near = SUB
    base = 2 * span * layers
    base_z = 2 * SUB * layers
    ends = halo_ref.shape[0] // 2
    p_buf, w_buf, d_buf, wet_buf, scale_buf, half_buf, p_two, w_two = state
    lane = lanes_of((SUB, cols))
    row = rows_of((SUB, cols))
    offset = (span - near) * core

    def main_rows(ref, at):
        return ref[pl.ds(pl.multiple_of(at + offset, SUB), near)]

    def joined(main, halo):
        return jnp.where(
            low, jnp.concatenate([halo, main], 0), jnp.concatenate([main, halo], 0)
        )

    seam_at = base_z + 2 * SUB
    seam_halo = jnp.where(
        low, halo_ref[seam_at : seam_at + SUB], halo_ref[ends + seam_at : ends + seam_at + SUB]
    )
    seam_main = jnp.where(
        low, main_rows(keep_ref, base + 2 * span), main_rows(other_ref, base + 2 * span)
    )
    seam = joined(seam_main, seam_halo)
    top_row = row == jnp.where(low, 0, -1)
    end_row = row == jnp.where(low, -1, 0)
    wide_lane = lanes_of((near + SUB, cols))
    for tile, main_ref, end, seam_core in ((core, keep_ref, 0, 1), (1 - core, other_ref, ends, 0)):
        seam_lane = wide_lane == jnp.where(core == seam_core, 0, -1)

        def end_rows(at):
            return halo_ref[end + at : end + at + SUB]

        masks(
            joined(main_rows(main_ref, base), end_rows(base_z)),
            joined(main_rows(main_ref, base + span), end_rows(base_z + SUB)),
            d_buf, wet_buf, scale_buf, half_buf, tile,
        )
        for z in range(layers):
            at = 2 * span * z
            at_z = 2 * SUB * z
            p_buf[tile, z, SUB : 2 * SUB + near] = joined(main_rows(main_ref, at), end_rows(at_z))
            w = main_rows(main_ref, at + span)
            w_end = end_rows(at_z + SUB)
            slot = jnp.broadcast_to(w_end[0:1], (SUB, cols))
            final = base + 3 * span + z
            final = jnp.broadcast_to(main_ref[final : final + 1], (SUB, cols))
            w = joined(w - jnp.where(top_row, slot, 0.0), w_end - jnp.where(end_row, final, 0.0))
            turned = pltpu.roll(seam, cols - z, 1) if z else seam
            w_buf[tile, z] = w - jnp.where(seam_lane, turned, 0.0)
        for z in range(layers):
            first, second = base + SUB, base + span - SUB - 1
            depth = jnp.where(
                low, main_ref[first : first + 1], main_ref[second : second + 1]
            )
            wet_buf[tile, z, SUB - 1 : SUB] = jnp.where(depth > float(z), 1.0, 0.0)

    def before_step(t, p_now):
        for i in range(2):
            for z in range(layers):
                value = border_ref[t, i, z : z + 1]
                p_now[i, z, SUB - 1 : SUB] = value
                p_now[i, z, 2 * SUB + near : 2 * SUB + near + 1] = value

    def after_step(t, i, surface):
        trace[t, i] = jnp.where(low, surface[SUB:], surface[:SUB])

    advance(state, before_step, after_step, 8)
    own = pl.multiple_of(SUB + SUB * (1 - core), SUB)
    for z in range(layers):
        p_keep_ref[z] = p_buf[core, z, pl.ds(own, SUB)]
        p_send_ref[z] = p_buf[1 - core, z, pl.ds(own, SUB)]

    width = cols // 2
    lane_rows = lanes_of((inner_rows + SUB, cols))
    parts = STEPS // 2
    wholes = []
    for j in range(parts):
        pieces = []
        for i in range(2):
            one = jnp.concatenate([trace[2 * j, i], inner_ref[2 * j, i]], 0)
            two = jnp.concatenate([trace[2 * j + 1, i], inner_ref[2 * j + 1, i]], 0)
            pieces.append(jnp.where(lane_rows < width, one, pltpu.roll(two, width, 1)))
            pieces.append(jnp.where(lane_rows < width, pltpu.roll(one, width, 1), two))
        wholes.append(jnp.concatenate(pieces, 0))
    both = jnp.concatenate(wholes, 1)
    part_a = both.astype(jnp.bfloat16)
    rest = both - part_a.astype(jnp.float32)
    part_b = rest.astype(jnp.bfloat16)
    part_c = (rest - part_b.astype(jnp.float32)).astype(jnp.bfloat16)
    total = jnp.dot(
        jnp.concatenate([place_ref[...]] * 3, 1),
        jnp.concatenate([part_a, part_b, part_c], 0),
        preferred_element_type=jnp.float32,
    )
    for j in range(parts):
        piece = total[:, j * cols : (j + 1) * cols]
        at = 0
        for ref in (panel_keep_ref, panel_send_ref, panel_rest_ref):
            count = ref.shape[0] // parts
            ref[pl.ds(j, count, stride=parts)] = piece[at : at + count]
            at += count


def shards(
    pressure_start, along_start, cross_start, depth_layers, stiffness, patch_lists, owner_map
):
    sensors, layers, rows, cols = pressure_start.shape
    f32 = jnp.float32
    along_count = lax.axis_size("along")
    cross_count = lax.axis_size("cross")
    low = lax.axis_index("cross") == 0
    swap = [(0, 1), (1, 0)]
    pair = ("along", "cross")
    steps_up = range(along_count - 1)
    route = [(2 * i, 2 * i + 2) for i in steps_up] + [(2 * i + 3, 2 * i + 1) for i in steps_up]
    half_rows = rows // 2
    span = half_rows + SUB
    pack_rows = 2 * span * layers + 3 * span + layers
    end_rows = 2 * SUB * layers + 3 * SUB

    spec = pl.BlockSpec(memory_space=VMEM)
    hbm = pl.BlockSpec(memory_space=pltpu.HBM)
    params = pltpu.CompilerParams(vmem_limit_bytes=32 * 1024 * 1024)
    keep, send, one, two, ids, owners = pl.pallas_call(
        edges_kernel,
        out_shape=[
            jax.ShapeDtypeStruct((pack_rows, cols), f32),
            jax.ShapeDtypeStruct((pack_rows + SUB, cols), f32),
            jax.ShapeDtypeStruct((end_rows, cols), f32),
            jax.ShapeDtypeStruct((end_rows, cols), f32),
            jax.ShapeDtypeStruct(patch_lists.shape, jnp.int32),
            jax.ShapeDtypeStruct((SUB, cols), f32),
        ],
        in_specs=[hbm] * 7,
        out_specs=[spec] * 6,
        scratch_shapes=[
            VMEM((layers, rows, cols), f32),
            VMEM((layers, rows, cols), f32),
            VMEM((layers, rows, cols), f32),
            VMEM((rows, cols), jnp.int32),
            VMEM((rows, cols), f32),
            VMEM(owner_map.shape, jnp.int32),
            pltpu.SemaphoreType.DMA((10,)),
        ],
        compiler_params=params,
        name="edges",
    )(
        *(
            pltpu.with_memory_space_constraint(x, pltpu.HBM)
            for x in (
                pressure_start[0],
                along_start[0],
                cross_start[0],
                depth_layers,
                stiffness,
                owner_map,
                patch_lists,
            )
        )
    )

    two = lax.ppermute(two, "cross", swap)
    halo = jnp.concatenate([one, two], 0)
    send = lax.optimization_barrier((send, two))[0]
    other = lax.ppermute(send, "cross", swap)
    halo = lax.ppermute(halo, pair, route)

    patch_count = 2 * rows
    owner_count = along_count * cross_count
    capacity = patch_count // owner_count + 1
    count = owner_count * capacity
    place = pl.pallas_call(
        functools.partial(
            place_kernel, owner_count=owner_count, chips=along_count, capacity=capacity
        ),
        out_shape=jax.ShapeDtypeStruct((2 * count, patch_count), jnp.bfloat16),
        in_specs=[spec] * 3,
        out_specs=spec,
        compiler_params=params,
        name="place",
    )(ids.reshape(-1, patch_count).T, owners, other)

    parts = STEPS // 2
    inner_rows = half_rows - SUB
    inner_shape = jax.ShapeDtypeStruct((layers, inner_rows, cols), f32)
    inner_keep, inner_send, inner_trace, border = pl.pallas_call(
        inner_kernel,
        out_shape=[
            inner_shape,
            inner_shape,
            jax.ShapeDtypeStruct((STEPS, 2, inner_rows, cols), f32),
            jax.ShapeDtypeStruct((STEPS, 2, layers, cols), f32),
        ],
        in_specs=[spec] * 2,
        out_specs=[spec] * 4,
        scratch_shapes=state_buffers(layers, span, cols),
        compiler_params=params,
        cost_estimate=pl.CostEstimate(
            flops=400 * layers * span * cols,
            bytes_accessed=200 * layers * span * cols,
            transcendentals=0,
        ),
        name="inner",
    )(keep, other)
    outer_shape = jax.ShapeDtypeStruct((layers, SUB, cols), f32)
    some = 2 * capacity * parts
    outer_keep, outer_send, panel_keep, panel_send, panel_rest = pl.pallas_call(
        outer_kernel,
        out_shape=[outer_shape, outer_shape]
        + [
            jax.ShapeDtypeStruct((number, cols), f32)
            for number in (along_count * some, some, (along_count - 1) * some)
        ],
        in_specs=[spec] * 6,
        out_specs=[spec] * 5,
        scratch_shapes=[VMEM((STEPS, 2, SUB, cols), f32)] + state_buffers(layers, 2 * SUB, cols),
        compiler_params=params,
        name="outer",
    )(keep, other, halo, place, inner_trace, border)

    panel_first = panel_keep[:some] + lax.ppermute(panel_send, "cross", swap)
    rest_other = lax.ppermute(panel_rest, "cross", swap)
    panel_rest = panel_keep[some:] + rest_other
    if along_count == 4:
        pieces = [panel_rest[2 * some :]]
        for k in range(1, along_count):
            piece = panel_first if k == 1 else panel_rest[(k - 2) * some : (k - 1) * some]
            route = [(i, (i + k) % along_count) for i in range(along_count)]
            pieces.append(lax.ppermute(piece, "along", route))
        received = pl.pallas_call(
            gather_kernel,
            out_shape=jax.ShapeDtypeStruct((count * parts, cols), f32),
            in_specs=[spec] * 4,
            out_specs=hbm,
            scratch_shapes=[pltpu.SemaphoreType.DMA((4,))],
            compiler_params=params,
            name="gather",
        )(*pieces)
    else:
        panels = jnp.concatenate([panel_first, panel_rest], 0).reshape(along_count, some, cols)
        received = lax.all_to_all(panels, "along", split_axis=0, concat_axis=0, tiled=True)
    received = received.reshape(1, count, 1, parts * cols)

    inner_other = lax.ppermute(inner_send, "cross", swap)
    outer_other = lax.ppermute(outer_send, "cross", swap)
    pressure = jnp.where(
        low,
        jnp.concatenate([outer_keep, inner_keep, inner_other, outer_other], 1),
        jnp.concatenate([outer_other, inner_other, inner_keep, outer_keep], 1),
    )
    return (pressure[None], received)


def solution(mesh):
    in_specs = (
        P("batch", None, "along", "cross"),
        P("batch", None, "along", "cross"),
        P("batch", None, "along", "cross"),
        P("along", "cross"),
        P("along", "cross"),
        P("batch", None),
        P(("along", "cross"), None),
    )
    out_specs = (P("batch", None, "along", "cross"), P(("along", "cross"), None, "batch", None))
    return jax.shard_map(shards, mesh=mesh, in_specs=in_specs, out_specs=out_specs, check_vma=False)
```

```python
import functools

import jax
import jax.numpy as jnp
from jax import lax
from jax.experimental import pallas as pl
from jax.experimental.pallas import tpu as pltpu
from jax.sharding import PartitionSpec as P

STEPS = 8
SUB = 8
VMEM = pltpu.VMEM


def lanes_of(shape):
    return lax.broadcasted_iota(jnp.int32, shape, len(shape) - 1)


def rows_of(shape):
    return lax.broadcasted_iota(jnp.int32, shape, len(shape) - 2)


def edges_kernel(
    p_hbm, fa_hbm, fc_hbm, depth_hbm, stiff_hbm, owner_hbm, ids_hbm,
    keep_ref, send_ref, one_ref, two_ref, ids_ref, owners_ref,
    p_ref, fa_ref, fc_ref, depth_ref, stiff_ref, owner_ref, sems,
):
    layers, rows, cols = p_ref.shape
    half = layers // 2
    pairs = []
    for part in (slice(0, half), slice(half, layers)):
        for source, target in ((fa_hbm, fa_ref), (fc_hbm, fc_ref), (p_hbm, p_ref)):
            pairs.append((source.at[part], target.at[part]))
        if not part.start:
            pairs += [
                (depth_hbm, depth_ref), (stiff_hbm, stiff_ref), (owner_hbm, owner_ref), (ids_hbm, ids_ref)
            ]
    copies = [
        pltpu.make_async_copy(source, target, sems.at[i]) for i, (source, target) in enumerate(pairs)
    ]
    for copy in copies:
        copy.start()
    for copy in copies[:7]:
        copy.wait()
    low = lax.axis_index("cross") == 0
    span = rows // 2 + SUB
    last = rows - SUB
    lane = lanes_of((rows, cols))
    row = rows_of((rows, cols))
    row_sub = rows_of((SUB, cols))
    depth = depth_ref[...]
    stiff = stiff_ref[...]
    first_lane = lane == 0
    slot_one = row_sub == jnp.where(low, 0, -1)
    slot_two = row_sub == jnp.where(low, -1, 0)
    base = 2 * span * layers
    base_z = 2 * SUB * layers
    velocity = jnp.zeros((rows, cols), jnp.float32)

    def halves(array):
        first, second = array[:span], array[rows - span :]
        return jnp.where(low, first, second), jnp.where(low, second, first)

    def ends(array):
        first, second = array[:SUB], array[last:]
        return jnp.where(low, second, first), jnp.where(low, first, second)

    for z in range(layers):
        if z == half:
            for copy in copies[7:]:
                copy.wait()
        wet = depth > z
        p = p_ref[z]
        va = jnp.where(wet, fa_ref[z], 0.0)
        vc = jnp.where(wet, fc_ref[z], 0.0)
        behind = jnp.where(row == 0, 0.0, pltpu.roll(va, 1, 0))
        before = jnp.where(first_lane, 0.0, pltpu.roll(vc, 1, 1))
        w = (va - behind) + (vc - before)
        velocity = jnp.where(lane == z, pltpu.roll(vc, z + 1, 1), velocity)
        at = 2 * span * z
        keep_ref[at : at + span], send_ref[at : at + span] = halves(p)
        at += span
        keep_ref[at : at + span], send_ref[at : at + span] = halves(w)
        final = va[rows - 1 : rows]
        at = base + 3 * span + z
        keep_ref[at : at + 1] = final
        send_ref[at : at + 1] = final
        at = 2 * SUB * z
        one_ref[at : at + SUB], two_ref[at : at + SUB] = ends(p)
        at += SUB
        one, two = ends(w)
        final = jnp.broadcast_to(final, (SUB, cols))
        one_ref[at : at + SUB] = jnp.where(slot_one, final, one)
        two_ref[at : at + SUB] = jnp.where(slot_two, final, two)
    for i, array in enumerate((depth.astype(jnp.float32), stiff, velocity)):
        at = base + span * i
        keep_ref[at : at + span], send_ref[at : at + span] = halves(array)
        at = base_z + SUB * i
        one_ref[at : at + SUB], two_ref[at : at + SUB] = ends(array)
    at = base + 3 * span + layers
    owners = jnp.broadcast_to(owner_ref[...].astype(jnp.float32), (SUB, cols))
    owners_ref[...] = owners
    send_ref[at : at + SUB] = owners


def place_kernel(ids_ref, own_ref, other_ref, place_ref, *, owner_count, chips, capacity):
    along = lax.axis_index("along")
    cross = lax.axis_index("cross")
    low = cross == 0
    cores = owner_count // chips
    patches = own_ref.shape[1]
    last = other_ref.shape[0] - SUB
    own = own_ref[0:1]
    other = other_ref[last : last + 1]
    owners = [jnp.where(low, own, other), jnp.where(low, other, own)]
    lane = lanes_of((patches, patches))
    half = patches // 2
    block = lane // half
    within = lane % half
    held = half // 2
    turn = (held - SUB) * cross
    patch = half * cross + 2 * lax.rem(within % held + turn, held) + within // held
    source = rows_of((patches, patches))
    number = rows_of((owner_count, patches)).astype(jnp.float32)
    chosen = jnp.zeros((owner_count, patches), jnp.float32)
    counts = jnp.zeros((owner_count, patches), jnp.float32)
    for i in range(2):
        owned = (number == owners[i]).astype(jnp.bfloat16)
        pick = jnp.where(block == i, jnp.where(source == patch, 1.0, 0.0), 0.0).astype(jnp.bfloat16)
        earlier = jnp.where(block == i, jnp.where(source < patch, 1.0, 0.0), 0.0).astype(jnp.bfloat16)
        chosen += jnp.dot(owned, pick, preferred_element_type=jnp.float32)
        counts += jnp.dot(owned, earlier, preferred_element_type=jnp.float32)
    rank = jnp.sum(chosen * counts, axis=0, keepdims=True).astype(jnp.int32)
    owner = jnp.sum(chosen * number, axis=0, keepdims=True).astype(jnp.int32)
    wanted = (along * cores + block) * patches + patch
    found = jnp.zeros((patches, patches), jnp.float32)
    for j in range(ids_ref.shape[1]):
        found = jnp.where(ids_ref[:, j : j + 1] == wanted, 1.0, found)
    member = jnp.sum(found, axis=0, keepdims=True)
    block = block[:1]
    chip = owner // cores
    owner_core = owner % cores
    some = 2 * capacity
    slot = block * capacity + rank
    if chips == 4:
        slot = slot + lax.rem(chip - along + 2 * chips - 1, chips) * some
    else:
        slot = slot + chip * some
    handler = owner_core
    slot = jnp.where(handler == cross, slot, slot + chips * some)
    slot = jnp.where(member > 0.0, slot, -1)
    place_ref[...] = jnp.where(rows_of(place_ref.shape) == slot, 1.0, 0.0).astype(jnp.bfloat16)


def gather_kernel(own_ref, one_ref, two_ref, three_ref, out_ref, sems):
    chips = 4
    along = lax.axis_index("along")
    count = out_ref.shape[0] // chips
    copies = []
    for i, (ref, ahead) in enumerate(
        ((own_ref, 0), (one_ref, 3), (two_ref, 2), (three_ref, 1))
    ):
        at = pl.multiple_of(lax.rem(along + ahead, chips) * count, SUB)
        copies.append(pltpu.make_async_copy(ref, out_ref.at[pl.ds(at, count)], sems.at[i]))
    for copy in copies:
        copy.start()
    for copy in copies:
        copy.wait()


def masks(depth, stiff, d_buf, wet_buf, scale_buf, half_buf, tile):
    layers = wet_buf.shape[1]
    zeros = jnp.zeros((SUB, depth.shape[1]), jnp.float32)
    d_buf[tile] = depth
    for z in range(layers):
        wet = depth > float(z)
        wet_buf[tile, z, :SUB] = zeros
        wet_buf[tile, z, SUB:] = jnp.where(wet, 1.0, 0.0)
        scale_buf[tile, z] = jnp.where(wet, stiff, 0.0)
        if z > 0:
            half_buf[tile, z - 1] = jnp.where(wet, 0.5, 0.0)


def advance(state, before_step, after_step, ZB, low_row=0, high_row=None):
    p_buf, w_buf, d_buf, wet_buf, scale_buf, half_buf, p_two, w_two = state
    layers = p_buf.shape[1]
    wide, cols = w_buf.shape[2:]
    groups = layers // ZB
    zeros = jnp.zeros((SUB, cols), jnp.float32)
    for tile in range(2):
        for z in range(layers):
            for buf in (p_buf, p_two):
                buf[tile, z, :SUB] = zeros
                buf[tile, z, SUB + wide :] = zeros
    def step(t, first, p_buf, w_buf, p_out, w_out, low_row=0, high_row=wide):
        rows = slice(low_row, high_row)
        here = slice(SUB + low_row, SUB + high_row)
        ahead = slice(SUB + low_row + 1, SUB + high_row + 1)
        back_rows = slice(SUB + low_row - 1, SUB + high_row - 1)
        lane = lanes_of((ZB, high_row - low_row, cols))
        last_lane = lane == cols - 1
        first_lane = lane == 0
        zero_layer = jnp.zeros((1, high_row - low_row, cols), jnp.float32)
        before_step(t, p_buf)

        def stage_a(g):
            zs = slice(g * ZB, (g + 1) * ZB)
            return [pltpu.roll(p_buf[i, zs, here], cols - 1, 2) for i in range(2)]

        def stage_b(g, turned):
            zs = slice(g * ZB, (g + 1) * ZB)
            right = [
                jnp.where(last_lane, turned[1], turned[0]),
                jnp.where(last_lane, 0.0, turned[1]),
            ]
            gy = [wet_buf[i, zs, here] * (right[i] - p_buf[i, zs, here]) for i in range(2)]
            return gy, [pltpu.roll(gy[i], 1, 2) for i in range(2)]

        hz_last = [None, None]
        surface = [None, None]

        def stage_c(g, gy, back):
            zs = slice(g * ZB, (g + 1) * ZB)
            before = [
                jnp.where(first_lane, 0.0, back[0]),
                jnp.where(first_lane, back[0], back[1]),
            ]
            for i in range(2):
                p = p_buf[i, zs, here]
                gx = wet_buf[i, zs, here] * (p_buf[i, zs, ahead] - p)
                behind = wet_buf[i, zs, back_rows] * (p - p_buf[i, zs, back_rows])
                w = w_buf[i, zs, rows] - (gx - behind)
                w = w - (gy[i] - before[i])
                w_out[i, zs, rows] = w
                if g + 1 < groups:
                    hz = half_buf[i, zs, rows] * (p_buf[i, g * ZB + 1 : (g + 1) * ZB + 1, here] - p)
                elif ZB > 1:
                    hz = jnp.concatenate([half_buf[i, g * ZB :, rows] * (p[1:] - p[:-1]), zero_layer], 0)
                else:
                    hz = zero_layer
                prev = zero_layer if g == 0 else hz_last[i]
                flux = w - (hz - (jnp.concatenate([prev, hz[:-1]], 0) if ZB > 1 else prev))
                hz_last[i] = hz[-1:]
                old = wet_buf[i, zs, here] * p if first else p
                new = old - scale_buf[i, zs, rows] * flux
                p_out[i, zs, here] = new
                for k in range(ZB):
                    part = new[k]
                    z = g * ZB + k
                    surface[i] = part if z == 0 else jnp.where(d_buf[i, rows] > float(z), part, surface[i])

        turned = [stage_a(0), stage_a(1)]
        ready = stage_b(0, turned[0])
        for g in range(groups):
            if g + 2 < groups:
                turned.append(stage_a(g + 2))
            coming = stage_b(g + 1, turned[g + 1]) if g + 1 < groups else None
            stage_c(g, *ready)
            ready = coming
        for i in range(2):
            after_step(t, i, surface[i])

    def two(k, carry):
        step(2 * k, False, p_buf, w_buf, p_two, w_two)
        step(2 * k + 1, False, p_two, w_two, p_buf, w_buf)
        return carry

    step(0, True, p_buf, w_buf, p_two, w_two)
    step(1, False, p_two, w_two, p_buf, w_buf)
    lax.fori_loop(1, STEPS // 2 - 1, two, 0)
    step(STEPS - 2, False, p_buf, w_buf, p_two, w_two)
    step(STEPS - 1, False, p_two, w_two, p_buf, w_buf, low_row, high_row or wide)


def state_buffers(layers, wide, cols):
    return [
        VMEM(shape, jnp.float32)
        for shape in (
            (2, layers, wide + 2 * SUB, cols),
            (2, layers, wide, cols),
            (2, wide, cols),
            (2, layers, wide + SUB, cols),
            (2, layers, wide, cols),
            (2, layers - 1, wide, cols),
            (2, layers, wide + 2 * SUB, cols),
            (2, layers, wide, cols),
        )
    ]


def inner_kernel(keep_ref, other_ref, p_keep_ref, p_send_ref, trace_ref, border_ref, *state):
    layers, inner_rows, cols = p_keep_ref.shape
    core = lax.axis_index("cross")
    low = core == 0
    span = inner_rows + 2 * SUB
    base = 2 * span * layers
    p_buf, w_buf, d_buf, wet_buf, scale_buf, half_buf, p_two, w_two = state
    lane = lanes_of((span, cols))
    at = base + 2 * span
    seam = jnp.where(low, keep_ref[at : at + span], other_ref[at : at + span])
    for tile, main_ref, seam_core in ((core, keep_ref, 1), (1 - core, other_ref, 0)):
        seam_lane = lane == jnp.where(core == seam_core, 0, -1)
        masks(
            main_ref[base : base + span],
            main_ref[base + span : base + 2 * span],
            d_buf, wet_buf, scale_buf, half_buf, tile,
        )
        for z in range(layers):
            at = 2 * span * z
            p_buf[tile, z, SUB : SUB + span] = main_ref[at : at + span]
            turned = pltpu.roll(seam, cols - z, 1) if z else seam
            w_buf[tile, z] = main_ref[at + span : at + 2 * span] - jnp.where(seam_lane, turned, 0.0)

    def before_step(t, p_now):
        for i in range(2):
            for z in range(layers):
                first, second = 2 * SUB, span - 1
                border_ref[t, i, z : z + 1] = jnp.where(
                    low, p_now[i, z, first : first + 1], p_now[i, z, second : second + 1]
                )

    def after_step(t, i, surface):
        trace_ref[t, i] = surface if surface.shape[0] == inner_rows else surface[SUB : SUB + inner_rows]

    advance(state, before_step, after_step, 4, SUB, SUB + inner_rows)
    for z in range(layers):
        p_keep_ref[z] = p_buf[core, z, 2 * SUB : 2 * SUB + inner_rows]
        p_send_ref[z] = p_buf[1 - core, z, 2 * SUB : 2 * SUB + inner_rows]


def outer_kernel(
    keep_ref, other_ref, halo_ref, place_ref, inner_ref, border_ref,
    p_keep_ref, p_send_ref, panel_keep_ref, panel_send_ref, panel_rest_ref, trace, *state,
):
    layers, cols = p_keep_ref.shape[0], p_keep_ref.shape[2]
    inner_rows = inner_ref.shape[2]
    core = lax.axis_index("cross")
    low = core == 0
    span = inner_rows + 2 * SUB
    near = SUB
    base = 2 * span * layers
    base_z = 2 * SUB * layers
    ends = halo_ref.shape[0] // 2
    p_buf, w_buf, d_buf, wet_buf, scale_buf, half_buf, p_two, w_two = state
    lane = lanes_of((SUB, cols))
    row = rows_of((SUB, cols))
    offset = (span - near) * core

    def main_rows(ref, at):
        return ref[pl.ds(pl.multiple_of(at + offset, SUB), near)]

    def joined(main, halo):
        return jnp.where(
            low, jnp.concatenate([halo, main], 0), jnp.concatenate([main, halo], 0)
        )

    seam_at = base_z + 2 * SUB
    seam_halo = jnp.where(
        low, halo_ref[seam_at : seam_at + SUB], halo_ref[ends + seam_at : ends + seam_at + SUB]
    )
    seam_main = jnp.where(
        low, main_rows(keep_ref, base + 2 * span), main_rows(other_ref, base + 2 * span)
    )
    seam = joined(seam_main, seam_halo)
    top_row = row == jnp.where(low, 0, -1)
    end_row = row == jnp.where(low, -1, 0)
    wide_lane = lanes_of((near + SUB, cols))
    for tile, main_ref, end, seam_core in ((core, keep_ref, 0, 1), (1 - core, other_ref, ends, 0)):
        seam_lane = wide_lane == jnp.where(core == seam_core, 0, -1)

        def end_rows(at):
            return halo_ref[end + at : end + at + SUB]

        masks(
            joined(main_rows(main_ref, base), end_rows(base_z)),
            joined(main_rows(main_ref, base + span), end_rows(base_z + SUB)),
            d_buf, wet_buf, scale_buf, half_buf, tile,
        )
        for z in range(layers):
            at = 2 * span * z
            at_z = 2 * SUB * z
            p_buf[tile, z, SUB : 2 * SUB + near] = joined(main_rows(main_ref, at), end_rows(at_z))
            w = main_rows(main_ref, at + span)
            w_end = end_rows(at_z + SUB)
            slot = jnp.broadcast_to(w_end[0:1], (SUB, cols))
            final = base + 3 * span + z
            final = jnp.broadcast_to(main_ref[final : final + 1], (SUB, cols))
            w = joined(w - jnp.where(top_row, slot, 0.0), w_end - jnp.where(end_row, final, 0.0))
            turned = pltpu.roll(seam, cols - z, 1) if z else seam
            w_buf[tile, z] = w - jnp.where(seam_lane, turned, 0.0)
        for z in range(layers):
            first, second = base + SUB, base + span - SUB - 1
            depth = jnp.where(
                low, main_ref[first : first + 1], main_ref[second : second + 1]
            )
            wet_buf[tile, z, SUB - 1 : SUB] = jnp.where(depth > float(z), 1.0, 0.0)

    def before_step(t, p_now):
        for i in range(2):
            for z in range(layers):
                value = border_ref[t, i, z : z + 1]
                p_now[i, z, SUB - 1 : SUB] = value
                p_now[i, z, 2 * SUB + near : 2 * SUB + near + 1] = value

    def after_step(t, i, surface):
        trace[t, i] = jnp.where(low, surface[SUB:], surface[:SUB])

    advance(state, before_step, after_step, 8)
    own = pl.multiple_of(SUB + SUB * (1 - core), SUB)
    for z in range(layers):
        p_keep_ref[z] = p_buf[core, z, pl.ds(own, SUB)]
        p_send_ref[z] = p_buf[1 - core, z, pl.ds(own, SUB)]

    width = cols // 2
    lane_rows = lanes_of((inner_rows + SUB, cols))
    parts = STEPS // 2
    wholes = []
    for j in range(parts):
        pieces = []
        for i in range(2):
            one = jnp.concatenate([trace[2 * j, i], inner_ref[2 * j, i]], 0)
            two = jnp.concatenate([trace[2 * j + 1, i], inner_ref[2 * j + 1, i]], 0)
            pieces.append(jnp.where(lane_rows < width, one, pltpu.roll(two, width, 1)))
            pieces.append(jnp.where(lane_rows < width, pltpu.roll(one, width, 1), two))
        wholes.append(jnp.concatenate(pieces, 0))
    both = jnp.concatenate(wholes, 1)
    part_a = both.astype(jnp.bfloat16)
    rest = both - part_a.astype(jnp.float32)
    part_b = rest.astype(jnp.bfloat16)
    part_c = (rest - part_b.astype(jnp.float32)).astype(jnp.bfloat16)
    total = jnp.dot(
        jnp.concatenate([place_ref[...]] * 3, 1),
        jnp.concatenate([part_a, part_b, part_c], 0),
        preferred_element_type=jnp.float32,
    )
    for j in range(parts):
        piece = total[:, j * cols : (j + 1) * cols]
        at = 0
        for ref in (panel_keep_ref, panel_send_ref, panel_rest_ref):
            count = ref.shape[0] // parts
            ref[pl.ds(j, count, stride=parts)] = piece[at : at + count]
            at += count


def shards(
    pressure_start, along_start, cross_start, depth_layers, stiffness, patch_lists, owner_map
):
    sensors, layers, rows, cols = pressure_start.shape
    f32 = jnp.float32
    along_count = lax.axis_size("along")
    cross_count = lax.axis_size("cross")
    low = lax.axis_index("cross") == 0
    swap = [(0, 1), (1, 0)]
    pair = ("along", "cross")
    steps_up = range(along_count - 1)
    route = [(2 * i, 2 * i + 2) for i in steps_up] + [(2 * i + 3, 2 * i + 1) for i in steps_up]
    half_rows = rows // 2
    span = half_rows + SUB
    pack_rows = 2 * span * layers + 3 * span + layers
    end_rows = 2 * SUB * layers + 3 * SUB

    spec = pl.BlockSpec(memory_space=VMEM)
    hbm = pl.BlockSpec(memory_space=pltpu.HBM)
    params = pltpu.CompilerParams(vmem_limit_bytes=32 * 1024 * 1024)
    keep, send, one, two, ids, owners = pl.pallas_call(
        edges_kernel,
        out_shape=[
            jax.ShapeDtypeStruct((pack_rows, cols), f32),
            jax.ShapeDtypeStruct((pack_rows + SUB, cols), f32),
            jax.ShapeDtypeStruct((end_rows, cols), f32),
            jax.ShapeDtypeStruct((end_rows, cols), f32),
            jax.ShapeDtypeStruct(patch_lists.shape, jnp.int32),
            jax.ShapeDtypeStruct((SUB, cols), f32),
        ],
        in_specs=[hbm] * 7,
        out_specs=[spec] * 6,
        scratch_shapes=[
            VMEM((layers, rows, cols), f32),
            VMEM((layers, rows, cols), f32),
            VMEM((layers, rows, cols), f32),
            VMEM((rows, cols), jnp.int32),
            VMEM((rows, cols), f32),
            VMEM(owner_map.shape, jnp.int32),
            pltpu.SemaphoreType.DMA((10,)),
        ],
        compiler_params=params,
        name="edges",
    )(
        *(
            pltpu.with_memory_space_constraint(x, pltpu.HBM)
            for x in (
                pressure_start[0],
                along_start[0],
                cross_start[0],
                depth_layers,
                stiffness,
                owner_map,
                patch_lists,
            )
        )
    )

    two = lax.ppermute(two, "cross", swap)
    halo = jnp.concatenate([one, two], 0)
    send = lax.optimization_barrier((send, two))[0]
    other = lax.ppermute(send, "cross", swap)
    halo = lax.ppermute(halo, pair, route)

    patch_count = 2 * rows
    owner_count = along_count * cross_count
    capacity = patch_count // owner_count + 1
    count = owner_count * capacity
    place = pl.pallas_call(
        functools.partial(
            place_kernel, owner_count=owner_count, chips=along_count, capacity=capacity
        ),
        out_shape=jax.ShapeDtypeStruct((2 * count, patch_count), jnp.bfloat16),
        in_specs=[spec] * 3,
        out_specs=spec,
        compiler_params=params,
        name="place",
    )(ids.reshape(-1, patch_count).T, owners, other)

    parts = STEPS // 2
    inner_rows = half_rows - SUB
    inner_shape = jax.ShapeDtypeStruct((layers, inner_rows, cols), f32)
    inner_keep, inner_send, inner_trace, border = pl.pallas_call(
        inner_kernel,
        out_shape=[
            inner_shape,
            inner_shape,
            jax.ShapeDtypeStruct((STEPS, 2, inner_rows, cols), f32),
            jax.ShapeDtypeStruct((STEPS, 2, layers, cols), f32),
        ],
        in_specs=[spec] * 2,
        out_specs=[spec] * 4,
        scratch_shapes=state_buffers(layers, span, cols),
        compiler_params=params,
        cost_estimate=pl.CostEstimate(
            flops=400 * layers * span * cols,
            bytes_accessed=200 * layers * span * cols,
            transcendentals=0,
        ),
        name="inner",
    )(keep, other)
    outer_shape = jax.ShapeDtypeStruct((layers, SUB, cols), f32)
    some = 2 * capacity * parts
    outer_keep, outer_send, panel_keep, panel_send, panel_rest = pl.pallas_call(
        outer_kernel,
        out_shape=[outer_shape, outer_shape]
        + [
            jax.ShapeDtypeStruct((number, cols), f32)
            for number in (along_count * some, some, (along_count - 1) * some)
        ],
        in_specs=[spec] * 6,
        out_specs=[spec] * 5,
        scratch_shapes=[VMEM((STEPS, 2, SUB, cols), f32)] + state_buffers(layers, 2 * SUB, cols),
        compiler_params=params,
        name="outer",
    )(keep, other, halo, place, inner_trace, border)

    panel_first = panel_keep[:some] + lax.ppermute(panel_send, "cross", swap)
    rest_other = lax.ppermute(panel_rest, "cross", swap)
    panel_rest = panel_keep[some:] + rest_other
    if along_count == 4:
        pieces = [panel_rest[2 * some :]]
        for k in range(1, along_count):
            piece = panel_first if k == 1 else panel_rest[(k - 2) * some : (k - 1) * some]
            route = [(i, (i + k) % along_count) for i in range(along_count)]
            pieces.append(lax.ppermute(piece, "along", route))
        received = pl.pallas_call(
            gather_kernel,
            out_shape=jax.ShapeDtypeStruct((count * parts, cols), f32),
            in_specs=[spec] * 4,
            out_specs=hbm,
            scratch_shapes=[pltpu.SemaphoreType.DMA((4,))],
            compiler_params=params,
            name="gather",
        )(*pieces)
    else:
        panels = jnp.concatenate([panel_first, panel_rest], 0).reshape(along_count, some, cols)
        received = lax.all_to_all(panels, "along", split_axis=0, concat_axis=0, tiled=True)
    received = received.reshape(1, count, 1, parts * cols)

    inner_other = lax.ppermute(inner_send, "cross", swap)
    outer_other = lax.ppermute(outer_send, "cross", swap)
    pressure = jnp.where(
        low,
        jnp.concatenate([outer_keep, inner_keep, inner_other, outer_other], 1),
        jnp.concatenate([outer_other, inner_other, inner_keep, outer_keep], 1),
    )
    return (pressure[None], received)


def solution(mesh):
    in_specs = (
        P("batch", None, "along", "cross"),
        P("batch", None, "along", "cross"),
        P("batch", None, "along", "cross"),
        P("along", "cross"),
        P("along", "cross"),
        P("batch", None),
        P(("along", "cross"), None),
    )
    out_specs = (P("batch", None, "along", "cross"), P(("along", "cross"), None, "batch", None))
    return jax.shard_map(shards, mesh=mesh, in_specs=in_specs, out_specs=out_specs, check_vma=False)
```

```python
import functools

import jax
import jax.numpy as jnp
from jax import lax
from jax.experimental import pallas as pl
from jax.experimental.pallas import tpu as pltpu
from jax.sharding import PartitionSpec as P

STEPS = 8
SUB = 8
VMEM = pltpu.VMEM


def lanes_of(shape):
    return lax.broadcasted_iota(jnp.int32, shape, len(shape) - 1)


def rows_of(shape):
    return lax.broadcasted_iota(jnp.int32, shape, len(shape) - 2)


def edges_kernel(
    p_hbm, fa_hbm, fc_hbm, depth_hbm, stiff_hbm, owner_hbm, ids_hbm,
    keep_ref, send_ref, one_ref, two_ref, ids_ref, owners_ref,
    p_ref, fa_ref, fc_ref, depth_ref, stiff_ref, owner_ref, sems,
):
    layers, rows, cols = p_ref.shape
    half = layers // 2
    pairs = []
    for part in (slice(0, half), slice(half, layers)):
        for source, target in ((fa_hbm, fa_ref), (fc_hbm, fc_ref), (p_hbm, p_ref)):
            pairs.append((source.at[part], target.at[part]))
        if not part.start:
            pairs += [
                (depth_hbm, depth_ref), (stiff_hbm, stiff_ref), (owner_hbm, owner_ref), (ids_hbm, ids_ref)
            ]
    copies = [
        pltpu.make_async_copy(source, target, sems.at[i]) for i, (source, target) in enumerate(pairs)
    ]
    for copy in copies:
        copy.start()
    for copy in copies[:7]:
        copy.wait()
    low = lax.axis_index("cross") == 0
    span = rows // 2 + SUB
    last = rows - SUB
    lane = lanes_of((rows, cols))
    row = rows_of((rows, cols))
    row_sub = rows_of((SUB, cols))
    depth = depth_ref[...]
    stiff = stiff_ref[...]
    first_lane = lane == 0
    slot_one = row_sub == jnp.where(low, 0, -1)
    slot_two = row_sub == jnp.where(low, -1, 0)
    base = 2 * span * layers
    base_z = 2 * SUB * layers
    velocity = jnp.zeros((rows, cols), jnp.float32)

    def halves(array):
        first, second = array[:span], array[rows - span :]
        return jnp.where(low, first, second), jnp.where(low, second, first)

    def ends(array):
        first, second = array[:SUB], array[last:]
        return jnp.where(low, second, first), jnp.where(low, first, second)

    for z in range(layers):
        if z == half:
            for copy in copies[7:]:
                copy.wait()
        wet = depth > z
        p = p_ref[z]
        va = jnp.where(wet, fa_ref[z], 0.0)
        vc = jnp.where(wet, fc_ref[z], 0.0)
        behind = jnp.where(row == 0, 0.0, pltpu.roll(va, 1, 0))
        before = jnp.where(first_lane, 0.0, pltpu.roll(vc, 1, 1))
        w = (va - behind) + (vc - before)
        velocity = jnp.where(lane == z, pltpu.roll(vc, z + 1, 1), velocity)
        at = 2 * span * z
        keep_ref[at : at + span], send_ref[at : at + span] = halves(p)
        at += span
        keep_ref[at : at + span], send_ref[at : at + span] = halves(w)
        final = va[rows - 1 : rows]
        at = base + 3 * span + z
        keep_ref[at : at + 1] = final
        send_ref[at : at + 1] = final
        at = 2 * SUB * z
        one_ref[at : at + SUB], two_ref[at : at + SUB] = ends(p)
        at += SUB
        one, two = ends(w)
        final = jnp.broadcast_to(final, (SUB, cols))
        one_ref[at : at + SUB] = jnp.where(slot_one, final, one)
        two_ref[at : at + SUB] = jnp.where(slot_two, final, two)
    for i, array in enumerate((depth.astype(jnp.float32), stiff, velocity)):
        at = base + span * i
        keep_ref[at : at + span], send_ref[at : at + span] = halves(array)
        at = base_z + SUB * i
        one_ref[at : at + SUB], two_ref[at : at + SUB] = ends(array)
    at = base + 3 * span + layers
    owners = jnp.broadcast_to(owner_ref[...].astype(jnp.float32), (SUB, cols))
    owners_ref[...] = owners
    send_ref[at : at + SUB] = owners


def place_kernel(ids_ref, own_ref, other_ref, place_ref, *, owner_count, chips, capacity):
    along = lax.axis_index("along")
    cross = lax.axis_index("cross")
    low = cross == 0
    cores = owner_count // chips
    patches = own_ref.shape[1]
    last = other_ref.shape[0] - SUB
    own = own_ref[0:1]
    other = other_ref[last : last + 1]
    owners = [jnp.where(low, own, other), jnp.where(low, other, own)]
    lane = lanes_of((patches, patches))
    half = patches // 2
    block = lane // half
    within = lane % half
    held = half // 2
    turn = (held - SUB) * cross
    patch = half * cross + 2 * lax.rem(within % held + turn, held) + within // held
    source = rows_of((patches, patches))
    number = rows_of((owner_count, patches)).astype(jnp.float32)
    chosen = jnp.zeros((owner_count, patches), jnp.float32)
    counts = jnp.zeros((owner_count, patches), jnp.float32)
    for i in range(2):
        owned = (number == owners[i]).astype(jnp.bfloat16)
        pick = jnp.where(block == i, jnp.where(source == patch, 1.0, 0.0), 0.0).astype(jnp.bfloat16)
        earlier = jnp.where(block == i, jnp.where(source < patch, 1.0, 0.0), 0.0).astype(jnp.bfloat16)
        chosen += jnp.dot(owned, pick, preferred_element_type=jnp.float32)
        counts += jnp.dot(owned, earlier, preferred_element_type=jnp.float32)
    rank = jnp.sum(chosen * counts, axis=0, keepdims=True).astype(jnp.int32)
    owner = jnp.sum(chosen * number, axis=0, keepdims=True).astype(jnp.int32)
    wanted = (along * cores + block) * patches + patch
    found = jnp.zeros((patches, patches), jnp.float32)
    for j in range(ids_ref.shape[1]):
        found = jnp.where(ids_ref[:, j : j + 1] == wanted, 1.0, found)
    member = jnp.sum(found, axis=0, keepdims=True)
    block = block[:1]
    chip = owner // cores
    owner_core = owner % cores
    some = 2 * capacity
    slot = block * capacity + rank
    if chips == 4:
        slot = slot + lax.rem(chip - along + 2 * chips - 1, chips) * some
    else:
        slot = slot + chip * some
    handler = owner_core
    slot = jnp.where(handler == cross, slot, slot + chips * some)
    slot = jnp.where(member > 0.0, slot, -1)
    place_ref[...] = jnp.where(rows_of(place_ref.shape) == slot, 1.0, 0.0).astype(jnp.bfloat16)


def copy_blocks(blocks, out_ref, sems):
    chips = 4
    along = lax.axis_index("along")
    count = out_ref.shape[0] // chips
    copies = []
    for i, (ref, ahead) in enumerate(blocks):
        at = pl.multiple_of(lax.rem(along + ahead, chips) * count, SUB)
        copies.append(pltpu.make_async_copy(ref, out_ref.at[pl.ds(at, count)], sems.at[i]))
    for copy in copies:
        copy.start()
    for copy in copies:
        copy.wait()


def gather_kernel(own_ref, one_ref, out_ref, sems):
    copy_blocks(((own_ref, 0), (one_ref, 3)), out_ref, sems)


def last_kernel(two_ref, three_ref, in_ref, out_ref, sems):
    copy_blocks(((two_ref, 2), (three_ref, 1)), out_ref, sems)


def masks(depth, stiff, d_buf, wet_buf, scale_buf, half_buf, tile):
    layers = wet_buf.shape[1]
    zeros = jnp.zeros((SUB, depth.shape[1]), jnp.float32)
    d_buf[tile] = depth
    for z in range(layers):
        wet = depth > float(z)
        wet_buf[tile, z, :SUB] = zeros
        wet_buf[tile, z, SUB:] = jnp.where(wet, 1.0, 0.0)
        scale_buf[tile, z] = jnp.where(wet, stiff, 0.0)
        if z > 0:
            half_buf[tile, z - 1] = jnp.where(wet, 0.5, 0.0)


def advance(state, before_step, after_step, ZB, low_row=0, high_row=None):
    p_buf, w_buf, d_buf, wet_buf, scale_buf, half_buf, p_two, w_two = state
    layers = p_buf.shape[1]
    wide, cols = w_buf.shape[2:]
    groups = layers // ZB
    zeros = jnp.zeros((SUB, cols), jnp.float32)
    for tile in range(2):
        for z in range(layers):
            for buf in (p_buf, p_two):
                buf[tile, z, :SUB] = zeros
                buf[tile, z, SUB + wide :] = zeros
    def step(t, first, p_buf, w_buf, p_out, w_out, low_row=0, high_row=wide):
        rows = slice(low_row, high_row)
        here = slice(SUB + low_row, SUB + high_row)
        ahead = slice(SUB + low_row + 1, SUB + high_row + 1)
        back_rows = slice(SUB + low_row - 1, SUB + high_row - 1)
        lane = lanes_of((ZB, high_row - low_row, cols))
        last_lane = lane == cols - 1
        first_lane = lane == 0
        zero_layer = jnp.zeros((1, high_row - low_row, cols), jnp.float32)
        before_step(t, p_buf)

        def stage_a(g):
            zs = slice(g * ZB, (g + 1) * ZB)
            return [pltpu.roll(p_buf[i, zs, here], cols - 1, 2) for i in range(2)]

        def stage_b(g, turned):
            zs = slice(g * ZB, (g + 1) * ZB)
            right = [
                jnp.where(last_lane, turned[1], turned[0]),
                jnp.where(last_lane, 0.0, turned[1]),
            ]
            gy = [wet_buf[i, zs, here] * (right[i] - p_buf[i, zs, here]) for i in range(2)]
            return gy, [pltpu.roll(gy[i], 1, 2) for i in range(2)]

        hz_last = [None, None]
        surface = [None, None]

        def stage_c(g, gy, back):
            zs = slice(g * ZB, (g + 1) * ZB)
            before = [
                jnp.where(first_lane, 0.0, back[0]),
                jnp.where(first_lane, back[0], back[1]),
            ]
            for i in range(2):
                p = p_buf[i, zs, here]
                gx = wet_buf[i, zs, here] * (p_buf[i, zs, ahead] - p)
                behind = wet_buf[i, zs, back_rows] * (p - p_buf[i, zs, back_rows])
                w = w_buf[i, zs, rows] - (gx - behind)
                w = w - (gy[i] - before[i])
                w_out[i, zs, rows] = w
                if g + 1 < groups:
                    hz = half_buf[i, zs, rows] * (p_buf[i, g * ZB + 1 : (g + 1) * ZB + 1, here] - p)
                elif ZB > 1:
                    hz = jnp.concatenate([half_buf[i, g * ZB :, rows] * (p[1:] - p[:-1]), zero_layer], 0)
                else:
                    hz = zero_layer
                prev = zero_layer if g == 0 else hz_last[i]
                flux = w - (hz - (jnp.concatenate([prev, hz[:-1]], 0) if ZB > 1 else prev))
                hz_last[i] = hz[-1:]
                old = wet_buf[i, zs, here] * p if first else p
                new = old - scale_buf[i, zs, rows] * flux
                p_out[i, zs, here] = new
                for k in range(ZB):
                    part = new[k]
                    z = g * ZB + k
                    surface[i] = part if z == 0 else jnp.where(d_buf[i, rows] > float(z), part, surface[i])

        turned = [stage_a(0), stage_a(1)]
        ready = stage_b(0, turned[0])
        for g in range(groups):
            if g + 2 < groups:
                turned.append(stage_a(g + 2))
            coming = stage_b(g + 1, turned[g + 1]) if g + 1 < groups else None
            stage_c(g, *ready)
            ready = coming
        for i in range(2):
            after_step(t, i, surface[i])

    def two(k, carry):
        step(2 * k, False, p_buf, w_buf, p_two, w_two)
        step(2 * k + 1, False, p_two, w_two, p_buf, w_buf)
        return carry

    step(0, True, p_buf, w_buf, p_two, w_two)
    step(1, False, p_two, w_two, p_buf, w_buf)
    lax.fori_loop(1, STEPS // 2 - 1, two, 0)
    step(STEPS - 2, False, p_buf, w_buf, p_two, w_two)
    step(STEPS - 1, False, p_two, w_two, p_buf, w_buf, low_row, high_row or wide)


def state_buffers(layers, wide, cols):
    return [
        VMEM(shape, jnp.float32)
        for shape in (
            (2, layers, wide + 2 * SUB, cols),
            (2, layers, wide, cols),
            (2, wide, cols),
            (2, layers, wide + SUB, cols),
            (2, layers, wide, cols),
            (2, layers - 1, wide, cols),
            (2, layers, wide + 2 * SUB, cols),
            (2, layers, wide, cols),
        )
    ]


def inner_kernel(keep_ref, other_ref, p_keep_ref, p_send_ref, trace_ref, border_ref, *state):
    layers, inner_rows, cols = p_keep_ref.shape
    core = lax.axis_index("cross")
    low = core == 0
    span = inner_rows + 2 * SUB
    base = 2 * span * layers
    p_buf, w_buf, d_buf, wet_buf, scale_buf, half_buf, p_two, w_two = state
    lane = lanes_of((span, cols))
    at = base + 2 * span
    seam = jnp.where(low, keep_ref[at : at + span], other_ref[at : at + span])
    for tile, main_ref, seam_core in ((core, keep_ref, 1), (1 - core, other_ref, 0)):
        seam_lane = lane == jnp.where(core == seam_core, 0, -1)
        masks(
            main_ref[base : base + span],
            main_ref[base + span : base + 2 * span],
            d_buf, wet_buf, scale_buf, half_buf, tile,
        )
        for z in range(layers):
            at = 2 * span * z
            p_buf[tile, z, SUB : SUB + span] = main_ref[at : at + span]
            turned = pltpu.roll(seam, cols - z, 1) if z else seam
            w_buf[tile, z] = main_ref[at + span : at + 2 * span] - jnp.where(seam_lane, turned, 0.0)

    def before_step(t, p_now):
        for i in range(2):
            for z in range(layers):
                first, second = 2 * SUB, span - 1
                border_ref[t, i, z : z + 1] = jnp.where(
                    low, p_now[i, z, first : first + 1], p_now[i, z, second : second + 1]
                )

    def after_step(t, i, surface):
        trace_ref[t, i] = surface if surface.shape[0] == inner_rows else surface[SUB : SUB + inner_rows]

    advance(state, before_step, after_step, 4, SUB, SUB + inner_rows)
    for z in range(layers):
        p_keep_ref[z] = p_buf[core, z, 2 * SUB : 2 * SUB + inner_rows]
        p_send_ref[z] = p_buf[1 - core, z, 2 * SUB : 2 * SUB + inner_rows]


def outer_kernel(
    keep_ref, other_ref, halo_ref, place_ref, inner_ref, border_ref,
    p_keep_ref, p_send_ref, panel_keep_ref, panel_send_ref, panel_rest_ref, trace, *state,
):
    layers, cols = p_keep_ref.shape[0], p_keep_ref.shape[2]
    inner_rows = inner_ref.shape[2]
    core = lax.axis_index("cross")
    low = core == 0
    span = inner_rows + 2 * SUB
    near = SUB
    base = 2 * span * layers
    base_z = 2 * SUB * layers
    ends = halo_ref.shape[0] // 2
    p_buf, w_buf, d_buf, wet_buf, scale_buf, half_buf, p_two, w_two = state
    lane = lanes_of((SUB, cols))
    row = rows_of((SUB, cols))
    offset = (span - near) * core

    def main_rows(ref, at):
        return ref[pl.ds(pl.multiple_of(at + offset, SUB), near)]

    def joined(main, halo):
        return jnp.where(
            low, jnp.concatenate([halo, main], 0), jnp.concatenate([main, halo], 0)
        )

    seam_at = base_z + 2 * SUB
    seam_halo = jnp.where(
        low, halo_ref[seam_at : seam_at + SUB], halo_ref[ends + seam_at : ends + seam_at + SUB]
    )
    seam_main = jnp.where(
        low, main_rows(keep_ref, base + 2 * span), main_rows(other_ref, base + 2 * span)
    )
    seam = joined(seam_main, seam_halo)
    top_row = row == jnp.where(low, 0, -1)
    end_row = row == jnp.where(low, -1, 0)
    wide_lane = lanes_of((near + SUB, cols))
    for tile, main_ref, end, seam_core in ((core, keep_ref, 0, 1), (1 - core, other_ref, ends, 0)):
        seam_lane = wide_lane == jnp.where(core == seam_core, 0, -1)

        def end_rows(at):
            return halo_ref[end + at : end + at + SUB]

        masks(
            joined(main_rows(main_ref, base), end_rows(base_z)),
            joined(main_rows(main_ref, base + span), end_rows(base_z + SUB)),
            d_buf, wet_buf, scale_buf, half_buf, tile,
        )
        for z in range(layers):
            at = 2 * span * z
            at_z = 2 * SUB * z
            p_buf[tile, z, SUB : 2 * SUB + near] = joined(main_rows(main_ref, at), end_rows(at_z))
            w = main_rows(main_ref, at + span)
            w_end = end_rows(at_z + SUB)
            slot = jnp.broadcast_to(w_end[0:1], (SUB, cols))
            final = base + 3 * span + z
            final = jnp.broadcast_to(main_ref[final : final + 1], (SUB, cols))
            w = joined(w - jnp.where(top_row, slot, 0.0), w_end - jnp.where(end_row, final, 0.0))
            turned = pltpu.roll(seam, cols - z, 1) if z else seam
            w_buf[tile, z] = w - jnp.where(seam_lane, turned, 0.0)
        for z in range(layers):
            first, second = base + SUB, base + span - SUB - 1
            depth = jnp.where(
                low, main_ref[first : first + 1], main_ref[second : second + 1]
            )
            wet_buf[tile, z, SUB - 1 : SUB] = jnp.where(depth > float(z), 1.0, 0.0)

    def before_step(t, p_now):
        for i in range(2):
            for z in range(layers):
                value = border_ref[t, i, z : z + 1]
                p_now[i, z, SUB - 1 : SUB] = value
                p_now[i, z, 2 * SUB + near : 2 * SUB + near + 1] = value

    def after_step(t, i, surface):
        trace[t, i] = jnp.where(low, surface[SUB:], surface[:SUB])

    advance(state, before_step, after_step, 8)
    own = pl.multiple_of(SUB + SUB * (1 - core), SUB)
    for z in range(layers):
        p_keep_ref[z] = p_buf[core, z, pl.ds(own, SUB)]
        p_send_ref[z] = p_buf[1 - core, z, pl.ds(own, SUB)]

    width = cols // 2
    lane_rows = lanes_of((inner_rows + SUB, cols))
    parts = STEPS // 2
    wholes = []
    for j in range(parts):
        pieces = []
        for i in range(2):
            one = jnp.concatenate([trace[2 * j, i], inner_ref[2 * j, i]], 0)
            two = jnp.concatenate([trace[2 * j + 1, i], inner_ref[2 * j + 1, i]], 0)
            pieces.append(jnp.where(lane_rows < width, one, pltpu.roll(two, width, 1)))
            pieces.append(jnp.where(lane_rows < width, pltpu.roll(one, width, 1), two))
        wholes.append(jnp.concatenate(pieces, 0))
    both = jnp.concatenate(wholes, 1)
    part_a = both.astype(jnp.bfloat16)
    rest = both - part_a.astype(jnp.float32)
    part_b = rest.astype(jnp.bfloat16)
    part_c = (rest - part_b.astype(jnp.float32)).astype(jnp.bfloat16)
    total = jnp.dot(
        jnp.concatenate([place_ref[...]] * 3, 1),
        jnp.concatenate([part_a, part_b, part_c], 0),
        preferred_element_type=jnp.float32,
    )
    for j in range(parts):
        piece = total[:, j * cols : (j + 1) * cols]
        at = 0
        for ref in (panel_keep_ref, panel_send_ref, panel_rest_ref):
            count = ref.shape[0] // parts
            ref[pl.ds(j, count, stride=parts)] = piece[at : at + count]
            at += count


def shards(
    pressure_start, along_start, cross_start, depth_layers, stiffness, patch_lists, owner_map
):
    sensors, layers, rows, cols = pressure_start.shape
    f32 = jnp.float32
    along_count = lax.axis_size("along")
    cross_count = lax.axis_size("cross")
    low = lax.axis_index("cross") == 0
    swap = [(0, 1), (1, 0)]
    pair = ("along", "cross")
    steps_up = range(along_count - 1)
    route = [(2 * i, 2 * i + 2) for i in steps_up] + [(2 * i + 3, 2 * i + 1) for i in steps_up]
    half_rows = rows // 2
    span = half_rows + SUB
    pack_rows = 2 * span * layers + 3 * span + layers
    end_rows = 2 * SUB * layers + 3 * SUB

    spec = pl.BlockSpec(memory_space=VMEM)
    hbm = pl.BlockSpec(memory_space=pltpu.HBM)
    params = pltpu.CompilerParams(vmem_limit_bytes=32 * 1024 * 1024)
    keep, send, one, two, ids, owners = pl.pallas_call(
        edges_kernel,
        out_shape=[
            jax.ShapeDtypeStruct((pack_rows, cols), f32),
            jax.ShapeDtypeStruct((pack_rows + SUB, cols), f32),
            jax.ShapeDtypeStruct((end_rows, cols), f32),
            jax.ShapeDtypeStruct((end_rows, cols), f32),
            jax.ShapeDtypeStruct(patch_lists.shape, jnp.int32),
            jax.ShapeDtypeStruct((SUB, cols), f32),
        ],
        in_specs=[hbm] * 7,
        out_specs=[spec] * 6,
        scratch_shapes=[
            VMEM((layers, rows, cols), f32),
            VMEM((layers, rows, cols), f32),
            VMEM((layers, rows, cols), f32),
            VMEM((rows, cols), jnp.int32),
            VMEM((rows, cols), f32),
            VMEM(owner_map.shape, jnp.int32),
            pltpu.SemaphoreType.DMA((10,)),
        ],
        compiler_params=params,
        name="edges",
    )(
        *(
            pltpu.with_memory_space_constraint(x, pltpu.HBM)
            for x in (
                pressure_start[0],
                along_start[0],
                cross_start[0],
                depth_layers,
                stiffness,
                owner_map,
                patch_lists,
            )
        )
    )

    two = lax.ppermute(two, "cross", swap)
    halo = jnp.concatenate([one, two], 0)
    send = lax.optimization_barrier((send, two))[0]
    other = lax.ppermute(send, "cross", swap)
    halo = lax.ppermute(halo, pair, route)

    patch_count = 2 * rows
    owner_count = along_count * cross_count
    capacity = patch_count // owner_count + 1
    count = owner_count * capacity
    place = pl.pallas_call(
        functools.partial(
            place_kernel, owner_count=owner_count, chips=along_count, capacity=capacity
        ),
        out_shape=jax.ShapeDtypeStruct((2 * count, patch_count), jnp.bfloat16),
        in_specs=[spec] * 3,
        out_specs=spec,
        compiler_params=params,
        name="place",
    )(ids.reshape(-1, patch_count).T, owners, other)

    parts = STEPS // 2
    inner_rows = half_rows - SUB
    inner_shape = jax.ShapeDtypeStruct((layers, inner_rows, cols), f32)
    inner_keep, inner_send, inner_trace, border = pl.pallas_call(
        inner_kernel,
        out_shape=[
            inner_shape,
            inner_shape,
            jax.ShapeDtypeStruct((STEPS, 2, inner_rows, cols), f32),
            jax.ShapeDtypeStruct((STEPS, 2, layers, cols), f32),
        ],
        in_specs=[spec] * 2,
        out_specs=[spec] * 4,
        scratch_shapes=state_buffers(layers, span, cols),
        compiler_params=params,
        cost_estimate=pl.CostEstimate(
            flops=400 * layers * span * cols,
            bytes_accessed=200 * layers * span * cols,
            transcendentals=0,
        ),
        name="inner",
    )(keep, other)
    outer_shape = jax.ShapeDtypeStruct((layers, SUB, cols), f32)
    some = 2 * capacity * parts
    outer_keep, outer_send, panel_keep, panel_send, panel_rest = pl.pallas_call(
        outer_kernel,
        out_shape=[outer_shape, outer_shape]
        + [
            jax.ShapeDtypeStruct((number, cols), f32)
            for number in (along_count * some, some, (along_count - 1) * some)
        ],
        in_specs=[spec] * 6,
        out_specs=[spec] * 5,
        scratch_shapes=[VMEM((STEPS, 2, SUB, cols), f32)] + state_buffers(layers, 2 * SUB, cols),
        compiler_params=params,
        name="outer",
    )(keep, other, halo, place, inner_trace, border)

    panel_first = panel_keep[:some] + lax.ppermute(panel_send, "cross", swap)
    rest_other = lax.ppermute(panel_rest, "cross", swap)
    panel_rest = panel_keep[some:] + rest_other
    if along_count == 4:
        pieces = [panel_rest[2 * some :]]
        for k in range(1, along_count):
            piece = panel_first if k == 1 else panel_rest[(k - 2) * some : (k - 1) * some]
            route = [(i, (i + k) % along_count) for i in range(along_count)]
            pieces.append(lax.ppermute(piece, "along", route))
        out_shape = jax.ShapeDtypeStruct((count * parts, cols), f32)
        received = pl.pallas_call(
            gather_kernel,
            out_shape=out_shape,
            in_specs=[spec] * 2,
            out_specs=hbm,
            scratch_shapes=[pltpu.SemaphoreType.DMA((2,))],
            compiler_params=params,
            name="gather",
        )(*pieces[:2])
        received = pl.pallas_call(
            last_kernel,
            out_shape=out_shape,
            in_specs=[spec, spec, hbm],
            out_specs=hbm,
            scratch_shapes=[pltpu.SemaphoreType.DMA((2,))],
            input_output_aliases={2: 0},
            compiler_params=params,
            name="last",
        )(pieces[2], pieces[3], pltpu.with_memory_space_constraint(received, pltpu.HBM))
    else:
        panels = jnp.concatenate([panel_first, panel_rest], 0).reshape(along_count, some, cols)
        received = lax.all_to_all(panels, "along", split_axis=0, concat_axis=0, tiled=True)
    received = received.reshape(1, count, 1, parts * cols)

    inner_other = lax.ppermute(inner_send, "cross", swap)
    outer_other = lax.ppermute(outer_send, "cross", swap)
    pressure = jnp.where(
        low,
        jnp.concatenate([outer_keep, inner_keep, inner_other, outer_other], 1),
        jnp.concatenate([outer_other, inner_other, inner_keep, outer_keep], 1),
    )
    return (pressure[None], received)


def solution(mesh):
    in_specs = (
        P("batch", None, "along", "cross"),
        P("batch", None, "along", "cross"),
        P("batch", None, "along", "cross"),
        P("along", "cross"),
        P("along", "cross"),
        P("batch", None),
        P(("along", "cross"), None),
    )
    out_specs = (P("batch", None, "along", "cross"), P(("along", "cross"), None, "batch", None))
    return jax.shard_map(shards, mesh=mesh, in_specs=in_specs, out_specs=out_specs, check_vma=False)
```
